256 devices in a mesh: section: 8 (over y_lo, x), dp: 32 (over y_hi, z, core).
Axes of the slice: x: 4, y: 4 (y_hi: 2, y_lo: 2; y = y_hi * 2 + y_lo), z: 8, core: 2. Of those that a mesh axis runs over, the one named last changes fastest.
Arguments:
- saved_inputs: bfloat16 [8, 4, 2048, 1024], P('section', None, 'dp'), may hold values from -6 to 6
- norm_gain: float32 [8, 1024], P('section'), may hold values from 0.1 to 1.9
- down_weight: bfloat16 [8, 1024, 2048], P('section'), may hold values from -0.1875 to 0.1875
- up_weight: bfloat16 [8, 1024, 2048], P('section'), may hold values from -0.125 to 0.125
- head_weight: bfloat16 [1024, 128], P('dp'), may hold values from -0.1875 to 0.1875
- head_gain: float32 [1024], replicated, may hold values from 0.1 to 1.9
- targets: float32 [4, 2048, 64], P(None, 'dp'), may hold values from -6 to 6
- levels: float32 [64, 8], replicated, may hold values from -3 to 3
- level_index: int32 [64], replicated, may hold values from 0 to 7
- plan: int32 [4], replicated, may hold values from 0 to 3, each once
Outputs:
- input_grads: bfloat16 [8, 4, 2048, 1024], P('section', None, 'dp')
- down_grad: float32 [8, 1024, 2048], P('section', 'dp')
- up_grad: float32 [8, 1024, 2048], P('section', 'dp')
- head_grad: float32 [1024, 128], P(('section', 'dp'))
The draws below stay inside these ranges and needn't reach their ends.
Inputs may be any that keep to these rules, and one draw needn't show every extreme that they name: `plan`: a permutation of the 4 micro-batches.
All inputs are finite; a program needn't handle non-finite values.
Results may differ from the reference program's by a relative error of at most 0.03.
Values may be sent and summed in bfloat16 or wider, within the bound.
A program may use at most 128 MiB of HBM per device.

```python
import jax
import jax.numpy as jnp
from jax import lax

D = 1024
FF = 2048
VARS = 64
ENS = 2
HC = 128
NLEV = 8
MB = 4
TOK_MB = 64
TOKENS = 2048
SECTIONS = 8
N_DP = 32


def set_ends(array, key, low, largest):
    longest = array.shape.index(max(array.shape))
    spots = []
    for shift in (0, 1):
        where = [jax.random.randint(jax.random.fold_in(key, axis), (), 0, length) for axis, length in enumerate(array.shape)]
        where[longest] = (where[longest] + shift) % array.shape[longest]
        spots.append(tuple(where))
    return array.at[spots[0]].set(low).at[spots[1]].set(largest)


def spiked(values, own_key, source, target, blocks, factor):
    owner, partner = [(jnp.arange(values.shape[position]) // (values.shape[position] // blocks)).reshape([-1 if axis == position else 1 for axis in range(values.ndim)]) for position in (source, target)]
    chosen = jax.random.permutation(own_key, blocks)[partner]
    strong = (owner == chosen) | (owner == (partner + blocks // 2) % blocks)
    return jnp.where(strong, factor * values, values)


def shard_levels(own_key, dims, cuts, least, high):
    factor_of, own = 1.0, jax.random.fold_in(own_key, 6)
    for axis_at, shards_of in cuts:
        steps = jnp.exp(jax.random.uniform(jax.random.fold_in(own, axis_at), (shards_of,), jnp.float32, least / len(cuts), high / len(cuts)))
        factor_of = factor_of * jnp.repeat(steps, dims[axis_at] // shards_of).reshape([-1 if axis == axis_at else 1 for axis in range(len(dims))])
    return factor_of


def bell_draw(rng, dims, spread, most, pieces=(), dtype=jnp.bfloat16):
    drawn = spread * jax.random.normal(rng, dims, jnp.float32)
    if pieces:
        drawn = drawn * shard_levels(rng, dims, pieces, -0.22, 0.18)
    return jnp.clip(drawn, -most, most).astype(dtype)


def gaussian_with(key, extent, deviation, limit, cuts, heavy, held_as=jnp.bfloat16):
    array = deviation * jax.random.normal(key, extent, jnp.float32)
    if cuts:
        array = array * shard_levels(key, extent, cuts, -0.22, 0.18)
    return jnp.clip(spiked(array, jax.random.fold_in(key, 3), *heavy), -limit, limit).astype(held_as)


def setup_inputs(seed: int = 0) -> dict:
    arg_keys = jax.random.split(jax.random.key(seed), 11)
    saved_inputs = gaussian_with(arg_keys[0], (SECTIONS, MB, TOKENS, D), 1.0, 6.0, ((0, 8), (2, 32)), (2, 3, 32, 2.75))
    norm_gain = jnp.clip(1.0 + 0.18 * jax.random.normal(arg_keys[1], (SECTIONS, D), jnp.float32), 0.1, 1.9)
    down_weight = bell_draw(arg_keys[2], (SECTIONS, D, FF), D ** -0.5, 0.1875, ((0, 8),))
    up_weight = bell_draw(arg_keys[3], (SECTIONS, D, FF), FF ** -0.5, 0.125, ((0, 8),))
    head_weight = bell_draw(arg_keys[4], (D, HC), D ** -0.5, 0.1875, ((0, 32),))
    head_gain = jnp.clip(1.0 + 0.18 * jax.random.normal(arg_keys[5], (D,), jnp.float32), 0.1, 1.9)
    targets = bell_draw(arg_keys[6], (MB, TOKENS, VARS), 1.0, 6.0, ((1, 32),), jnp.float32)
    levels = bell_draw(arg_keys[7], (VARS, NLEV), 1.0, 3.0, (), jnp.float32)
    level_index = set_ends(jax.random.randint(arg_keys[8], (VARS,), 0, NLEV), jax.random.fold_in(arg_keys[8], 1), 0, NLEV - 1).astype(jnp.int32)
    plan = jax.random.permutation(arg_keys[9], MB).astype(jnp.int32)
    return {"saved_inputs": saved_inputs, "norm_gain": norm_gain, "down_weight": down_weight, "up_weight": up_weight, "head_weight": head_weight, "head_gain": head_gain, "targets": targets, "levels": levels, "level_index": level_index, "plan": plan}


EPS = 1e-06
DELTA = 0.25
BETA = 0.25
LOSS_SCALE = 64.0
SQRT_HALF = 0.7071067811865476
INV_SQRT_TAU = 0.3989422804014327

def norm_forward(values, scaling):
    inverse = lax.rsqrt(lax.optimization_barrier(jnp.mean(values * values, axis=-1, keepdims=True)) + EPS)
    return (values * inverse * scaling, inverse)

def norm_backward(values, inverse, scaling, upstream):
    weighted = upstream * scaling
    return inverse * weighted - values * inverse ** 3 * lax.optimization_barrier(jnp.mean(weighted * values, axis=-1, keepdims=True))

def gelu_value(hidden):
    return 0.5 * hidden * (1.0 + lax.erf(hidden * SQRT_HALF))

def gelu_slope(hidden):
    return 0.5 * (1.0 + lax.erf(hidden * SQRT_HALF)) + hidden * jnp.exp(-0.5 * hidden * hidden) * INV_SQRT_TAU

def chained(values, threshold):
    shifted = (values - threshold) / BETA
    return (threshold + BETA * jax.nn.softplus(shifted), jax.nn.sigmoid(shifted))

def crps_slope(predicted, observed, threshold):
    columns = predicted.reshape(predicted.shape[0], ENS, VARS)
    chain_pred, chain_rate = chained(columns, threshold)
    chain_obs, unused_rate = chained(observed, threshold)
    spread_obs = chain_pred - chain_obs[:, None, :]
    term_obs = spread_obs / jnp.sqrt(spread_obs * spread_obs + DELTA * DELTA)
    pairs = chain_pred[:, :, None, :] - chain_pred[:, None, :, :]
    term_pair = lax.optimization_barrier(jnp.sum(pairs / jnp.sqrt(pairs * pairs + DELTA * DELTA), axis=2))
    slope = chain_rate * (term_obs / ENS - term_pair / (ENS * ENS))
    return (LOSS_SCALE * slope).reshape(predicted.shape)

def section_forward(inputs, scaling, down_local, up_local):
    wide = inputs.astype(jnp.float32)
    normed_wide, inverse = norm_forward(wide, scaling)
    normed = normed_wide.astype(jnp.bfloat16)
    hidden = jnp.dot(normed, down_local, preferred_element_type=jnp.float32)
    active = gelu_value(hidden).astype(jnp.bfloat16)
    branch = lax.dot_general(active, up_local, (((1,), (1,)), ((), ())), preferred_element_type=jnp.float32)
    output = (wide + branch).astype(jnp.bfloat16)
    return (wide, inverse, normed, hidden, active, output)

def head_backward(output, full_head, head_scaling, observed, threshold):
    wide = output.astype(jnp.float32)
    normed_wide, inverse = norm_forward(wide, head_scaling)
    head_in = normed_wide.astype(jnp.bfloat16)
    predicted = jnp.dot(head_in, full_head, preferred_element_type=jnp.float32)
    head_slope = crps_slope(predicted, observed, threshold).astype(jnp.bfloat16)
    upstream = lax.dot_general(head_slope, full_head, (((1,), (1,)), ((), ())), preferred_element_type=jnp.float32)
    cotangent = norm_backward(wide, inverse, head_scaling, upstream).astype(jnp.bfloat16)
    return (cotangent, head_in, head_slope)

def section_backward(cotangent, wide, inverse, scaling, hidden, down_local, up_local):
    back_active = jnp.dot(cotangent, up_local, preferred_element_type=jnp.float32)
    back_hidden = (back_active * gelu_slope(hidden)).astype(jnp.bfloat16)
    back_normed = lax.dot_general(back_hidden, down_local, (((1,), (1,)), ((), ())), preferred_element_type=jnp.float32)
    grad_in = (cotangent.astype(jnp.float32) + norm_backward(wide, inverse, scaling, back_normed)).astype(jnp.bfloat16)
    return (back_hidden, grad_in)

def to_blocks(stacked):
    micro = stacked.shape[0]
    columns = stacked.shape[2]
    split = stacked.reshape(micro, N_DP, TOK_MB, columns).transpose(1, 0, 2, 3)
    return split.reshape(N_DP, micro * TOK_MB, columns)

def replica_sum(left, right):
    left_blocks = to_blocks(left)
    right_blocks = to_blocks(right)

    def add_block(total, pair):
        part = jnp.dot(pair[0].T, pair[1], preferred_element_type=jnp.float32)
        rounded = lax.optimization_barrier(part.astype(jnp.bfloat16))
        return (total + rounded.astype(jnp.float32), None)
    start = jnp.zeros((left.shape[2], right.shape[2]), jnp.float32)
    total, unused = lax.scan(add_block, start, (left_blocks, right_blocks))
    return total

def reference(saved_inputs, norm_gain, down_weight, up_weight, head_weight, head_gain, targets, levels, level_index, plan):
    sections = saved_inputs.shape[0]
    micro = saved_inputs.shape[1]
    threshold = jnp.take_along_axis(levels, level_index[:, None].astype(jnp.int32), axis=1)[:, 0]
    head_total = jnp.zeros(head_weight.shape, jnp.float32)
    carried = [None] * micro
    grad_list = []
    down_list = []
    up_list = []
    for section_index in range(sections - 1, -1, -1):
        slot_grads = []
        normed_list = []
        back_list = []
        cot_list = []
        active_list = []
        for slot_index in range(micro):
            batch = plan[slot_index]
            inputs = saved_inputs[section_index][batch]
            wide, inverse, normed, hidden, active, output = section_forward(inputs, norm_gain[section_index], down_weight[section_index], up_weight[section_index])
            if section_index == sections - 1:
                cotangent, head_in, head_slope = head_backward(output, head_weight, head_gain, targets[batch], threshold)
                head_total = head_total + jnp.dot(head_in.T, head_slope, preferred_element_type=jnp.float32)
            else:
                cotangent = carried[slot_index]
            back_hidden, grad_in = section_backward(cotangent, wide, inverse, norm_gain[section_index], hidden, down_weight[section_index], up_weight[section_index])
            normed_list.append(normed)
            back_list.append(back_hidden)
            cot_list.append(cotangent)
            active_list.append(active)
            carried[slot_index] = grad_in
            slot_grads.append(grad_in)
        down_total = replica_sum(jnp.stack(normed_list), jnp.stack(back_list))
        up_total = replica_sum(jnp.stack(cot_list), jnp.stack(active_list))
        grad_list.insert(0, jnp.stack(slot_grads))
        down_list.insert(0, down_total / LOSS_SCALE)
        up_list.insert(0, up_total / LOSS_SCALE)
    return (jnp.stack(grad_list), jnp.stack(down_list), jnp.stack(up_list), head_total / LOSS_SCALE)
```

```python
import functools

import jax
import jax.numpy as jnp
from jax import lax
from jax.experimental import pallas as pl
from jax.experimental.pallas import tpu as pltpu
from jax.sharding import PartitionSpec as P

EPS = 1e-06
DELTA = 0.25
BETA = 0.25
LOSS_SCALE = 64.0
SQRT_HALF = 0.7071067811865476
INV_SQRT_TAU = 0.3989422804014327
MESH = pl.DeviceIdType.MESH
F32 = jnp.float32
BF16 = jnp.bfloat16
NN = (((1,), (0,)), ((), ()))
NT = (((1,), (1,)), ((), ()))
TN = (((0,), (0,)), ((), ()))


def matmul(left, right, dims=NN):
    return lax.dot_general(left, right, dims, preferred_element_type=F32)


def inverse_rms(values):
    return lax.rsqrt(jnp.mean(values * values, axis=-1, keepdims=True) + EPS)


def norm_backward(values, inverse, scaling, upstream):
    weighted = upstream * scaling
    mean = jnp.mean(weighted * values, axis=-1, keepdims=True)
    return inverse * weighted - values * (inverse * inverse * inverse) * mean


def soft(values):
    return values * lax.rsqrt(values * values + DELTA * DELTA)


def chain(values, threshold):
    shifted = (values - threshold) / BETA
    softplus = jnp.maximum(shifted, 0.0) + jnp.log1p(jnp.exp(-jnp.abs(shifted)))
    return threshold + BETA * softplus


def chain_rate(values, threshold):
    shifted = (values - threshold) / BETA
    small = jnp.exp(-jnp.abs(shifted))
    return jnp.where(shifted >= 0.0, 1.0, small) / (1.0 + small)


def crps_slope(predicted, observed, threshold):
    variables = observed.shape[1]
    first, second = predicted[:, :variables], predicted[:, variables:]
    chain_first, chain_second = chain(first, threshold), chain(second, threshold)
    chain_obs = chain(observed, threshold)
    pair = soft(chain_first - chain_second)
    slope_first = soft(chain_first - chain_obs) / 2 - pair / 4
    slope_second = soft(chain_second - chain_obs) / 2 + pair / 4
    return jnp.concatenate(
        [
            LOSS_SCALE * chain_rate(first, threshold) * slope_first,
            LOSS_SCALE * chain_rate(second, threshold) * slope_second,
        ],
        axis=1,
    )


def body(
    sections,
    replicas,
    plan_ref,
    index_ref,
    saved_ref,
    gain_ref,
    down_ref,
    up_ref,
    head_ref,
    head_gain_ref,
    targets_ref,
    levels_ref,
    grads_out,
    down_out,
    up_out,
    head_out,
    saved,
    down,
    up,
    wide,
    inverses,
    normed,
    active,
    slopes,
    cots,
    backs,
    products,
    ring,
    across,
    halves,
    mates,
    full_head,
    outputs,
    head_ins,
    head_slopes,
    head_parts,
    head_terms,
    head_sums,
    head_mine,
    load_sem,
    cot_send,
    cot_recv,
    pair_send,
    pair_recv,
    slot_send,
    slot_recv,
    ring_send,
    ring_recv,
    across_send,
    across_recv,
    mate_send,
    mate_recv,
    gather_send,
    gather_recv,
    term_send,
    term_recv,
    share_send,
    share_recv,
):
    micro, tokens, width = wide.shape
    rows_all = micro * tokens
    half = active.shape[-1]
    levels = replicas // 4
    chunk = width // (2 * levels)
    share = width // replicas
    final = head_mine.shape[0]

    section = lax.axis_index("section")
    me = lax.axis_index("dp")
    core = lax.rem(me, 2)
    level = lax.rem(lax.div(me, 2), levels)
    side = lax.div(me, 2 * levels)
    is_last = section == sections - 1
    not_last = section < sections - 1
    not_first = section > 0

    def member(side_of, level_of, core_of):
        return (section, (side_of * levels + level_of) * 2 + core_of)

    ahead = member(side, lax.rem(level + 1, levels), core)
    behind = member(side, lax.rem(level + levels - 1, levels), core)
    mate = member(side, level, 1 - core)
    opposite = member(1 - side, level, core)
    sender = (lax.rem(section + 1, sections), me)
    receiver = (lax.rem(section + sections - 1, sections), me)
    head_source = lax.div(section * replicas + me, sections)
    source_is_me = jnp.logical_and(is_last, head_source == me)

    def remote(src, dst, send, recv, device):
        return pltpu.make_async_remote_copy(
            src_ref=src,
            dst_ref=dst,
            send_sem=send,
            recv_sem=recv,
            device_id=device,
            device_id_type=MESH,
        )

    saved_load = pltpu.make_async_copy(saved_ref, saved, load_sem.at[0])
    down_load = pltpu.make_async_copy(down_ref, down, load_sem.at[1])
    up_load = pltpu.make_async_copy(up_ref, up, load_sem.at[2])
    saved_load.start()
    down_load.start()
    up_load.start()

    barrier = pltpu.get_barrier_semaphore()

    def greet(device):
        pl.semaphore_signal(barrier, inc=1, device_id=device, device_id_type=MESH)

    @pl.when(not_last)
    def _():
        greet(sender)
        for device in (ahead, behind, mate, opposite):
            greet(device)

    @pl.when(is_last)
    def _():
        def greet_peer(offset, unused):
            greet((section, lax.rem(me + offset, replicas)))
            return unused

        lax.fori_loop(1, replicas, greet_peer, 0)

    @pl.when(jnp.logical_not(source_is_me))
    def _():
        greet((sections - 1, head_source))

    saved_load.wait()

    def norm_slot(slot, unused):
        values = saved[plan_ref[slot]]
        wide[slot] = values
        values = values.astype(F32)
        inverse = inverse_rms(values)
        inverses[slot] = inverse
        normed[0, slot] = (values * inverse * gain_ref[...]).astype(BF16)
        return unused

    lax.fori_loop(0, micro, norm_slot, 0)

    heard = jnp.where(
        is_last,
        replicas + sections - jnp.where(me == replicas - 1, 1, 0),
        4 + jnp.where(not_first, 1, 0),
    )
    pl.semaphore_wait(barrier, heard)

    def gather_copy(offset):
        peer = lax.rem(me + offset, replicas)
        return remote(
            head_ref, full_head.at[me], gather_send.at[offset], gather_recv.at[me], (section, peer)
        )

    def gather_wait(offset):
        peer = lax.rem(me + offset, replicas)
        remote(
            head_ref, full_head.at[peer], gather_send.at[offset], gather_recv.at[peer], (section, peer)
        ).wait_recv()

    @pl.when(is_last)
    def _():
        def send(offset, unused):
            gather_copy(offset).start()
            return unused

        lax.fori_loop(1, replicas, send, 0)
        full_head[me] = head_ref[...]

    normed_copy = remote(normed.at[0], normed.at[1], pair_send.at[0], pair_recv.at[0], mate)
    normed_copy.start()

    down_load.wait()
    step = min(256, half)
    all_normed = normed[0].reshape(rows_all, width)
    for part in range(2):
        where = 2 * lax.rem(core + part, 2)

        def forward(number, unused, part=part, where=where):
            columns = pl.ds(pl.multiple_of(part * half + number * step, step), step)
            inner = pl.ds(pl.multiple_of(number * step, step), step)
            hidden = matmul(all_normed, down[:, columns])
            bell = 0.5 * (1.0 + lax.erf(hidden * SQRT_HALF))
            active[where, :, :, inner] = (
                (hidden * bell).astype(BF16).reshape(micro, tokens, step)
            )
            slope = bell + hidden * jnp.exp(-0.5 * hidden * hidden) * INV_SQRT_TAU
            slopes[part, :, :, inner] = slope.reshape(micro, tokens, step)
            return unused

        lax.fori_loop(0, half // step, forward, 0)

    active_copy = remote(active.at[2], active.at[1], pair_send.at[1], pair_recv.at[1], mate)
    active_copy.start()
    up_load.wait()

    @pl.when(is_last)
    def _():
        wide_step = min(256, width)

        def output_columns(number, unused):
            columns = pl.ds(pl.multiple_of(number * wide_step, wide_step), wide_step)
            total = wide[:, :, columns].astype(F32).reshape(rows_all, wide_step)
            for part in range(2):
                where = 2 * lax.rem(core + part, 2)
                total = total + matmul(
                    active[where].reshape(rows_all, half),
                    up[columns, part * half : (part + 1) * half],
                    NT,
                )
            outputs[:, :, columns] = total.astype(BF16).reshape(micro, tokens, wide_step)
            return unused

        lax.fori_loop(0, width // wide_step, output_columns, 0)

        def arrive(offset, unused):
            gather_wait(offset)
            return unused

        lax.fori_loop(1, replicas, arrive, 0)

    def head_slot(slot):
        variables, count = levels_ref.shape
        diagonal = lax.broadcasted_iota(jnp.int32, (variables, variables), 0) == (
            lax.broadcasted_iota(jnp.int32, (variables, variables), 1)
        )
        threshold = jnp.zeros((1, variables), F32)
        for number in range(count):
            row = jnp.sum(
                jnp.where(diagonal, levels_ref[:, number : number + 1], 0.0), axis=0, keepdims=True
            )
            threshold = jnp.where(index_ref[...] == number, row, threshold)
        head = full_head[...].reshape(width, full_head.shape[2])
        values = outputs[slot].astype(F32)
        inverse = inverse_rms(values)
        head_in = (values * inverse * head_gain_ref[...]).astype(BF16)
        head_ins[slot] = head_in
        predicted = matmul(head_in, head)
        slope = crps_slope(predicted, targets_ref[plan_ref[slot]], threshold).astype(BF16)
        head_slopes[slot] = slope
        upstream = matmul(slope, head, NT)
        cots[0, slot] = norm_backward(values, inverse, head_gain_ref[...], upstream).astype(BF16)

    def cot_copy(slot):
        return remote(
            grads_out.at[slot], cots.at[0, slot], cot_send.at[slot], cot_recv.at[slot], receiver
        )

    def pass_cot(slot):
        return remote(
            cots.at[0, slot], cots.at[1, slot], slot_send.at[0, slot], slot_recv.at[0, slot], mate
        )

    def pass_back(slot):
        return remote(
            backs.at[2, slot], backs.at[1, slot], slot_send.at[1, slot], slot_recv.at[1, slot], mate
        )

    def backward(slot, unused):
        @pl.when(not_last)
        def _():
            cot_copy(slot).wait_recv()

        @pl.when(is_last)
        def _():
            head_slot(slot)

        pass_cot(slot).start()
        cotangent = cots[0, slot]
        back_normed = jnp.zeros((tokens, width), F32)
        for part in range(2):
            columns = slice(part * half, (part + 1) * half)
            back = (matmul(cotangent, up[:, columns]) * slopes[part, slot]).astype(BF16)
            backs[2 * lax.rem(core + part, 2), slot] = back
            back_normed = back_normed + matmul(back, down[:, columns], NT)
        grads_out[slot] = (
            cotangent.astype(F32)
            + norm_backward(wide[slot].astype(F32), inverses[slot], gain_ref[...], back_normed)
        ).astype(BF16)

        @pl.when(not_first)
        def _():
            cot_copy(slot).start()

        pass_back(slot).start()
        return unused

    lax.fori_loop(0, micro, backward, 0)

    def slot_arrived(slot, unused):
        pass_cot(slot).wait_recv()
        pass_back(slot).wait_recv()
        return unused

    normed_copy.wait_recv()
    active_copy.wait_recv()
    lax.fori_loop(0, micro, slot_arrived, 0)
    row_step = min(256, width)

    def multiply(number, unused):
        rows = pl.ds(pl.multiple_of(number * row_step, row_step), row_step)
        for matrix, left, right in ((1, cots, active), (0, normed, backs)):
            products[matrix, rows] = matmul(
                left[:, :, :, rows].reshape(2 * rows_all, row_step),
                right[0:2].reshape(2 * rows_all, half),
                TN,
            ).astype(BF16)
        return unused

    lax.fori_loop(0, width // row_step, multiply, 0)

    def term_copy(offset):
        peer = lax.rem(me + offset, replicas)
        return remote(
            head_parts.at[peer], head_terms.at[me], term_send.at[offset], term_recv.at[me], (section, peer)
        )

    def term_wait(offset):
        peer = lax.rem(me + offset, replicas)
        remote(
            head_parts.at[peer], head_terms.at[peer], term_send.at[offset], term_recv.at[peer], (section, peer)
        ).wait_recv()

    def share_copy(number):
        block = sections * me + number
        target = (lax.div(block, replicas), lax.rem(block, replicas))
        return block, remote(head_sums.at[number], head_mine, share_send.at[number], share_recv, target)

    @pl.when(is_last)
    def _():
        part = matmul(
            head_ins[...].reshape(rows_all, width),
            head_slopes[...].reshape(rows_all, head_slopes.shape[2]),
            TN,
        )
        head_parts[...] = part.reshape(head_parts.shape)

        def send(offset, unused):
            term_copy(offset).start()
            return unused

        lax.fori_loop(1, replicas, send, 0)

    def place(matrix, turn):
        if matrix == 0:
            return lax.rem(level + 2 * levels - 1 - turn, levels)
        return lax.rem(level + 1 + turn, levels)

    def rows_of(which, position):
        side_of = 1 - side if which == 0 else side
        return pl.ds(pl.multiple_of((side_of * levels + position) * chunk, chunk), chunk)

    def ring_copy(matrix, which, turn):
        return remote(
            products.at[matrix, rows_of(which, place(matrix, turn))],
            ring.at[matrix, which, turn],
            ring_send.at[matrix, which, turn],
            ring_recv.at[matrix, which, turn],
            ahead if matrix == 0 else behind,
        )

    def add_arrived(matrix, which, turn):
        ring_copy(matrix, which, turn - 1).wait_recv()
        rows = rows_of(which, place(matrix, turn))
        return products[matrix, rows].astype(F32) + ring[matrix, which, turn - 1].astype(F32)

    for which in range(2):
        for matrix in range(2):
            ring_copy(matrix, which, 0).start()

    def turn_ring(turn, unused):
        for which in range(2):
            for matrix in range(2):
                rows = rows_of(which, place(matrix, turn))
                products[matrix, rows] = add_arrived(matrix, which, turn).astype(BF16)
                ring_copy(matrix, which, turn).start()
        return unused

    lax.fori_loop(1, levels - 1, turn_ring, 0)

    def across_copy(matrix):
        return remote(
            products.at[matrix, rows_of(0, level)],
            across.at[matrix],
            across_send.at[matrix],
            across_recv.at[matrix],
            opposite,
        )

    for matrix in range(2):
        products[matrix, rows_of(0, level)] = add_arrived(matrix, 0, levels - 1).astype(BF16)
        across_copy(matrix).start()

    def mate_copy(matrix):
        return remote(
            halves.at[matrix, 1 - core], mates.at[matrix], mate_send.at[matrix], mate_recv.at[matrix], mate
        )

    mine = pl.ds(pl.multiple_of(core * half, half), half)
    theirs = pl.ds(pl.multiple_of((1 - core) * half, half), half)
    for matrix, result in ((0, down_out), (1, up_out)):
        total = add_arrived(matrix, 1, levels - 1)
        across_copy(matrix).wait_recv()
        total = (total + across[matrix].astype(F32)) / LOSS_SCALE
        halves[matrix] = total.reshape(2, share, half)
        mate_copy(matrix).start()
        result[:, mine] = halves[matrix, core]

    @pl.when(is_last)
    def _():
        def add_term(offset, total):
            term_wait(offset)
            return total + head_terms[lax.rem(me + offset, replicas)]

        total = lax.fori_loop(1, replicas, add_term, head_parts[me]) / LOSS_SCALE
        for number in range(sections):
            head_sums[number] = total[number * final : (number + 1) * final]
        for number in range(sections):
            block, copy = share_copy(number)
            to_me = block == (sections - 1) * replicas + me

            @pl.when(to_me)
            def _():
                head_mine[...] = head_sums[number]

            @pl.when(jnp.logical_not(to_me))
            def _():
                copy.start()

    for matrix, result in ((0, down_out), (1, up_out)):
        mate_copy(matrix).wait_recv()
        result[:, theirs] = mates[matrix]

    @pl.when(jnp.logical_not(source_is_me))
    def _():
        share_copy(0)[1].wait_recv()

    head_out[...] = head_mine[...]

    normed_copy.wait_send()
    active_copy.wait_send()

    def slot_left(slot, unused):
        pass_cot(slot).wait_send()
        pass_back(slot).wait_send()
        return unused

    lax.fori_loop(0, micro, slot_left, 0)

    @pl.when(not_first)
    def _():
        def cot_left(slot, unused):
            cot_copy(slot).wait_send()
            return unused

        lax.fori_loop(0, micro, cot_left, 0)

    def ring_left(turn, unused):
        for which in range(2):
            for matrix in range(2):
                ring_copy(matrix, which, turn).wait_send()
        return unused

    lax.fori_loop(0, levels - 1, ring_left, 0)
    for matrix in range(2):
        across_copy(matrix).wait_send()
        mate_copy(matrix).wait_send()

    @pl.when(is_last)
    def _():
        def head_left(offset, unused):
            gather_copy(offset).wait_send()
            term_copy(offset).wait_send()
            return unused

        lax.fori_loop(1, replicas, head_left, 0)
        for number in range(sections):
            block, copy = share_copy(number)

            @pl.when(block != (sections - 1) * replicas + me)
            def _():
                copy.wait_send()


def local(
    sections,
    replicas,
    saved_inputs,
    norm_gain,
    down_weight,
    up_weight,
    head_weight,
    head_gain,
    targets,
    levels,
    level_index,
    plan,
):
    micro, tokens, width = saved_inputs.shape[1:]
    units = down_weight.shape[2]
    half = units // 2
    cols = head_weight.shape[1]
    rings = replicas // 4
    chunk = width // (2 * rings)
    share = width // replicas
    final = share // sections
    whole = pl.BlockSpec(memory_space=pltpu.VMEM)
    anywhere = pl.BlockSpec(memory_space=pl.ANY)
    dma = pltpu.SemaphoreType.DMA
    grads, down_grad, up_grad, head_grad = pl.pallas_call(
        functools.partial(body, sections, replicas),
        out_shape=(
            jax.ShapeDtypeStruct((micro, tokens, width), BF16),
            jax.ShapeDtypeStruct((share, units), F32),
            jax.ShapeDtypeStruct((share, units), F32),
            jax.ShapeDtypeStruct((final, cols), F32),
        ),
        in_specs=[
            pl.BlockSpec(memory_space=pltpu.SMEM),
            whole,
            anywhere,
            whole,
            anywhere,
            anywhere,
            whole,
            whole,
            whole,
            whole,
        ],
        out_specs=(whole, whole, whole, whole),
        scratch_shapes=[
            pltpu.VMEM((micro, tokens, width), BF16),
            pltpu.VMEM((width, units), BF16),
            pltpu.VMEM((width, units), BF16),
            pltpu.VMEM((micro, tokens, width), BF16),
            pltpu.VMEM((micro, tokens, 1), F32),
            pltpu.VMEM((2, micro, tokens, width), BF16),
            pltpu.VMEM((3, micro, tokens, half), BF16),
            pltpu.VMEM((2, micro, tokens, half), F32),
            pltpu.VMEM((2, micro, tokens, width), BF16),
            pltpu.VMEM((3, micro, tokens, half), BF16),
            pltpu.VMEM((2, width, half), BF16),
            pltpu.VMEM((2, 2, rings - 1, chunk, half), BF16),
            pltpu.VMEM((2, chunk, half), BF16),
            pltpu.VMEM((2, 2, share, half), F32),
            pltpu.VMEM((2, share, half), F32),
            pltpu.VMEM((replicas, share, cols), BF16),
            pltpu.VMEM((micro, tokens, width), BF16),
            pltpu.VMEM((micro, tokens, width), BF16),
            pltpu.VMEM((micro, tokens, cols), BF16),
            pltpu.VMEM((replicas, share, cols), F32),
            pltpu.VMEM((replicas, share, cols), F32),
            pltpu.VMEM((sections, final, cols), F32),
            pltpu.VMEM((final, cols), F32),
            dma((3,)),
            dma((micro,)),
            dma((micro,)),
            dma((2,)),
            dma((2,)),
            dma((2, micro)),
            dma((2, micro)),
            dma((2, 2, rings - 1)),
            dma((2, 2, rings - 1)),
            dma((2,)),
            dma((2,)),
            dma((2,)),
            dma((2,)),
            dma((replicas,)),
            dma((replicas,)),
            dma((replicas,)),
            dma((replicas,)),
            dma((sections,)),
            dma(()),
        ],
        compiler_params=pltpu.CompilerParams(
            collective_id=0, has_side_effects=True, vmem_limit_bytes=56 * 1024 * 1024
        ),
    )(
        plan,
        level_index.reshape(1, -1),
        saved_inputs[0],
        norm_gain,
        down_weight[0],
        up_weight[0],
        head_weight,
        head_gain.reshape(1, -1),
        targets,
        levels,
    )
    return grads[None], down_grad[None], up_grad[None], head_grad


def solution(mesh):
    return jax.shard_map(
        functools.partial(local, mesh.shape["section"], mesh.shape["dp"]),
        mesh=mesh,
        in_specs=(
            P("section", None, "dp", None),
            P("section", None),
            P("section", None, None),
            P("section", None, None),
            P("dp", None),
            P(),
            P(None, "dp", None),
            P(),
            P(),
            P(),
        ),
        out_specs=(
            P("section", None, "dp", None),
            P("section", "dp", None),
            P("section", "dp", None),
            P(("section", "dp"), None),
        ),
        check_vma=False,
    )
```

```python
import functools

import jax
import jax.numpy as jnp
from jax import lax
from jax.experimental import pallas as pl
from jax.experimental.pallas import tpu as pltpu
from jax.sharding import PartitionSpec as P

EPS = 1e-06
DELTA = 0.25
BETA = 0.25
LOSS_SCALE = 64.0
SQRT_HALF = 0.7071067811865476
INV_SQRT_TAU = 0.3989422804014327
MESH = pl.DeviceIdType.MESH
F32 = jnp.float32
BF16 = jnp.bfloat16
NN = (((1,), (0,)), ((), ()))
NT = (((1,), (1,)), ((), ()))
TN = (((0,), (0,)), ((), ()))


def matmul(left, right, dims=NN):
    return lax.dot_general(left, right, dims, preferred_element_type=F32)


def inverse_rms(values):
    return lax.rsqrt(jnp.mean(values * values, axis=-1, keepdims=True) + EPS)


def norm_backward(values, inverse, scaling, upstream):
    weighted = upstream * scaling
    mean = jnp.mean(weighted * values, axis=-1, keepdims=True)
    return inverse * weighted - values * (inverse * inverse * inverse) * mean


def soft(values):
    return values * lax.rsqrt(values * values + DELTA * DELTA)


def chain(values, threshold):
    shifted = (values - threshold) / BETA
    softplus = jnp.maximum(shifted, 0.0) + jnp.log1p(jnp.exp(-jnp.abs(shifted)))
    return threshold + BETA * softplus


def chain_rate(values, threshold):
    shifted = (values - threshold) / BETA
    small = jnp.exp(-jnp.abs(shifted))
    return jnp.where(shifted >= 0.0, 1.0, small) / (1.0 + small)


def crps_slope(predicted, observed, threshold):
    variables = observed.shape[1]
    first, second = predicted[:, :variables], predicted[:, variables:]
    chain_first, chain_second = chain(first, threshold), chain(second, threshold)
    chain_obs = chain(observed, threshold)
    pair = soft(chain_first - chain_second)
    slope_first = soft(chain_first - chain_obs) / 2 - pair / 4
    slope_second = soft(chain_second - chain_obs) / 2 + pair / 4
    return jnp.concatenate(
        [
            LOSS_SCALE * chain_rate(first, threshold) * slope_first,
            LOSS_SCALE * chain_rate(second, threshold) * slope_second,
        ],
        axis=1,
    )


def body(
    sections,
    replicas,
    plan_ref,
    index_ref,
    saved_ref,
    gain_ref,
    down_ref,
    up_ref,
    head_ref,
    head_gain_ref,
    targets_ref,
    levels_ref,
    grads_out,
    down_out,
    up_out,
    head_out,
    saved,
    down,
    up,
    down_turned,
    wide,
    inverses,
    normed,
    active,
    slopes,
    cots,
    backs,
    products,
    early,
    ring_other,
    ring_own,
    across,
    halves,
    mates,
    full_head,
    outputs,
    head_ins,
    head_slopes,
    head_parts,
    head_terms,
    head_sums,
    head_mine,
    load_sem,
    cot_send,
    cot_recv,
    pair_send,
    pair_recv,
    slot_send,
    slot_recv,
    early_send,
    early_recv,
    ring_send,
    ring_recv,
    across_send,
    across_recv,
    mate_send,
    mate_recv,
    gather_send,
    gather_recv,
    term_send,
    term_recv,
    share_send,
    share_recv,
):
    units, unit, width = wide.shape
    micro = saved.shape[0]
    per_slot = units // micro
    rows_all = units * unit
    half = active.shape[-1]
    levels = replicas // 4
    positions = replicas // 2
    chunk = width // (2 * levels)
    side_rows = width // 2
    main = ring_other.shape[-1]
    share = width // replicas
    final = head_mine.shape[0]

    section = lax.axis_index("section")
    me = lax.axis_index("dp")
    core = lax.rem(me, 2)
    level = lax.rem(lax.div(me, 2), levels)
    side = lax.div(me, 2 * levels)
    is_last = section == sections - 1
    not_last = section < sections - 1
    not_first = section > 0

    def member(side_of, level_of, core_of):
        return (section, (side_of * levels + level_of) * 2 + core_of)

    ahead = member(side, lax.rem(level + 1, levels), core)
    behind = member(side, lax.rem(level + levels - 1, levels), core)
    mate = member(side, level, 1 - core)
    opposite = member(1 - side, level, core)
    sender = (lax.rem(section + 1, sections), me)
    receiver = (lax.rem(section + sections - 1, sections), me)
    head_source = lax.div(section * replicas + me, sections)
    source_is_me = jnp.logical_and(is_last, head_source == me)

    def remote(src, dst, send, recv, device):
        return pltpu.make_async_remote_copy(
            src_ref=src,
            dst_ref=dst,
            send_sem=send,
            recv_sem=recv,
            device_id=device,
            device_id_type=MESH,
        )

    saved_load = pltpu.make_async_copy(saved_ref, saved, load_sem.at[0])
    down_load = pltpu.make_async_copy(down_ref, down, load_sem.at[1])
    up_load = pltpu.make_async_copy(up_ref, up, load_sem.at[2])
    saved_load.start()
    down_load.start()
    up_load.start()

    barrier = pltpu.get_barrier_semaphore()

    def greet(device):
        pl.semaphore_signal(barrier, inc=1, device_id=device, device_id_type=MESH)

    @pl.when(not_last)
    def _():
        greet(sender)
        for device in (ahead, behind, mate, opposite):
            greet(device)

    @pl.when(is_last)
    def _():
        def greet_peer(offset, unused):
            greet((section, lax.rem(me + offset, replicas)))
            return unused

        lax.fori_loop(1, replicas, greet_peer, 0)

    @pl.when(jnp.logical_not(source_is_me))
    def _():
        greet((sections - 1, head_source))

    saved_load.wait()

    def norm_slot(slot, unused):
        values = saved[plan_ref[slot]]
        these = pl.ds(slot * per_slot, per_slot)
        wide[these] = values.reshape(per_slot, unit, width)
        values = values.astype(F32)
        inverse = inverse_rms(values)
        inverses[these] = inverse.reshape(per_slot, unit, 1)
        normed[0, these] = (
            (values * inverse * gain_ref[...]).astype(BF16).reshape(per_slot, unit, width)
        )
        return unused

    lax.fori_loop(0, micro, norm_slot, 0)

    heard = jnp.where(
        is_last,
        replicas + sections - jnp.where(me == replicas - 1, 1, 0),
        4 + jnp.where(not_first, 1, 0),
    )
    pl.semaphore_wait(barrier, heard)

    position = side * levels + level

    def gather_copy(offset):
        peer = lax.rem(position + offset, positions)
        return remote(
            head_ref,
            full_head.at[position, core],
            gather_send.at[offset],
            gather_recv.at[position],
            (section, peer * 2 + core),
        )

    def gather_wait(offset):
        peer = lax.rem(position + offset, positions)
        remote(
            head_ref,
            full_head.at[peer, core],
            gather_send.at[offset],
            gather_recv.at[peer],
            (section, peer * 2 + core),
        ).wait_recv()

    def gather_mate(which):
        return remote(
            full_head.at[:, which],
            full_head.at[:, which],
            gather_send.at[0],
            gather_recv.at[positions],
            mate,
        )

    @pl.when(is_last)
    def _():
        def send(offset, unused):
            gather_copy(offset).start()
            return unused

        lax.fori_loop(1, positions, send, 0)
        full_head[position, core] = head_ref[...]

    normed_copy = remote(normed.at[0], normed.at[1], pair_send.at[0], pair_recv.at[0], mate)
    normed_copy.start()

    down_load.wait()
    step = min(256, half)
    all_normed = normed[0].reshape(rows_all, width)
    for part in range(2):
        where = 2 * lax.rem(core + part, 2)

        def forward(number, unused, part=part, where=where):
            columns = pl.ds(pl.multiple_of(part * half + number * step, step), step)
            inner = pl.ds(pl.multiple_of(number * step, step), step)
            hidden = matmul(all_normed, down[:, columns])
            bell = 0.5 * (1.0 + lax.erf(hidden * SQRT_HALF))
            active[where, :, :, inner] = (
                (hidden * bell).astype(BF16).reshape(units, unit, step)
            )
            slope = bell + hidden * jnp.exp(-0.5 * hidden * hidden) * INV_SQRT_TAU
            slopes[part, :, :, inner] = slope.reshape(units, unit, step)
            return unused

        lax.fori_loop(0, half // step, forward, 0)

    active_copy = remote(active.at[2], active.at[1], pair_send.at[1], pair_recv.at[1], mate)
    active_copy.start()
    up_load.wait()

    @pl.when(is_last)
    def _():
        wide_step = min(256, width)

        def output_columns(number, unused):
            columns = pl.ds(pl.multiple_of(number * wide_step, wide_step), wide_step)
            total = wide[:, :, columns].astype(F32).reshape(rows_all, wide_step)
            for part in range(2):
                where = 2 * lax.rem(core + part, 2)
                total = total + matmul(
                    active[where].reshape(rows_all, half),
                    up[columns, part * half : (part + 1) * half],
                    NT,
                )
            outputs[:, :, columns] = total.astype(BF16).reshape(units, unit, wide_step)
            return unused

        lax.fori_loop(0, width // wide_step, output_columns, 0)

        def arrive(offset, unused):
            gather_wait(offset)
            return unused

        lax.fori_loop(1, positions, arrive, 0)
        gather_mate(core).start()
        gather_mate(1 - core).wait_recv()

    @pl.when(not_last)
    def _():
        turn_step = min(256, width)

        def turn_columns(number, unused):
            block = pl.ds(pl.multiple_of(number * turn_step, turn_step), turn_step)
            down_turned[block, :] = down[:, block].T
            return unused

        lax.fori_loop(0, 2 * half // turn_step, turn_columns, 0)

    def head_slot(slot):
        these = pl.ds(slot * per_slot, per_slot)
        rows = per_slot * unit
        choice = lax.broadcasted_iota(jnp.int32, levels_ref.shape, 0) == index_ref[...]
        threshold = jnp.sum(jnp.where(choice, levels_ref[...], 0.0), axis=0, keepdims=True)
        head = full_head[...].reshape(width, full_head.shape[3])
        values = outputs[these].astype(F32).reshape(rows, width)
        inverse = inverse_rms(values)
        head_in = (values * inverse * head_gain_ref[...]).astype(BF16)
        head_ins[these] = head_in.reshape(per_slot, unit, width)
        predicted = matmul(head_in, head)
        slope = crps_slope(predicted, targets_ref[plan_ref[slot]], threshold).astype(BF16)
        head_slopes[these] = slope.reshape(per_slot, unit, slope.shape[1])
        upstream = matmul(slope, head, NT)
        cotangent = norm_backward(values, inverse, head_gain_ref[...], upstream)
        cots[0, these] = cotangent.astype(BF16).reshape(per_slot, unit, width)

    def cot_copy(slot):
        return remote(
            grads_out.at[slot], cots.at[0, slot], cot_send.at[slot], cot_recv.at[slot], receiver
        )

    def pass_cot(slot):
        return remote(
            cots.at[0, slot], cots.at[1, slot], slot_send.at[0, slot], slot_recv.at[0, slot], mate
        )

    def pass_back(slot):
        return remote(
            backs.at[2, slot], backs.at[1, slot], slot_send.at[1, slot], slot_recv.at[1, slot], mate
        )

    def backward(first, count, turned):
        these = pl.ds(first, count)
        rows = count * unit
        cotangent = cots[0, these].reshape(rows, width)
        back_normed = jnp.zeros((rows, width), F32)
        for part in range(2):
            columns = slice(part * half, (part + 1) * half)
            back_active = matmul(cotangent, up[:, columns])
            back = (back_active * slopes[part, these].reshape(rows, half)).astype(BF16)
            backs[2 * lax.rem(core + part, 2), these] = back.reshape(count, unit, half)
            if turned:
                back_normed = back_normed + matmul(back, down_turned[columns, :])
            else:
                back_normed = back_normed + matmul(back, down[:, columns], NT)
        values = wide[these].astype(F32).reshape(rows, width)
        correction = norm_backward(
            values, inverses[these].reshape(rows, 1), gain_ref[...], back_normed
        )
        grads_out[these] = (
            (cotangent.astype(F32) + correction).astype(BF16).reshape(count, unit, width)
        )

        @pl.when(not_first)
        def _():
            for number in range(count):
                cot_copy(first + number).start()

        for number in range(count):
            pass_cot(first + number).start()
            pass_back(first + number).start()

    @pl.when(is_last)
    def _():
        def from_head(slot, unused):
            head_slot(slot)
            backward(slot * per_slot, per_slot, False)
            return unused

        lax.fori_loop(0, micro, from_head, 0)

    @pl.when(not_last)
    def _():
        def from_next(number, unused):
            cot_copy(number).wait_recv()
            backward(number, 1, True)
            return unused

        lax.fori_loop(0, units, from_next, 0)

    def slot_arrived(slot, unused):
        pass_cot(slot).wait_recv()
        pass_back(slot).wait_recv()
        return unused

    normed_copy.wait_recv()
    active_copy.wait_recv()
    lax.fori_loop(0, units, slot_arrived, 0)
    row_step = min(256, side_rows)

    def multiply(of_side):
        def block(number, unused):
            first = of_side * side_rows + number * row_step
            rows = pl.ds(pl.multiple_of(first, row_step), row_step)
            for matrix, left, right in ((1, cots, active), (0, normed, backs)):
                products[matrix, rows] = matmul(
                    left[:, :, :, rows].reshape(2 * rows_all, row_step),
                    right[0:2].reshape(2 * rows_all, half),
                    TN,
                ).astype(BF16)
            return unused

        lax.fori_loop(0, side_rows // row_step, block, 0)

    multiply(1 - side)
    theirs_rows = pl.ds(pl.multiple_of((1 - side) * side_rows, side_rows), side_rows)

    def early_copy(matrix):
        return remote(
            products.at[matrix, theirs_rows, main:half],
            early.at[matrix],
            early_send.at[matrix],
            early_recv.at[matrix],
            opposite,
        )

    for matrix in range(2):
        early_copy(matrix).start()

    longest = levels // 2
    chains = ((0, 0), (1, 1), (1, 0), (0, 1))

    def hops(matrix, way):
        return longest if matrix == way else longest - 1

    def rows_of(phase, position):
        side_of = 1 - side if phase == 0 else side
        return pl.ds(pl.multiple_of((side_of * levels + position) * chunk, chunk), chunk)

    def ring_rows(phase, matrix, way, hop):
        left = hops(matrix, way) - hop
        return rows_of(phase, lax.rem(level + levels + (left if way == 0 else -left), levels))

    def ring_copy(phase, matrix, way, hop):
        rows = ring_rows(phase, matrix, way, hop)
        buffer = ring_other if phase == 0 else ring_own
        source = products.at[matrix, rows, 0:main] if phase == 0 else products.at[matrix, rows]
        return remote(
            source,
            buffer.at[matrix, way, hop],
            ring_send.at[phase, matrix, way, hop],
            ring_recv.at[phase, matrix, way, hop],
            ahead if way == 0 else behind,
        )

    def ring_start(phase):
        for matrix, way in chains:
            ring_copy(phase, matrix, way, 0).start()

    def ring_turns(phase):
        buffer = ring_other if phase == 0 else ring_own
        span = buffer.shape[-1]
        for hop in range(1, longest):
            for matrix, way in chains:
                if hop < hops(matrix, way):
                    ring_copy(phase, matrix, way, hop - 1).wait_recv()
                    rows = ring_rows(phase, matrix, way, hop)
                    total = products[matrix, rows, 0:span].astype(F32) + (
                        buffer[matrix, way, hop - 1].astype(F32)
                    )
                    products[matrix, rows, 0:span] = total.astype(BF16)
                    ring_copy(phase, matrix, way, hop).start()

    def ring_total(phase, matrix):
        buffer = ring_other if phase == 0 else ring_own
        total = products[matrix, rows_of(phase, level), 0 : buffer.shape[-1]].astype(F32)
        for way in (1, 0) if matrix == 0 else (0, 1):
            last = hops(matrix, way) - 1
            ring_copy(phase, matrix, way, last).wait_recv()
            total = total + buffer[matrix, way, last].astype(F32)
        return total

    ring_start(0)
    multiply(side)

    def term_copy(offset):
        peer = lax.rem(me + offset, replicas)
        return remote(
            head_parts.at[peer], head_terms.at[me], term_send.at[offset], term_recv.at[me], (section, peer)
        )

    def term_wait(offset):
        peer = lax.rem(me + offset, replicas)
        remote(
            head_parts.at[peer], head_terms.at[peer], term_send.at[offset], term_recv.at[peer], (section, peer)
        ).wait_recv()

    def share_copy(number):
        block = sections * me + number
        target = (lax.div(block, replicas), lax.rem(block, replicas))
        return block, remote(head_sums.at[number], head_mine, share_send.at[number], share_recv, target)

    @pl.when(is_last)
    def _():
        part = matmul(
            head_ins[...].reshape(rows_all, width),
            head_slopes[...].reshape(rows_all, head_slopes.shape[2]),
            TN,
        )
        head_parts[...] = part.reshape(head_parts.shape)

        def send(offset, unused):
            term_copy(offset).start()
            return unused

        lax.fori_loop(1, replicas, send, 0)

    ring_turns(0)
    for matrix in range(2):
        early_copy(matrix).wait_recv()

        def add_early(number, unused, matrix=matrix):
            rows = pl.ds(pl.multiple_of(side * side_rows + number * chunk, chunk), chunk)
            from_rows = pl.ds(pl.multiple_of(number * chunk, chunk), chunk)
            total = products[matrix, rows, main:half].astype(F32) + (
                early[matrix, from_rows].astype(F32)
            )
            products[matrix, rows, main:half] = total.astype(BF16)
            return unused

        lax.fori_loop(0, levels, add_early, 0)
    ring_start(1)

    def across_copy(matrix):
        return remote(
            products.at[matrix, rows_of(0, level), 0:main],
            across.at[matrix],
            across_send.at[matrix],
            across_recv.at[matrix],
            opposite,
        )

    for matrix in range(2):
        products[matrix, rows_of(0, level), 0:main] = ring_total(0, matrix).astype(BF16)
        across_copy(matrix).start()
    ring_turns(1)

    def mate_copy(matrix):
        return remote(
            halves.at[matrix, 1 - core], mates.at[matrix], mate_send.at[matrix], mate_recv.at[matrix], mate
        )

    mine = pl.ds(pl.multiple_of(core * half, half), half)
    theirs = pl.ds(pl.multiple_of((1 - core) * half, half), half)
    for matrix, result in ((0, down_out), (1, up_out)):
        total = ring_total(1, matrix) / LOSS_SCALE
        across_copy(matrix).wait_recv()
        other = across[matrix].astype(F32) / LOSS_SCALE
        halves[matrix, :, :, 0:main] = (total[:, 0:main] + other).reshape(2, share, main)
        halves[matrix, :, :, main:half] = total[:, main:half].reshape(2, share, half - main)
        mate_copy(matrix).start()
        result[:, mine] = halves[matrix, core]

    @pl.when(is_last)
    def _():
        def add_term(offset, total):
            term_wait(offset)
            return total + head_terms[lax.rem(me + offset, replicas)]

        total = lax.fori_loop(1, replicas, add_term, head_parts[me]) / LOSS_SCALE
        for number in range(sections):
            head_sums[number] = total[number * final : (number + 1) * final]
        for number in range(sections):
            block, copy = share_copy(number)
            to_me = block == (sections - 1) * replicas + me

            @pl.when(to_me)
            def _():
                head_mine[...] = head_sums[number]

            @pl.when(jnp.logical_not(to_me))
            def _():
                copy.start()

    for matrix, result in ((0, down_out), (1, up_out)):
        mate_copy(matrix).wait_recv()
        result[:, theirs] = mates[matrix]

    @pl.when(jnp.logical_not(source_is_me))
    def _():
        share_copy(0)[1].wait_recv()

    head_out[...] = head_mine[...]

    normed_copy.wait_send()
    active_copy.wait_send()

    def slot_left(slot, unused):
        pass_cot(slot).wait_send()
        pass_back(slot).wait_send()
        return unused

    lax.fori_loop(0, units, slot_left, 0)

    @pl.when(not_first)
    def _():
        def cot_left(slot, unused):
            cot_copy(slot).wait_send()
            return unused

        lax.fori_loop(0, units, cot_left, 0)

    for phase in range(2):
        for matrix, way in chains:
            for hop in range(hops(matrix, way)):
                ring_copy(phase, matrix, way, hop).wait_send()
    for matrix in range(2):
        early_copy(matrix).wait_send()
        across_copy(matrix).wait_send()
        mate_copy(matrix).wait_send()

    @pl.when(is_last)
    def _():
        def head_left(offset, unused):
            term_copy(offset).wait_send()
            return unused

        lax.fori_loop(1, replicas, head_left, 0)

        def gather_left(offset, unused):
            gather_copy(offset).wait_send()
            return unused

        lax.fori_loop(1, positions, gather_left, 0)
        gather_mate(core).wait_send()
        for number in range(sections):
            block, copy = share_copy(number)

            @pl.when(block != (sections - 1) * replicas + me)
            def _():
                copy.wait_send()


def hand_out(*refs):
    sources, results, sem = refs[:4], refs[4:8], refs[8]
    copies = [
        pltpu.make_async_copy(source, result, sem.at[number])
        for number, (source, result) in enumerate(zip(sources, results))
    ]
    for copy in copies:
        copy.start()
    for copy in copies:
        copy.wait()


def local(
    sections,
    replicas,
    saved_inputs,
    norm_gain,
    down_weight,
    up_weight,
    head_weight,
    head_gain,
    targets,
    levels,
    level_index,
    plan,
):
    micro, tokens, width = saved_inputs.shape[1:]
    units = down_weight.shape[2]
    half = units // 2
    cols = head_weight.shape[1]
    rings = replicas // 4
    chunk = width // (2 * rings)
    share = width // replicas
    final = share // sections
    unit = tokens // 2
    units_all = 2 * micro
    main = half - half // 4
    longest = rings // 2
    whole = pl.BlockSpec(memory_space=pltpu.VMEM)
    anywhere = pl.BlockSpec(memory_space=pl.ANY)
    dma = pltpu.SemaphoreType.DMA
    grads, down_grad, up_grad, head_grad = pl.pallas_call(
        functools.partial(body, sections, replicas),
        out_shape=(
            jax.ShapeDtypeStruct((units_all, unit, width), BF16),
            jax.ShapeDtypeStruct((share, units), F32),
            jax.ShapeDtypeStruct((share, units), F32),
            jax.ShapeDtypeStruct((final, cols), F32),
        ),
        in_specs=[
            pl.BlockSpec(memory_space=pltpu.SMEM),
            whole,
            anywhere,
            whole,
            anywhere,
            anywhere,
            whole,
            whole,
            whole,
            whole,
        ],
        out_specs=(whole, whole, whole, whole),
        scratch_shapes=[
            pltpu.VMEM((micro, tokens, width), BF16),
            pltpu.VMEM((width, units), BF16),
            pltpu.VMEM((width, units), BF16),
            pltpu.VMEM((units, width), BF16),
            pltpu.VMEM((units_all, unit, width), BF16),
            pltpu.VMEM((units_all, unit, 1), F32),
            pltpu.VMEM((2, units_all, unit, width), BF16),
            pltpu.VMEM((3, units_all, unit, half), BF16),
            pltpu.VMEM((2, units_all, unit, half), F32),
            pltpu.VMEM((2, units_all, unit, width), BF16),
            pltpu.VMEM((3, units_all, unit, half), BF16),
            pltpu.VMEM((2, width, half), BF16),
            pltpu.VMEM((2, width // 2, half - main), BF16),
            pltpu.VMEM((2, 2, longest, chunk, main), BF16),
            pltpu.VMEM((2, 2, longest, chunk, half), BF16),
            pltpu.VMEM((2, chunk, main), BF16),
            pltpu.VMEM((2, 2, share, half), F32),
            pltpu.VMEM((2, share, half), F32),
            pltpu.VMEM((replicas // 2, 2, share, cols), BF16),
            pltpu.VMEM((units_all, unit, width), BF16),
            pltpu.VMEM((units_all, unit, width), BF16),
            pltpu.VMEM((units_all, unit, cols), BF16),
            pltpu.VMEM((replicas, share, cols), F32),
            pltpu.VMEM((replicas, share, cols), F32),
            pltpu.VMEM((sections, final, cols), F32),
            pltpu.VMEM((final, cols), F32),
            dma((3,)),
            dma((units_all,)),
            dma((units_all,)),
            dma((2,)),
            dma((2,)),
            dma((2, units_all)),
            dma((2, units_all)),
            dma((2,)),
            dma((2,)),
            dma((2, 2, 2, longest)),
            dma((2, 2, 2, longest)),
            dma((2,)),
            dma((2,)),
            dma((2,)),
            dma((2,)),
            dma((replicas // 2,)),
            dma((replicas // 2 + 1,)),
            dma((replicas,)),
            dma((replicas,)),
            dma((sections,)),
            dma(()),
        ],
        compiler_params=pltpu.CompilerParams(
            collective_id=0, has_side_effects=True, vmem_limit_bytes=56 * 1024 * 1024
        ),
    )(
        plan,
        level_index.reshape(1, -1),
        saved_inputs[0],
        norm_gain,
        down_weight[0],
        up_weight[0],
        head_weight,
        head_gain.reshape(1, -1),
        targets,
        levels.T,
    )
    grads, down_grad, up_grad, head_grad = pl.pallas_call(
        hand_out,
        out_shape=tuple(
            jax.ShapeDtypeStruct(value.shape, value.dtype)
            for value in (grads, down_grad, up_grad, head_grad)
        ),
        in_specs=[anywhere] * 4,
        out_specs=(anywhere,) * 4,
        scratch_shapes=[dma((4,))],
    )(grads, down_grad, up_grad, head_grad)
    return grads.reshape(1, micro, tokens, width), down_grad[None], up_grad[None], head_grad


def solution(mesh):
    return jax.shard_map(
        functools.partial(local, mesh.shape["section"], mesh.shape["dp"]),
        mesh=mesh,
        in_specs=(
            P("section", None, "dp", None),
            P("section", None),
            P("section", None, None),
            P("section", None, None),
            P("dp", None),
            P(),
            P(None, "dp", None),
            P(),
            P(),
            P(),
        ),
        out_specs=(
            P("section", None, "dp", None),
            P("section", "dp", None),
            P("section", "dp", None),
            P(("section", "dp"), None),
        ),
        check_vma=False,
    )
```

```python
import functools

import jax
import jax.numpy as jnp
from jax import lax
from jax.experimental import pallas as pl
from jax.experimental.pallas import tpu as pltpu
from jax.sharding import PartitionSpec as P

EPS = 1e-06
DELTA = 0.25
BETA = 0.25
LOSS_SCALE = 64.0
SQRT_HALF = 0.7071067811865476
INV_SQRT_TAU = 0.3989422804014327
MESH = pl.DeviceIdType.MESH
F32 = jnp.float32
BF16 = jnp.bfloat16
NN = (((1,), (0,)), ((), ()))
NT = (((1,), (1,)), ((), ()))
TN = (((0,), (0,)), ((), ()))


def matmul(left, right, dims=NN):
    return lax.dot_general(left, right, dims, preferred_element_type=F32)


def inverse_rms(values):
    return lax.rsqrt(jnp.mean(values * values, axis=-1, keepdims=True) + EPS)


def norm_backward(values, inverse, scaling, upstream):
    weighted = upstream * scaling
    mean = jnp.mean(weighted * values, axis=-1, keepdims=True)
    return inverse * weighted - values * (inverse * inverse * inverse) * mean


def soft(values):
    return values * lax.rsqrt(values * values + DELTA * DELTA)


def chain(values, threshold):
    shifted = (values - threshold) / BETA
    softplus = jnp.maximum(shifted, 0.0) + jnp.log1p(jnp.exp(-jnp.abs(shifted)))
    return threshold + BETA * softplus


def chain_rate(values, threshold):
    shifted = (values - threshold) / BETA
    small = jnp.exp(-jnp.abs(shifted))
    return jnp.where(shifted >= 0.0, 1.0, small) / (1.0 + small)


def crps_slope(predicted, observed, threshold):
    variables = observed.shape[1]
    first, second = predicted[:, :variables], predicted[:, variables:]
    chain_first, chain_second = chain(first, threshold), chain(second, threshold)
    chain_obs = chain(observed, threshold)
    pair = soft(chain_first - chain_second)
    slope_first = soft(chain_first - chain_obs) / 2 - pair / 4
    slope_second = soft(chain_second - chain_obs) / 2 + pair / 4
    return jnp.concatenate(
        [
            LOSS_SCALE * chain_rate(first, threshold) * slope_first,
            LOSS_SCALE * chain_rate(second, threshold) * slope_second,
        ],
        axis=1,
    )


def body(
    sections,
    replicas,
    plan_ref,
    index_ref,
    saved_ref,
    gain_ref,
    down_ref,
    up_ref,
    head_ref,
    head_gain_ref,
    targets_ref,
    levels_ref,
    grads_out,
    down_out,
    up_out,
    head_out,
    saved,
    down,
    up,
    down_turned,
    wide,
    inverses,
    normed,
    active,
    slopes,
    cots,
    backs,
    products,
    early,
    ring_other,
    ring_own,
    across,
    halves,
    mates,
    full_head,
    outputs,
    head_ins,
    head_slopes,
    head_parts,
    head_terms,
    head_sums,
    head_mine,
    load_sem,
    cot_send,
    cot_recv,
    pair_send,
    pair_recv,
    slot_send,
    slot_recv,
    early_send,
    early_recv,
    ring_send,
    ring_recv,
    across_send,
    across_recv,
    mate_send,
    mate_recv,
    gather_send,
    gather_recv,
    term_send,
    term_recv,
    share_send,
    share_recv,
):
    units, unit, width = wide.shape
    micro = saved.shape[0]
    per_slot = units // micro
    rows_all = units * unit
    half = active.shape[-1]
    levels = replicas // 4
    positions = replicas // 2
    chunk = width // (2 * levels)
    side_rows = width // 2
    main = ring_other.shape[-1]
    share = width // replicas
    final = head_mine.shape[0]

    section = lax.axis_index("section")
    me = lax.axis_index("dp")
    core = lax.rem(me, 2)
    level = lax.rem(lax.div(me, 2), levels)
    side = lax.div(me, 2 * levels)
    is_last = section == sections - 1
    not_last = section < sections - 1
    not_first = section > 0

    def member(side_of, level_of, core_of):
        return (section, (side_of * levels + level_of) * 2 + core_of)

    ahead = member(side, lax.rem(level + 1, levels), core)
    behind = member(side, lax.rem(level + levels - 1, levels), core)
    mate = member(side, level, 1 - core)
    opposite = member(1 - side, level, core)
    sender = (lax.rem(section + 1, sections), me)
    receiver = (lax.rem(section + sections - 1, sections), me)
    head_source = lax.div(section * replicas + me, sections)
    source_is_me = jnp.logical_and(is_last, head_source == me)

    def remote(src, dst, send, recv, device):
        return pltpu.make_async_remote_copy(
            src_ref=src,
            dst_ref=dst,
            send_sem=send,
            recv_sem=recv,
            device_id=device,
            device_id_type=MESH,
        )

    saved_load = pltpu.make_async_copy(saved_ref, saved, load_sem.at[0])
    down_load = pltpu.make_async_copy(down_ref, down, load_sem.at[1])
    up_load = pltpu.make_async_copy(up_ref, up, load_sem.at[2])
    saved_load.start()
    down_load.start()
    up_load.start()

    barrier = pltpu.get_barrier_semaphore()

    def greet(device):
        pl.semaphore_signal(barrier, inc=1, device_id=device, device_id_type=MESH)

    @pl.when(not_last)
    def _():
        greet(sender)
        for device in (ahead, behind, mate, opposite):
            greet(device)

    @pl.when(is_last)
    def _():
        def greet_peer(offset, unused):
            greet((section, lax.rem(me + offset, replicas)))
            return unused

        lax.fori_loop(1, replicas, greet_peer, 0)

    @pl.when(jnp.logical_not(source_is_me))
    def _():
        greet((sections - 1, head_source))

    saved_load.wait()

    def norm_slot(slot, unused):
        values = saved[plan_ref[slot]]
        these = pl.ds(slot * per_slot, per_slot)
        wide[these] = values.reshape(per_slot, unit, width)
        values = values.astype(F32)
        inverse = inverse_rms(values)
        inverses[these] = inverse.reshape(per_slot, unit, 1)
        normed[0, these] = (
            (values * inverse * gain_ref[...]).astype(BF16).reshape(per_slot, unit, width)
        )
        return unused

    lax.fori_loop(0, micro, norm_slot, 0)

    heard = jnp.where(
        is_last,
        replicas + sections - jnp.where(me == replicas - 1, 1, 0),
        4 + jnp.where(not_first, 1, 0),
    )
    pl.semaphore_wait(barrier, heard)

    position = side * levels + level

    def gather_copy(offset):
        peer = lax.rem(position + offset, positions)
        return remote(
            head_ref,
            full_head.at[position, core],
            gather_send.at[offset],
            gather_recv.at[position],
            (section, peer * 2 + core),
        )

    def gather_wait(offset):
        peer = lax.rem(position + offset, positions)
        remote(
            head_ref,
            full_head.at[peer, core],
            gather_send.at[offset],
            gather_recv.at[peer],
            (section, peer * 2 + core),
        ).wait_recv()

    def gather_mate(which):
        return remote(
            full_head.at[:, which],
            full_head.at[:, which],
            gather_send.at[0],
            gather_recv.at[positions],
            mate,
        )

    @pl.when(is_last)
    def _():
        def send(offset, unused):
            gather_copy(offset).start()
            return unused

        lax.fori_loop(1, positions, send, 0)
        full_head[position, core] = head_ref[...]

    normed_copy = remote(normed.at[0], normed.at[1], pair_send.at[0], pair_recv.at[0], mate)
    normed_copy.start()

    down_load.wait()
    step = min(256, half)
    all_normed = normed[0].reshape(rows_all, width)
    for part in range(2):
        where = 2 * lax.rem(core + part, 2)

        def forward(number, unused, part=part, where=where):
            columns = pl.ds(pl.multiple_of(part * half + number * step, step), step)
            inner = pl.ds(pl.multiple_of(number * step, step), step)
            hidden = matmul(all_normed, down[:, columns])
            bell = 0.5 * (1.0 + lax.erf(hidden * SQRT_HALF))
            active[where, :, :, inner] = (
                (hidden * bell).astype(BF16).reshape(units, unit, step)
            )
            slope = bell + hidden * jnp.exp(-0.5 * hidden * hidden) * INV_SQRT_TAU
            slopes[part, :, :, inner] = slope.reshape(units, unit, step)
            return unused

        lax.fori_loop(0, half // step, forward, 0)

    active_copy = remote(active.at[2], active.at[1], pair_send.at[1], pair_recv.at[1], mate)
    active_copy.start()
    up_load.wait()

    @pl.when(is_last)
    def _():
        wide_step = min(256, width)

        def output_columns(number, unused):
            columns = pl.ds(pl.multiple_of(number * wide_step, wide_step), wide_step)
            total = wide[:, :, columns].astype(F32).reshape(rows_all, wide_step)
            for part in range(2):
                where = 2 * lax.rem(core + part, 2)
                total = total + matmul(
                    active[where].reshape(rows_all, half),
                    up[columns, part * half : (part + 1) * half],
                    NT,
                )
            outputs[:, :, columns] = total.astype(BF16).reshape(units, unit, wide_step)
            return unused

        lax.fori_loop(0, width // wide_step, output_columns, 0)

        def arrive(offset, unused):
            gather_wait(offset)
            return unused

        lax.fori_loop(1, positions, arrive, 0)
        gather_mate(core).start()
        gather_mate(1 - core).wait_recv()

    @pl.when(not_last)
    def _():
        turn_step = min(256, width)

        def turn_columns(number, unused):
            block = pl.ds(pl.multiple_of(number * turn_step, turn_step), turn_step)
            down_turned[block, :] = down[:, block].T
            return unused

        lax.fori_loop(0, 2 * half // turn_step, turn_columns, 0)

    def head_slot(slot):
        these = pl.ds(slot * per_slot, per_slot)
        rows = per_slot * unit
        choice = lax.broadcasted_iota(jnp.int32, levels_ref.shape, 0) == index_ref[...]
        threshold = jnp.sum(jnp.where(choice, levels_ref[...], 0.0), axis=0, keepdims=True)
        head = full_head[...].reshape(width, full_head.shape[3])
        values = outputs[these].astype(F32).reshape(rows, width)
        inverse = inverse_rms(values)
        head_in = (values * inverse * head_gain_ref[...]).astype(BF16)
        head_ins[these] = head_in.reshape(per_slot, unit, width)
        predicted = matmul(head_in, head)
        slope = crps_slope(predicted, targets_ref[plan_ref[slot]], threshold).astype(BF16)
        head_slopes[these] = slope.reshape(per_slot, unit, slope.shape[1])
        upstream = matmul(slope, head, NT)
        cotangent = norm_backward(values, inverse, head_gain_ref[...], upstream)
        cots[0, these] = cotangent.astype(BF16).reshape(per_slot, unit, width)

    def cot_copy(slot):
        return remote(
            grads_out.at[slot], cots.at[0, slot], cot_send.at[slot], cot_recv.at[slot], receiver
        )

    def pass_cot(slot):
        return remote(
            cots.at[0, slot], cots.at[1, slot], slot_send.at[0, slot], slot_recv.at[0, slot], mate
        )

    def pass_back(slot):
        return remote(
            backs.at[2, slot], backs.at[1, slot], slot_send.at[1, slot], slot_recv.at[1, slot], mate
        )

    def backward(first, count, turned):
        these = pl.ds(first, count)
        rows = count * unit
        cotangent = cots[0, these].reshape(rows, width)
        back_normed = jnp.zeros((rows, width), F32)
        for part in range(2):
            columns = slice(part * half, (part + 1) * half)
            back_active = matmul(cotangent, up[:, columns])
            back = (back_active * slopes[part, these].reshape(rows, half)).astype(BF16)
            backs[2 * lax.rem(core + part, 2), these] = back.reshape(count, unit, half)
            if turned:
                back_normed = back_normed + matmul(back, down_turned[columns, :])
            else:
                back_normed = back_normed + matmul(back, down[:, columns], NT)
        values = wide[these].astype(F32).reshape(rows, width)
        correction = norm_backward(
            values, inverses[these].reshape(rows, 1), gain_ref[...], back_normed
        )
        grads_out[these] = (
            (cotangent.astype(F32) + correction).astype(BF16).reshape(count, unit, width)
        )

        @pl.when(not_first)
        def _():
            for number in range(count):
                cot_copy(first + number).start()

        for number in range(count):
            pass_cot(first + number).start()
            pass_back(first + number).start()

    @pl.when(is_last)
    def _():
        def from_head(slot, unused):
            head_slot(slot)
            backward(slot * per_slot, per_slot, False)
            return unused

        lax.fori_loop(0, micro, from_head, 0)

    @pl.when(not_last)
    def _():
        def from_next(number, unused):
            cot_copy(number).wait_recv()
            backward(number, 1, True)
            return unused

        lax.fori_loop(0, units, from_next, 0)

    def slot_arrived(slot, unused):
        pass_cot(slot).wait_recv()
        pass_back(slot).wait_recv()
        return unused

    normed_copy.wait_recv()
    active_copy.wait_recv()
    lax.fori_loop(0, units, slot_arrived, 0)
    row_step = min(256, side_rows)

    def multiply(of_side):
        def block(number, unused):
            first = of_side * side_rows + number * row_step
            rows = pl.ds(pl.multiple_of(first, row_step), row_step)
            for matrix, left, right in ((1, cots, active), (0, normed, backs)):
                products[matrix, rows] = matmul(
                    left[:, :, :, rows].reshape(2 * rows_all, row_step),
                    right[0:2].reshape(2 * rows_all, half),
                    TN,
                ).astype(BF16)
            return unused

        lax.fori_loop(0, side_rows // row_step, block, 0)

    multiply(1 - side)
    theirs_rows = pl.ds(pl.multiple_of((1 - side) * side_rows, side_rows), side_rows)

    def early_copy(matrix):
        return remote(
            products.at[matrix, theirs_rows, main:half],
            early.at[matrix],
            early_send.at[matrix],
            early_recv.at[matrix],
            opposite,
        )

    for matrix in range(2):
        early_copy(matrix).start()

    longest = levels // 2
    chains = ((0, 0), (1, 1), (1, 0), (0, 1))

    def hops(matrix, way):
        return longest if matrix == way else longest - 1

    def rows_of(phase, position):
        side_of = 1 - side if phase == 0 else side
        return pl.ds(pl.multiple_of((side_of * levels + position) * chunk, chunk), chunk)

    def ring_rows(phase, matrix, way, hop):
        left = hops(matrix, way) - hop
        return rows_of(phase, lax.rem(level + levels + (left if way == 0 else -left), levels))

    def ring_copy(phase, matrix, way, hop):
        rows = ring_rows(phase, matrix, way, hop)
        buffer = ring_other if phase == 0 else ring_own
        source = products.at[matrix, rows, 0:main] if phase == 0 else products.at[matrix, rows]
        return remote(
            source,
            buffer.at[matrix, way, hop],
            ring_send.at[phase, matrix, way, hop],
            ring_recv.at[phase, matrix, way, hop],
            ahead if way == 0 else behind,
        )

    def ring_start(phase):
        for matrix, way in chains:
            ring_copy(phase, matrix, way, 0).start()

    def ring_turns(phase):
        buffer = ring_other if phase == 0 else ring_own
        span = buffer.shape[-1]
        for hop in range(1, longest):
            for matrix, way in chains:
                if hop < hops(matrix, way):
                    ring_copy(phase, matrix, way, hop - 1).wait_recv()
                    rows = ring_rows(phase, matrix, way, hop)
                    total = products[matrix, rows, 0:span].astype(F32) + (
                        buffer[matrix, way, hop - 1].astype(F32)
                    )
                    products[matrix, rows, 0:span] = total.astype(BF16)
                    ring_copy(phase, matrix, way, hop).start()

    def ring_total(phase, matrix):
        buffer = ring_other if phase == 0 else ring_own
        total = products[matrix, rows_of(phase, level), 0 : buffer.shape[-1]].astype(F32)
        for way in (1, 0) if matrix == 0 else (0, 1):
            last = hops(matrix, way) - 1
            ring_copy(phase, matrix, way, last).wait_recv()
            total = total + buffer[matrix, way, last].astype(F32)
        return total

    ring_start(0)
    multiply(side)

    def term_copy(offset):
        peer = lax.rem(me + offset, replicas)
        return remote(
            head_parts.at[peer], head_terms.at[me], term_send.at[offset], term_recv.at[me], (section, peer)
        )

    def term_wait(offset):
        peer = lax.rem(me + offset, replicas)
        remote(
            head_parts.at[peer], head_terms.at[peer], term_send.at[offset], term_recv.at[peer], (section, peer)
        ).wait_recv()

    def share_copy(number):
        block = sections * me + number
        target = (lax.div(block, replicas), lax.rem(block, replicas))
        return block, remote(head_sums.at[number], head_mine, share_send.at[number], share_recv, target)

    @pl.when(is_last)
    def _():
        part = matmul(
            head_ins[...].reshape(rows_all, width),
            head_slopes[...].reshape(rows_all, head_slopes.shape[2]),
            TN,
        )
        head_parts[...] = part.reshape(head_parts.shape)

        def send(offset, unused):
            term_copy(offset).start()
            return unused

        lax.fori_loop(1, replicas, send, 0)

    ring_turns(0)
    for matrix in range(2):
        early_copy(matrix).wait_recv()

        def add_early(number, unused, matrix=matrix):
            rows = pl.ds(pl.multiple_of(side * side_rows + number * chunk, chunk), chunk)
            from_rows = pl.ds(pl.multiple_of(number * chunk, chunk), chunk)
            total = products[matrix, rows, main:half].astype(F32) + (
                early[matrix, from_rows].astype(F32)
            )
            products[matrix, rows, main:half] = total.astype(BF16)
            return unused

        lax.fori_loop(0, levels, add_early, 0)
    ring_start(1)

    def across_copy(matrix):
        return remote(
            products.at[matrix, rows_of(0, level), 0:main],
            across.at[matrix],
            across_send.at[matrix],
            across_recv.at[matrix],
            opposite,
        )

    for matrix in range(2):
        products[matrix, rows_of(0, level), 0:main] = ring_total(0, matrix).astype(BF16)
        across_copy(matrix).start()
    ring_turns(1)

    def mate_copy(matrix):
        return remote(
            halves.at[matrix, 1 - core], mates.at[matrix], mate_send.at[matrix], mate_recv.at[matrix], mate
        )

    mine = pl.ds(pl.multiple_of(core * half, half), half)
    theirs = pl.ds(pl.multiple_of((1 - core) * half, half), half)
    for matrix, result in ((0, down_out), (1, up_out)):
        total = ring_total(1, matrix) / LOSS_SCALE
        across_copy(matrix).wait_recv()
        other = across[matrix].astype(F32) / LOSS_SCALE
        halves[matrix, :, :, 0:main] = (total[:, 0:main] + other).reshape(2, share, main)
        halves[matrix, :, :, main:half] = total[:, main:half].reshape(2, share, half - main)
        mate_copy(matrix).start()
        result[:, mine] = halves[matrix, core]

    @pl.when(is_last)
    def _():
        def add_term(offset, total):
            term_wait(offset)
            return total + head_terms[lax.rem(me + offset, replicas)]

        total = lax.fori_loop(1, replicas, add_term, head_parts[me]) / LOSS_SCALE
        for number in range(sections):
            head_sums[number] = total[number * final : (number + 1) * final]
        for number in range(sections):
            block, copy = share_copy(number)
            to_me = block == (sections - 1) * replicas + me

            @pl.when(to_me)
            def _():
                head_mine[...] = head_sums[number]

            @pl.when(jnp.logical_not(to_me))
            def _():
                copy.start()

    for matrix, result in ((0, down_out), (1, up_out)):
        mate_copy(matrix).wait_recv()
        result[:, theirs] = mates[matrix]

    @pl.when(jnp.logical_not(source_is_me))
    def _():
        share_copy(0)[1].wait_recv()

    head_out[...] = head_mine[...]

    normed_copy.wait_send()
    active_copy.wait_send()

    def slot_left(slot, unused):
        pass_cot(slot).wait_send()
        pass_back(slot).wait_send()
        return unused

    lax.fori_loop(0, units, slot_left, 0)

    @pl.when(not_first)
    def _():
        def cot_left(slot, unused):
            cot_copy(slot).wait_send()
            return unused

        lax.fori_loop(0, units, cot_left, 0)

    for phase in range(2):
        for matrix, way in chains:
            for hop in range(hops(matrix, way)):
                ring_copy(phase, matrix, way, hop).wait_send()
    for matrix in range(2):
        early_copy(matrix).wait_send()
        across_copy(matrix).wait_send()
        mate_copy(matrix).wait_send()

    @pl.when(is_last)
    def _():
        def head_left(offset, unused):
            term_copy(offset).wait_send()
            return unused

        lax.fori_loop(1, replicas, head_left, 0)

        def gather_left(offset, unused):
            gather_copy(offset).wait_send()
            return unused

        lax.fori_loop(1, positions, gather_left, 0)
        gather_mate(core).wait_send()
        for number in range(sections):
            block, copy = share_copy(number)

            @pl.when(block != (sections - 1) * replicas + me)
            def _():
                copy.wait_send()


def hand_out(*refs):
    sources, results, held, sem = refs[:4], refs[4:8], refs[8:12], refs[12]
    incoming = [
        pltpu.make_async_copy(source, middle, sem.at[0, number])
        for number, (source, middle) in enumerate(zip(sources, held))
    ]
    outgoing = [
        pltpu.make_async_copy(middle, result, sem.at[1, number])
        for number, (middle, result) in enumerate(zip(held, results))
    ]
    for copy in incoming:
        copy.start()
    for arrival, copy in zip(incoming, outgoing):
        arrival.wait()
        copy.start()
    for copy in outgoing:
        copy.wait()


def local(
    sections,
    replicas,
    saved_inputs,
    norm_gain,
    down_weight,
    up_weight,
    head_weight,
    head_gain,
    targets,
    levels,
    level_index,
    plan,
):
    micro, tokens, width = saved_inputs.shape[1:]
    units = down_weight.shape[2]
    half = units // 2
    cols = head_weight.shape[1]
    rings = replicas // 4
    chunk = width // (2 * rings)
    share = width // replicas
    final = share // sections
    unit = tokens // 2
    units_all = 2 * micro
    main = half - half // 4
    longest = rings // 2
    whole = pl.BlockSpec(memory_space=pltpu.VMEM)
    anywhere = pl.BlockSpec(memory_space=pl.ANY)
    dma = pltpu.SemaphoreType.DMA
    grads, down_grad, up_grad, head_grad = pl.pallas_call(
        functools.partial(body, sections, replicas),
        out_shape=(
            jax.ShapeDtypeStruct((units_all, unit, width), BF16),
            jax.ShapeDtypeStruct((share, units), F32),
            jax.ShapeDtypeStruct((share, units), F32),
            jax.ShapeDtypeStruct((final, cols), F32),
        ),
        in_specs=[
            pl.BlockSpec(memory_space=pltpu.SMEM),
            whole,
            anywhere,
            whole,
            anywhere,
            anywhere,
            whole,
            whole,
            whole,
            whole,
        ],
        out_specs=(whole, whole, whole, whole),
        scratch_shapes=[
            pltpu.VMEM((micro, tokens, width), BF16),
            pltpu.VMEM((width, units), BF16),
            pltpu.VMEM((width, units), BF16),
            pltpu.VMEM((units, width), BF16),
            pltpu.VMEM((units_all, unit, width), BF16),
            pltpu.VMEM((units_all, unit, 1), F32),
            pltpu.VMEM((2, units_all, unit, width), BF16),
            pltpu.VMEM((3, units_all, unit, half), BF16),
            pltpu.VMEM((2, units_all, unit, half), F32),
            pltpu.VMEM((2, units_all, unit, width), BF16),
            pltpu.VMEM((3, units_all, unit, half), BF16),
            pltpu.VMEM((2, width, half), BF16),
            pltpu.VMEM((2, width // 2, half - main), BF16),
            pltpu.VMEM((2, 2, longest, chunk, main), BF16),
            pltpu.VMEM((2, 2, longest, chunk, half), BF16),
            pltpu.VMEM((2, chunk, main), BF16),
            pltpu.VMEM((2, 2, share, half), F32),
            pltpu.VMEM((2, share, half), F32),
            pltpu.VMEM((replicas // 2, 2, share, cols), BF16),
            pltpu.VMEM((units_all, unit, width), BF16),
            pltpu.VMEM((units_all, unit, width), BF16),
            pltpu.VMEM((units_all, unit, cols), BF16),
            pltpu.VMEM((replicas, share, cols), F32),
            pltpu.VMEM((replicas, share, cols), F32),
            pltpu.VMEM((sections, final, cols), F32),
            pltpu.VMEM((final, cols), F32),
            dma((3,)),
            dma((units_all,)),
            dma((units_all,)),
            dma((2,)),
            dma((2,)),
            dma((2, units_all)),
            dma((2, units_all)),
            dma((2,)),
            dma((2,)),
            dma((2, 2, 2, longest)),
            dma((2, 2, 2, longest)),
            dma((2,)),
            dma((2,)),
            dma((2,)),
            dma((2,)),
            dma((replicas // 2,)),
            dma((replicas // 2 + 1,)),
            dma((replicas,)),
            dma((replicas,)),
            dma((sections,)),
            dma(()),
        ],
        compiler_params=pltpu.CompilerParams(
            collective_id=0, has_side_effects=True, vmem_limit_bytes=56 * 1024 * 1024
        ),
    )(
        plan,
        level_index.reshape(1, -1),
        saved_inputs[0],
        norm_gain,
        down_weight[0],
        up_weight[0],
        head_weight,
        head_gain.reshape(1, -1),
        targets,
        levels.T,
    )
    grads, down_grad, up_grad, head_grad = pl.pallas_call(
        hand_out,
        out_shape=tuple(
            jax.ShapeDtypeStruct(value.shape, value.dtype)
            for value in (grads, down_grad, up_grad, head_grad)
        ),
        in_specs=[anywhere] * 4,
        out_specs=(anywhere,) * 4,
        scratch_shapes=[
            pltpu.VMEM(value.shape, value.dtype)
            for value in (grads, down_grad, up_grad, head_grad)
        ]
        + [dma((2, 4))],
    )(grads, down_grad, up_grad, head_grad)
    return grads.reshape(1, micro, tokens, width), down_grad[None], up_grad[None], head_grad


def solution(mesh):
    return jax.shard_map(
        functools.partial(local, mesh.shape["section"], mesh.shape["dp"]),
        mesh=mesh,
        in_specs=(
            P("section", None, "dp", None),
            P("section", None),
            P("section", None, None),
            P("section", None, None),
            P("dp", None),
            P(),
            P(None, "dp", None),
            P(),
            P(),
            P(),
        ),
        out_specs=(
            P("section", None, "dp", None),
            P("section", "dp", None),
            P("section", "dp", None),
            P(("section", "dp"), None),
        ),
        check_vma=False,
    )
```

```python
import functools

import jax
import jax.numpy as jnp
from jax import lax
from jax.experimental import pallas as pl
from jax.experimental.pallas import tpu as pltpu
from jax.sharding import PartitionSpec as P

EPS = 1e-06
DELTA = 0.25
BETA = 0.25
LOSS_SCALE = 64.0
SQRT_HALF = 0.7071067811865476
INV_SQRT_TAU = 0.3989422804014327
MESH = pl.DeviceIdType.MESH
F32 = jnp.float32
BF16 = jnp.bfloat16
NN = (((1,), (0,)), ((), ()))
NT = (((1,), (1,)), ((), ()))
TN = (((0,), (0,)), ((), ()))


def matmul(left, right, dims=NN):
    return lax.dot_general(left, right, dims, preferred_element_type=F32)


def inverse_rms(values):
    return lax.rsqrt(jnp.mean(values * values, axis=-1, keepdims=True) + EPS)


def norm_backward(values, inverse, scaling, upstream):
    weighted = upstream * scaling
    mean = jnp.mean(weighted * values, axis=-1, keepdims=True)
    return inverse * weighted - values * (inverse * inverse * inverse) * mean


def soft(values):
    return values * lax.rsqrt(values * values + DELTA * DELTA)


def chain(values, threshold):
    shifted = (values - threshold) / BETA
    softplus = jnp.maximum(shifted, 0.0) + jnp.log1p(jnp.exp(-jnp.abs(shifted)))
    return threshold + BETA * softplus


def chain_rate(values, threshold):
    shifted = (values - threshold) / BETA
    small = jnp.exp(-jnp.abs(shifted))
    return jnp.where(shifted >= 0.0, 1.0, small) / (1.0 + small)


def crps_slope(predicted, observed, threshold):
    variables = observed.shape[1]
    first, second = predicted[:, :variables], predicted[:, variables:]
    chain_first, chain_second = chain(first, threshold), chain(second, threshold)
    chain_obs = chain(observed, threshold)
    pair = soft(chain_first - chain_second)
    slope_first = soft(chain_first - chain_obs) / 2 - pair / 4
    slope_second = soft(chain_second - chain_obs) / 2 + pair / 4
    return jnp.concatenate(
        [
            LOSS_SCALE * chain_rate(first, threshold) * slope_first,
            LOSS_SCALE * chain_rate(second, threshold) * slope_second,
        ],
        axis=1,
    )


def body(
    sections,
    replicas,
    plan_ref,
    index_ref,
    saved_ref,
    gain_ref,
    down_ref,
    up_ref,
    head_ref,
    head_gain_ref,
    targets_ref,
    levels_ref,
    grads_out,
    down_out,
    up_out,
    head_out,
    saved,
    down,
    up,
    down_turned,
    wide,
    inverses,
    normed,
    active,
    slopes,
    hiddens,
    cots,
    backs,
    grads,
    products,
    early,
    ring_main,
    ring_early,
    across,
    halves,
    mates,
    full_head,
    outputs,
    head_ins,
    head_slopes,
    head_parts,
    head_terms,
    head_sums,
    head_mine,
    load_sem,
    cot_send,
    cot_recv,
    pair_send,
    pair_recv,
    slot_send,
    slot_recv,
    early_send,
    early_recv,
    ring_send,
    ring_recv,
    across_send,
    across_recv,
    mate_send,
    mate_recv,
    gather_send,
    gather_recv,
    term_send,
    term_recv,
    share_send,
    share_recv,
):
    units, unit, width = wide.shape
    micro = saved.shape[0]
    per_slot = units // micro
    rows_all = units * unit
    half = active.shape[-1]
    levels = replicas // 4
    positions = replicas // 2
    chunk = width // (2 * levels)
    side_rows = width // 2
    main = ring_main.shape[-1]
    column_half = width // 2
    share = width // replicas
    final = head_mine.shape[0]

    section = lax.axis_index("section")
    me = lax.axis_index("dp")
    core = lax.rem(me, 2)
    level = lax.rem(lax.div(me, 2), levels)
    side = lax.div(me, 2 * levels)
    is_last = section == sections - 1
    not_last = section < sections - 1
    not_first = section > 0

    def member(side_of, level_of, core_of):
        return (section, (side_of * levels + level_of) * 2 + core_of)

    ahead = member(side, lax.rem(level + 1, levels), core)
    behind = member(side, lax.rem(level + levels - 1, levels), core)
    mate = member(side, level, 1 - core)
    opposite = member(1 - side, level, core)
    sender = (lax.rem(section + 1, sections), me)
    receiver = (lax.rem(section + sections - 1, sections), me)
    head_source = lax.div(section * replicas + me, sections)
    source_is_me = jnp.logical_and(is_last, head_source == me)

    def remote(src, dst, send, recv, device):
        return pltpu.make_async_remote_copy(
            src_ref=src,
            dst_ref=dst,
            send_sem=send,
            recv_sem=recv,
            device_id=device,
            device_id_type=MESH,
        )

    saved_load = pltpu.make_async_copy(saved_ref, saved, load_sem.at[0])
    down_load = pltpu.make_async_copy(down_ref, down, load_sem.at[1])
    up_load = pltpu.make_async_copy(up_ref, up, load_sem.at[2])
    saved_load.start()
    down_load.start()
    up_load.start()

    barrier = pltpu.get_barrier_semaphore()

    def greet(device):
        pl.semaphore_signal(barrier, inc=1, device_id=device, device_id_type=MESH)

    @pl.when(not_last)
    def _():
        greet(sender)
        for device in (ahead, behind, mate, opposite):
            greet(device)

    @pl.when(is_last)
    def _():
        def greet_peer(offset, unused):
            greet((section, lax.rem(me + offset, replicas)))
            return unused

        lax.fori_loop(1, replicas, greet_peer, 0)

    @pl.when(jnp.logical_not(source_is_me))
    def _():
        greet((sections - 1, head_source))

    saved_load.wait()

    def norm_slot(slot, unused):
        values = saved[plan_ref[slot]]
        these = pl.ds(slot * per_slot, per_slot)
        wide[these] = values.reshape(per_slot, unit, width)
        values = values.astype(F32)
        inverse = inverse_rms(values)
        inverses[these] = inverse.reshape(per_slot, unit, 1)
        normed[0, these] = (
            (values * inverse * gain_ref[...]).astype(BF16).reshape(per_slot, unit, width)
        )
        return unused

    lax.fori_loop(0, micro, norm_slot, 0)

    heard = jnp.where(
        is_last,
        replicas + sections - jnp.where(me == replicas - 1, 1, 0),
        4 + jnp.where(not_first, 1, 0),
    )
    pl.semaphore_wait(barrier, heard)

    position = side * levels + level

    def gather_copy(offset):
        peer = lax.rem(position + offset, positions)
        return remote(
            head_ref,
            full_head.at[position, core],
            gather_send.at[offset],
            gather_recv.at[position],
            (section, peer * 2 + core),
        )

    def gather_wait(offset):
        peer = lax.rem(position + offset, positions)
        remote(
            head_ref,
            full_head.at[peer, core],
            gather_send.at[offset],
            gather_recv.at[peer],
            (section, peer * 2 + core),
        ).wait_recv()

    def gather_mate(which):
        return remote(
            full_head.at[:, which],
            full_head.at[:, which],
            gather_send.at[0],
            gather_recv.at[positions],
            mate,
        )

    @pl.when(is_last)
    def _():
        def send(offset, unused):
            gather_copy(offset).start()
            return unused

        lax.fori_loop(1, positions, send, 0)
        full_head[position, core] = head_ref[...]

    normed_copy = remote(normed.at[0], normed.at[1], pair_send.at[0], pair_recv.at[0], mate)
    normed_copy.start()

    down_load.wait()
    step = min(256, half)
    all_normed = normed[0].reshape(rows_all, width)
    for part in range(2):
        where = 2 * lax.rem(core + part, 2)

        def forward(number, unused, part=part, where=where):
            columns = pl.ds(pl.multiple_of(part * half + number * step, step), step)
            inner = pl.ds(pl.multiple_of(number * step, step), step)
            hidden = matmul(all_normed, down[:, columns])
            bell = 0.5 * (1.0 + lax.erf(hidden * SQRT_HALF))
            active[where, :, :, inner] = (
                (hidden * bell).astype(BF16).reshape(units, unit, step)
            )
            slope = bell + hidden * jnp.exp(-0.5 * hidden * hidden) * INV_SQRT_TAU
            slopes[part, :, :, inner] = slope.reshape(units, unit, step)
            hiddens[part, :, :, inner] = hidden.reshape(units, unit, step)
            return unused

        lax.fori_loop(0, half // step, forward, 0)

    active_copy = remote(active.at[2], active.at[1], pair_send.at[1], pair_recv.at[1], mate)
    active_copy.start()
    up_load.wait()

    @pl.when(is_last)
    def _():
        wide_step = min(256, width)

        def output_columns(number, unused):
            columns = pl.ds(pl.multiple_of(number * wide_step, wide_step), wide_step)
            total = wide[:, :, columns].astype(F32).reshape(rows_all, wide_step)
            for part in range(2):
                where = 2 * lax.rem(core + part, 2)
                total = total + matmul(
                    active[where].reshape(rows_all, half),
                    up[columns, part * half : (part + 1) * half],
                    NT,
                )
            outputs[:, :, columns] = total.astype(BF16).reshape(units, unit, wide_step)
            return unused

        lax.fori_loop(0, width // wide_step, output_columns, 0)

    turn_step = min(256, width)

    def turn_columns(number, unused):
        block = pl.ds(pl.multiple_of(number * turn_step, turn_step), turn_step)
        down_turned[block, :] = down[:, block].T
        return unused

    lax.fori_loop(0, 2 * half // turn_step, turn_columns, 0)

    @pl.when(is_last)
    def _():
        def arrive(offset, unused):
            gather_wait(offset)
            return unused

        lax.fori_loop(1, positions, arrive, 0)
        gather_mate(core).start()
        gather_mate(1 - core).wait_recv()

    def head_slot(slot):
        these = pl.ds(slot * per_slot, per_slot)
        rows = per_slot * unit
        choice = lax.broadcasted_iota(jnp.int32, levels_ref.shape, 0) == index_ref[...]
        threshold = jnp.sum(jnp.where(choice, levels_ref[...], 0.0), axis=0, keepdims=True)
        head = full_head[...].reshape(width, full_head.shape[3])
        values = outputs[these].astype(F32).reshape(rows, width)
        inverse = inverse_rms(values)
        head_in = (values * inverse * head_gain_ref[...]).astype(BF16)
        head_ins[these] = head_in.reshape(per_slot, unit, width)
        predicted = matmul(head_in, head)
        slope = crps_slope(predicted, targets_ref[plan_ref[slot]], threshold).astype(BF16)
        head_slopes[these] = slope.reshape(per_slot, unit, slope.shape[1])
        upstream = matmul(slope, head, NT)
        cotangent = norm_backward(values, inverse, head_gain_ref[...], upstream)
        cots[0, these] = cotangent.astype(BF16).reshape(per_slot, unit, width)

    def cot_copy(slot, piece):
        columns = slice(piece * column_half, (piece + 1) * column_half)
        return remote(
            grads.at[slot, :, columns],
            cots.at[0, slot, :, columns],
            cot_send.at[slot, piece],
            cot_recv.at[slot, piece],
            receiver,
        )

    def pass_cot(slot):
        return remote(
            cots.at[0, slot], cots.at[1, slot], slot_send.at[0, slot], slot_recv.at[0, slot], mate
        )

    def pass_back(slot):
        return remote(
            backs.at[2, slot], backs.at[1, slot], slot_send.at[1, slot], slot_recv.at[1, slot], mate
        )

    def backward(first, count, arriving):
        these = pl.ds(first, count)
        rows = count * unit
        back_active = None
        for piece in range(2):
            if arriving:
                cot_copy(first, piece).wait_recv()
            columns = slice(piece * column_half, (piece + 1) * column_half)
            part = matmul(cots[0, these, :, columns].reshape(rows, column_half), up[columns, :])
            back_active = part if back_active is None else back_active + part
        dot = jnp.zeros((rows, 1), F32)
        back_parts = []
        for part in range(2):
            columns = slice(part * half, (part + 1) * half)
            back = (back_active[:, columns] * slopes[part, these].reshape(rows, half)).astype(BF16)
            backs[2 * lax.rem(core + part, 2), these] = back.reshape(count, unit, half)
            dot = dot + jnp.sum(
                back.astype(F32) * hiddens[part, these].reshape(rows, half), axis=-1, keepdims=True
            )
            back_parts.append(back)
        inverse = inverses[these].reshape(rows, 1)
        pull = inverse * inverse * dot * (1.0 / width)
        for piece in range(2):
            columns = slice(piece * column_half, (piece + 1) * column_half)
            back_normed = matmul(back_parts[0], down_turned[0:half, columns]) + matmul(
                back_parts[1], down_turned[half : 2 * half, columns]
            )
            grad = (
                cots[0, these, :, columns].astype(F32).reshape(rows, column_half)
                + inverse * (gain_ref[:, columns] * back_normed)
                - wide[these, :, columns].astype(F32).reshape(rows, column_half) * pull
            )
            grads[these, :, columns] = grad.astype(BF16).reshape(count, unit, column_half)

            @pl.when(not_first)
            def _():
                for number in range(count):
                    cot_copy(first + number, piece).start()

        for number in range(count):
            pass_cot(first + number).start()
            pass_back(first + number).start()

    @pl.when(is_last)
    def _():
        def from_head(slot, unused):
            head_slot(slot)
            backward(slot * per_slot, per_slot, False)
            return unused

        lax.fori_loop(0, micro, from_head, 0)

    @pl.when(not_last)
    def _():
        def from_next(number, unused):
            backward(number, 1, True)
            return unused

        lax.fori_loop(0, units, from_next, 0)

    grads_copy = pltpu.make_async_copy(grads, grads_out, load_sem.at[3])
    grads_copy.start()

    row_step = min(256, side_rows)

    def multiply(matrix, of_side):
        left, right = (normed, backs) if matrix == 0 else (cots, active)

        def block(number, unused):
            first = of_side * side_rows + number * row_step
            rows = pl.ds(pl.multiple_of(first, row_step), row_step)
            products[matrix, rows] = matmul(
                left[:, :, :, rows].reshape(2 * rows_all, row_step),
                right[0:2].reshape(2 * rows_all, half),
                TN,
            ).astype(BF16)
            return unused

        lax.fori_loop(0, side_rows // row_step, block, 0)

    theirs_rows = pl.ds(pl.multiple_of((1 - side) * side_rows, side_rows), side_rows)

    def early_copy(matrix):
        return remote(
            products.at[matrix, theirs_rows, main:half],
            early.at[matrix],
            early_send.at[matrix],
            early_recv.at[matrix],
            opposite,
        )

    longest = levels // 2
    phase_columns = (slice(0, main), slice(0, main), slice(main, half))

    def buffer_of(phase):
        return ring_early if phase == 2 else ring_main.at[phase]

    def hops(matrix, way):
        return longest if matrix == way else longest - 1

    def rows_of(phase, position):
        side_of = 1 - side if phase == 0 else side
        return pl.ds(pl.multiple_of((side_of * levels + position) * chunk, chunk), chunk)

    def ring_rows(phase, matrix, way, hop):
        left = hops(matrix, way) - hop
        return rows_of(phase, lax.rem(level + levels + (left if way == 0 else -left), levels))

    def ring_copy(phase, matrix, way, hop):
        return remote(
            products.at[matrix, ring_rows(phase, matrix, way, hop), phase_columns[phase]],
            buffer_of(phase).at[matrix, way, hop],
            ring_send.at[phase, matrix, way, hop],
            ring_recv.at[phase, matrix, way, hop],
            ahead if way == 0 else behind,
        )

    def ways_of(matrix):
        return (0, 1) if matrix == 0 else (1, 0)

    def ring_start(phase, matrix):
        for way in ways_of(matrix):
            ring_copy(phase, matrix, way, 0).start()

    def ring_turn(phase, matrix, hop):
        columns = phase_columns[phase]
        for way in ways_of(matrix):
            if 0 < hop < hops(matrix, way):
                ring_copy(phase, matrix, way, hop - 1).wait_recv()
                rows = ring_rows(phase, matrix, way, hop)
                total = products[matrix, rows, columns].astype(F32) + (
                    buffer_of(phase)[matrix, way, hop - 1].astype(F32)
                )
                products[matrix, rows, columns] = total.astype(BF16)
                ring_copy(phase, matrix, way, hop).start()

    def ring_total(phase, matrix):
        total = products[matrix, rows_of(phase, level), phase_columns[phase]].astype(F32)
        for way in reversed(ways_of(matrix)):
            last = hops(matrix, way) - 1
            ring_copy(phase, matrix, way, last).wait_recv()
            total = total + buffer_of(phase)[matrix, way, last].astype(F32)
        return total

    def add_early(matrix):
        early_copy(matrix).wait_recv()

        def add(number, unused):
            rows = pl.ds(pl.multiple_of(side * side_rows + number * chunk, chunk), chunk)
            from_rows = pl.ds(pl.multiple_of(number * chunk, chunk), chunk)
            total = products[matrix, rows, main:half].astype(F32) + (
                early[matrix, from_rows].astype(F32)
            )
            products[matrix, rows, main:half] = total.astype(BF16)
            return unused

        lax.fori_loop(0, levels, add, 0)

    def cot_passed(number, unused):
        pass_cot(number).wait_recv()
        return unused

    def back_passed(number, unused):
        pass_back(number).wait_recv()
        return unused

    normed_copy.wait_recv()
    active_copy.wait_recv()
    lax.fori_loop(0, units, cot_passed, 0)
    multiply(1, 1 - side)
    early_copy(1).start()
    ring_start(0, 1)
    lax.fori_loop(0, units, back_passed, 0)
    multiply(0, 1 - side)
    early_copy(0).start()
    ring_start(0, 0)
    multiply(1, side)
    ring_start(1, 1)
    multiply(0, side)
    ring_start(1, 0)

    def term_copy(offset):
        peer = lax.rem(me + offset, replicas)
        return remote(
            head_parts.at[peer], head_terms.at[me], term_send.at[offset], term_recv.at[me], (section, peer)
        )

    def term_wait(offset):
        peer = lax.rem(me + offset, replicas)
        remote(
            head_parts.at[peer], head_terms.at[peer], term_send.at[offset], term_recv.at[peer], (section, peer)
        ).wait_recv()

    def share_copy(number):
        block = sections * me + number
        target = (lax.div(block, replicas), lax.rem(block, replicas))
        return block, remote(head_sums.at[number], head_mine, share_send.at[number], share_recv, target)

    @pl.when(is_last)
    def _():
        part = matmul(
            head_ins[...].reshape(rows_all, width),
            head_slopes[...].reshape(rows_all, head_slopes.shape[2]),
            TN,
        )
        head_parts[...] = part.reshape(head_parts.shape)

        def send(offset, unused):
            term_copy(offset).start()
            return unused

        lax.fori_loop(1, replicas, send, 0)

    def across_copy(matrix):
        return remote(
            products.at[matrix, rows_of(0, level), 0:main],
            across.at[matrix],
            across_send.at[matrix],
            across_recv.at[matrix],
            opposite,
        )

    for hop in range(1, longest):
        for phase in (0, 1):
            for matrix in (1, 0):
                ring_turn(phase, matrix, hop)
        if hop == 1:
            add_early(1)
            ring_start(2, 1)
        elif hop == 2:
            add_early(0)
            ring_start(2, 0)
            ring_turn(2, 1, 1)
        elif hop == 3:
            ring_turn(2, 0, 1)
            ring_turn(2, 1, 2)
    if longest < 3:
        add_early(0)
        ring_start(2, 0)
        ring_turn(2, 1, 1)
        ring_turn(2, 0, 1)
    for matrix in (1, 0):
        products[matrix, rows_of(0, level), 0:main] = ring_total(0, matrix).astype(BF16)
        across_copy(matrix).start()
    if longest >= 3:
        ring_turn(2, 0, 2)
        ring_turn(2, 1, 3)
        ring_turn(2, 0, 3)

    def mate_copy(matrix):
        return remote(
            halves.at[matrix, 1 - core], mates.at[matrix], mate_send.at[matrix], mate_recv.at[matrix], mate
        )

    mine = pl.ds(pl.multiple_of(core * half, half), half)
    theirs = pl.ds(pl.multiple_of((1 - core) * half, half), half)
    for matrix in (1, 0):
        total = ring_total(1, matrix)
        across_copy(matrix).wait_recv()
        total = (total + across[matrix].astype(F32)) / LOSS_SCALE
        halves[matrix, :, :, 0:main] = total.reshape(2, share, main)
    for matrix, result in ((1, up_out), (0, down_out)):
        total = ring_total(2, matrix) / LOSS_SCALE
        halves[matrix, :, :, main:half] = total.reshape(2, share, half - main)
        mate_copy(matrix).start()
        result[:, mine] = halves[matrix, core]

    @pl.when(is_last)
    def _():
        def add_term(offset, total):
            term_wait(offset)
            return total + head_terms[lax.rem(me + offset, replicas)]

        total = lax.fori_loop(1, replicas, add_term, head_parts[me]) / LOSS_SCALE
        for number in range(sections):
            head_sums[number] = total[number * final : (number + 1) * final]
        for number in range(sections):
            block, copy = share_copy(number)
            to_me = block == (sections - 1) * replicas + me

            @pl.when(to_me)
            def _():
                head_mine[...] = head_sums[number]

            @pl.when(jnp.logical_not(to_me))
            def _():
                copy.start()

    for matrix, result in ((0, down_out), (1, up_out)):
        mate_copy(matrix).wait_recv()
        result[:, theirs] = mates[matrix]

    @pl.when(jnp.logical_not(source_is_me))
    def _():
        share_copy(0)[1].wait_recv()

    head_out[...] = head_mine[...]

    grads_copy.wait()
    normed_copy.wait_send()
    active_copy.wait_send()

    def slot_left(slot, unused):
        pass_cot(slot).wait_send()
        pass_back(slot).wait_send()
        return unused

    lax.fori_loop(0, units, slot_left, 0)

    @pl.when(not_first)
    def _():
        def cot_left(slot, unused):
            cot_copy(slot, 0).wait_send()
            cot_copy(slot, 1).wait_send()
            return unused

        lax.fori_loop(0, units, cot_left, 0)

    for phase in range(3):
        for matrix in range(2):
            for way in range(2):
                for hop in range(hops(matrix, way)):
                    ring_copy(phase, matrix, way, hop).wait_send()
    for matrix in range(2):
        early_copy(matrix).wait_send()
        across_copy(matrix).wait_send()
        mate_copy(matrix).wait_send()

    @pl.when(is_last)
    def _():
        def head_left(offset, unused):
            term_copy(offset).wait_send()
            return unused

        lax.fori_loop(1, replicas, head_left, 0)

        def gather_left(offset, unused):
            gather_copy(offset).wait_send()
            return unused

        lax.fori_loop(1, positions, gather_left, 0)
        gather_mate(core).wait_send()
        for number in range(sections):
            block, copy = share_copy(number)

            @pl.when(block != (sections - 1) * replicas + me)
            def _():
                copy.wait_send()


def hand_out(*refs):
    sources, results, held, sem = refs[:4], refs[4:8], refs[8:12], refs[12]
    incoming = [
        pltpu.make_async_copy(source, middle, sem.at[0, number])
        for number, (source, middle) in enumerate(zip(sources, held))
    ]
    outgoing = [
        pltpu.make_async_copy(middle, result, sem.at[1, number])
        for number, (middle, result) in enumerate(zip(held, results))
    ]
    for copy in incoming:
        copy.start()
    for arrival, copy in zip(incoming, outgoing):
        arrival.wait()
        copy.start()
    for copy in outgoing:
        copy.wait()


def local(
    sections,
    replicas,
    saved_inputs,
    norm_gain,
    down_weight,
    up_weight,
    head_weight,
    head_gain,
    targets,
    levels,
    level_index,
    plan,
):
    micro, tokens, width = saved_inputs.shape[1:]
    units = down_weight.shape[2]
    half = units // 2
    cols = head_weight.shape[1]
    rings = replicas // 4
    chunk = width // (2 * rings)
    share = width // replicas
    final = share // sections
    unit = tokens // 2
    units_all = 2 * micro
    main = half - half // 4
    longest = rings // 2
    whole = pl.BlockSpec(memory_space=pltpu.VMEM)
    anywhere = pl.BlockSpec(memory_space=pl.ANY)
    dma = pltpu.SemaphoreType.DMA
    grads, down_grad, up_grad, head_grad = pl.pallas_call(
        functools.partial(body, sections, replicas),
        out_shape=(
            jax.ShapeDtypeStruct((units_all, unit, width), BF16),
            jax.ShapeDtypeStruct((share, units), F32),
            jax.ShapeDtypeStruct((share, units), F32),
            jax.ShapeDtypeStruct((final, cols), F32),
        ),
        in_specs=[
            pl.BlockSpec(memory_space=pltpu.SMEM),
            whole,
            anywhere,
            whole,
            anywhere,
            anywhere,
            whole,
            whole,
            whole,
            whole,
        ],
        out_specs=(anywhere, whole, whole, whole),
        scratch_shapes=[
            pltpu.VMEM((micro, tokens, width), BF16),
            pltpu.VMEM((width, units), BF16),
            pltpu.VMEM((width, units), BF16),
            pltpu.VMEM((units, width), BF16),
            pltpu.VMEM((units_all, unit, width), BF16),
            pltpu.VMEM((units_all, unit, 1), F32),
            pltpu.VMEM((2, units_all, unit, width), BF16),
            pltpu.VMEM((3, units_all, unit, half), BF16),
            pltpu.VMEM((2, units_all, unit, half), F32),
            pltpu.VMEM((2, units_all, unit, half), F32),
            pltpu.VMEM((2, units_all, unit, width), BF16),
            pltpu.VMEM((3, units_all, unit, half), BF16),
            pltpu.VMEM((units_all, unit, width), BF16),
            pltpu.VMEM((2, width, half), BF16),
            pltpu.VMEM((2, width // 2, half - main), BF16),
            pltpu.VMEM((2, 2, 2, longest, chunk, main), BF16),
            pltpu.VMEM((2, 2, longest, chunk, half - main), BF16),
            pltpu.VMEM((2, chunk, main), BF16),
            pltpu.VMEM((2, 2, share, half), F32),
            pltpu.VMEM((2, share, half), F32),
            pltpu.VMEM((replicas // 2, 2, share, cols), BF16),
            pltpu.VMEM((units_all, unit, width), BF16),
            pltpu.VMEM((units_all, unit, width), BF16),
            pltpu.VMEM((units_all, unit, cols), BF16),
            pltpu.VMEM((replicas, share, cols), F32),
            pltpu.VMEM((replicas, share, cols), F32),
            pltpu.VMEM((sections, final, cols), F32),
            pltpu.VMEM((final, cols), F32),
            dma((4,)),
            dma((units_all, 2)),
            dma((units_all, 2)),
            dma((2,)),
            dma((2,)),
            dma((2, units_all)),
            dma((2, units_all)),
            dma((2,)),
            dma((2,)),
            dma((3, 2, 2, longest)),
            dma((3, 2, 2, longest)),
            dma((2,)),
            dma((2,)),
            dma((2,)),
            dma((2,)),
            dma((replicas // 2,)),
            dma((replicas // 2 + 1,)),
            dma((replicas,)),
            dma((replicas,)),
            dma((sections,)),
            dma(()),
        ],
        compiler_params=pltpu.CompilerParams(
            collective_id=0, has_side_effects=True, vmem_limit_bytes=56 * 1024 * 1024
        ),
    )(
        plan,
        level_index.reshape(1, -1),
        saved_inputs[0],
        norm_gain,
        down_weight[0],
        up_weight[0],
        head_weight,
        head_gain.reshape(1, -1),
        targets,
        levels.T,
    )
    grads, down_grad, up_grad, head_grad = pl.pallas_call(
        hand_out,
        out_shape=tuple(
            jax.ShapeDtypeStruct(value.shape, value.dtype)
            for value in (grads, down_grad, up_grad, head_grad)
        ),
        in_specs=[anywhere] * 4,
        out_specs=(anywhere,) * 4,
        scratch_shapes=[
            pltpu.VMEM(value.shape, value.dtype)
            for value in (grads, down_grad, up_grad, head_grad)
        ]
        + [dma((2, 4))],
    )(grads, down_grad, up_grad, head_grad)
    return grads.reshape(1, micro, tokens, width), down_grad[None], up_grad[None], head_grad


def solution(mesh):
    return jax.shard_map(
        functools.partial(local, mesh.shape["section"], mesh.shape["dp"]),
        mesh=mesh,
        in_specs=(
            P("section", None, "dp", None),
            P("section", None),
            P("section", None, None),
            P("section", None, None),
            P("dp", None),
            P(),
            P(None, "dp", None),
            P(),
            P(),
            P(),
        ),
        out_specs=(
            P("section", None, "dp", None),
            P("section", "dp", None),
            P("section", "dp", None),
            P(("section", "dp"), None),
        ),
        check_vma=False,
    )
```

```python
import functools

import jax
import jax.numpy as jnp
from jax import lax
from jax.experimental import pallas as pl
from jax.experimental.pallas import tpu as pltpu
from jax.sharding import PartitionSpec as P

EPS = 1e-06
DELTA = 0.25
BETA = 0.25
LOSS_SCALE = 64.0
SQRT_HALF = 0.7071067811865476
INV_SQRT_TAU = 0.3989422804014327
MESH = pl.DeviceIdType.MESH
F32 = jnp.float32
BF16 = jnp.bfloat16
NN = (((1,), (0,)), ((), ()))
NT = (((1,), (1,)), ((), ()))
TN = (((0,), (0,)), ((), ()))


def matmul(left, right, dims=NN):
    return lax.dot_general(left, right, dims, preferred_element_type=F32)


def inverse_rms(values):
    return lax.rsqrt(jnp.mean(values * values, axis=-1, keepdims=True) + EPS)


def norm_backward(values, inverse, scaling, upstream):
    weighted = upstream * scaling
    mean = jnp.mean(weighted * values, axis=-1, keepdims=True)
    return inverse * weighted - values * (inverse * inverse * inverse) * mean


def soft(values):
    return values * lax.rsqrt(values * values + DELTA * DELTA)


def chain(values, threshold):
    shifted = (values - threshold) / BETA
    softplus = jnp.maximum(shifted, 0.0) + jnp.log1p(jnp.exp(-jnp.abs(shifted)))
    return threshold + BETA * softplus


def chain_rate(values, threshold):
    shifted = (values - threshold) / BETA
    small = jnp.exp(-jnp.abs(shifted))
    return jnp.where(shifted >= 0.0, 1.0, small) / (1.0 + small)


def crps_slope(predicted, observed, threshold):
    variables = observed.shape[1]
    first, second = predicted[:, :variables], predicted[:, variables:]
    chain_first, chain_second = chain(first, threshold), chain(second, threshold)
    chain_obs = chain(observed, threshold)
    pair = soft(chain_first - chain_second)
    slope_first = soft(chain_first - chain_obs) / 2 - pair / 4
    slope_second = soft(chain_second - chain_obs) / 2 + pair / 4
    return jnp.concatenate(
        [
            LOSS_SCALE * chain_rate(first, threshold) * slope_first,
            LOSS_SCALE * chain_rate(second, threshold) * slope_second,
        ],
        axis=1,
    )


def body(
    sections,
    replicas,
    plan_ref,
    index_ref,
    saved_ref,
    gain_ref,
    down_ref,
    up_ref,
    head_ref,
    head_gain_ref,
    targets_ref,
    levels_ref,
    grads_out,
    down_out,
    up_out,
    head_out,
    saved,
    down,
    up,
    down_turned,
    wide,
    inverses,
    normed,
    active,
    slopes,
    hiddens,
    cots,
    sided,
    backs,
    grads,
    products,
    ring,
    across,
    halves,
    mates,
    full_head,
    outputs,
    head_ins,
    head_slopes,
    head_parts,
    head_terms,
    head_sums,
    head_mine,
    load_sem,
    cot_send,
    cot_recv,
    pair_send,
    pair_recv,
    slot_send,
    slot_recv,
    far_send,
    far_recv,
    relay_send,
    relay_recv,
    ring_send,
    ring_recv,
    across_send,
    across_recv,
    mate_send,
    mate_recv,
    gather_send,
    gather_recv,
    term_send,
    term_recv,
    share_send,
    share_recv,
):
    units, unit, width = wide.shape
    micro = saved.shape[0]
    per_slot = units // micro
    rows_all = units * unit
    half = active.shape[-1]
    levels = replicas // 4
    positions = replicas // 2
    chunk = width // (2 * levels)
    column_half = width // 2
    quarter = half // 2
    share = width // replicas
    final = head_mine.shape[0]

    section = lax.axis_index("section")
    me = lax.axis_index("dp")
    core = lax.rem(me, 2)
    level = lax.rem(lax.div(me, 2), levels)
    side = lax.div(me, 2 * levels)
    is_last = section == sections - 1
    not_last = section < sections - 1
    not_first = section > 0
    streams = section < max(sections // 2 - 1, 1)

    def member(side_of, level_of, core_of):
        return (section, (side_of * levels + level_of) * 2 + core_of)

    ahead = member(side, lax.rem(level + 1, levels), core)
    behind = member(side, lax.rem(level + levels - 1, levels), core)
    mate = member(side, level, 1 - core)
    opposite = member(1 - side, level, core)
    diagonal = member(1 - side, level, 1 - core)
    sender = (lax.rem(section + 1, sections), me)
    receiver = (lax.rem(section + sections - 1, sections), me)
    head_source = lax.div(section * replicas + me, sections)
    source_is_me = jnp.logical_and(is_last, head_source == me)

    def remote(src, dst, send, recv, device):
        return pltpu.make_async_remote_copy(
            src_ref=src,
            dst_ref=dst,
            send_sem=send,
            recv_sem=recv,
            device_id=device,
            device_id_type=MESH,
        )

    saved_load = pltpu.make_async_copy(saved_ref, saved, load_sem.at[0])
    down_load = pltpu.make_async_copy(down_ref, down, load_sem.at[1])
    up_load = pltpu.make_async_copy(up_ref, up, load_sem.at[2])
    saved_load.start()
    down_load.start()
    up_load.start()

    barrier = pltpu.get_barrier_semaphore()

    def greet(device):
        pl.semaphore_signal(barrier, inc=1, device_id=device, device_id_type=MESH)

    @pl.when(not_last)
    def _():
        greet(sender)
        for device in (ahead, behind, mate, opposite, diagonal):
            greet(device)

    @pl.when(is_last)
    def _():
        def greet_peer(offset, unused):
            greet((section, lax.rem(me + offset, replicas)))
            return unused

        lax.fori_loop(1, replicas, greet_peer, 0)

    @pl.when(jnp.logical_not(source_is_me))
    def _():
        greet((sections - 1, head_source))

    saved_load.wait()

    def norm_slot(slot, unused):
        values = saved[plan_ref[slot]]
        these = pl.ds(slot * per_slot, per_slot)
        wide[these] = values.reshape(per_slot, unit, width)
        values = values.astype(F32)
        inverse = inverse_rms(values)
        inverses[these] = inverse.reshape(per_slot, unit, 1)
        normed[3, these] = (
            (values * inverse * gain_ref[...]).astype(BF16).reshape(per_slot, unit, width)
        )
        return unused

    lax.fori_loop(0, micro, norm_slot, 0)

    heard = jnp.where(
        is_last,
        replicas + sections - jnp.where(me == replicas - 1, 1, 0),
        5 + jnp.where(not_first, 1, 0),
    )
    pl.semaphore_wait(barrier, heard)

    position = side * levels + level

    def gather_copy(offset):
        peer = lax.rem(position + offset, positions)
        return remote(
            head_ref,
            full_head.at[position, core],
            gather_send.at[offset],
            gather_recv.at[position],
            (section, peer * 2 + core),
        )

    def gather_wait(offset):
        peer = lax.rem(position + offset, positions)
        remote(
            head_ref,
            full_head.at[peer, core],
            gather_send.at[offset],
            gather_recv.at[peer],
            (section, peer * 2 + core),
        ).wait_recv()

    def gather_mate(which):
        return remote(
            full_head.at[:, which],
            full_head.at[:, which],
            gather_send.at[0],
            gather_recv.at[positions],
            mate,
        )

    @pl.when(is_last)
    def _():
        def send(offset, unused):
            gather_copy(offset).start()
            return unused

        lax.fori_loop(1, positions, send, 0)
        full_head[position, core] = head_ref[...]

    normed_copy = remote(normed.at[3], normed.at[0], pair_send.at[0], pair_recv.at[0], mate)
    normed_copy.start()
    normed_far = remote(normed.at[3], normed.at[1], pair_send.at[1], pair_recv.at[1], opposite)
    normed_relay = remote(normed.at[1], normed.at[2], pair_send.at[2], pair_recv.at[2], mate)
    active_copy = remote(active.at[4], active.at[0], pair_send.at[3], pair_recv.at[3], mate)
    active_far = remote(active.at[3], active.at[1], pair_send.at[4], pair_recv.at[4], opposite)
    active_cross = remote(active.at[4], active.at[2], pair_send.at[5], pair_recv.at[5], diagonal)

    down_load.wait()
    step = min(256, half)
    all_normed = normed[3].reshape(rows_all, width)
    for part in range(2):
        where = 3 + lax.rem(core + part, 2)

        def forward(number, unused, part=part, where=where):
            columns = pl.ds(pl.multiple_of(part * half + number * step, step), step)
            inner = pl.ds(pl.multiple_of(number * step, step), step)
            hidden = matmul(all_normed, down[:, columns])
            bell = 0.5 * (1.0 + lax.erf(hidden * SQRT_HALF))
            active[where, :, :, inner] = (
                (hidden * bell).astype(BF16).reshape(units, unit, step)
            )
            slope = bell + hidden * jnp.exp(-0.5 * hidden * hidden) * INV_SQRT_TAU
            slopes[part, :, :, inner] = slope.reshape(units, unit, step)
            hiddens[part, :, :, inner] = hidden.reshape(units, unit, step)
            return unused

        lax.fori_loop(0, half // step, forward, 0)

    active_copy.start()
    up_load.wait()

    @pl.when(is_last)
    def _():
        wide_step = min(256, width)

        def output_columns(number, unused):
            columns = pl.ds(pl.multiple_of(number * wide_step, wide_step), wide_step)
            total = wide[:, :, columns].astype(F32).reshape(rows_all, wide_step)
            for part in range(2):
                where = 3 + lax.rem(core + part, 2)
                total = total + matmul(
                    active[where].reshape(rows_all, half),
                    up[columns, part * half : (part + 1) * half],
                    NT,
                )
            outputs[:, :, columns] = total.astype(BF16).reshape(units, unit, wide_step)
            return unused

        lax.fori_loop(0, width // wide_step, output_columns, 0)

    turn_step = min(256, width)

    def turn_columns(number, unused):
        block = pl.ds(pl.multiple_of(number * turn_step, turn_step), turn_step)
        down_turned[block, :] = down[:, block].T
        return unused

    lax.fori_loop(0, 2 * half // turn_step, turn_columns, 0)

    @pl.when(is_last)
    def _():
        def arrive(offset, unused):
            gather_wait(offset)
            return unused

        lax.fori_loop(1, positions, arrive, 0)
        gather_mate(core).start()
        gather_mate(1 - core).wait_recv()

    normed_far.start()
    active_far.start()
    active_cross.start()

    def head_slot(slot):
        these = pl.ds(slot * per_slot, per_slot)
        rows = per_slot * unit
        choice = lax.broadcasted_iota(jnp.int32, levels_ref.shape, 0) == index_ref[...]
        threshold = jnp.sum(jnp.where(choice, levels_ref[...], 0.0), axis=0, keepdims=True)
        head = full_head[...].reshape(width, full_head.shape[3])
        values = outputs[these].astype(F32).reshape(rows, width)
        inverse = inverse_rms(values)
        head_in = (values * inverse * head_gain_ref[...]).astype(BF16)
        head_ins[these] = head_in.reshape(per_slot, unit, width)
        predicted = matmul(head_in, head)
        slope = crps_slope(predicted, targets_ref[plan_ref[slot]], threshold).astype(BF16)
        head_slopes[these] = slope.reshape(per_slot, unit, slope.shape[1])
        upstream = matmul(slope, head, NT)
        cotangent = norm_backward(values, inverse, head_gain_ref[...], upstream)
        cots[these] = cotangent.astype(BF16).reshape(per_slot, unit, width)

    def cot_copy(slot, piece):
        columns = slice(piece * column_half, (piece + 1) * column_half)
        return remote(
            grads.at[slot, :, columns],
            cots.at[slot, :, columns],
            cot_send.at[slot, piece],
            cot_recv.at[slot, piece],
            receiver,
        )

    def slot_copies(slot):
        these = pl.ds(slot * per_slot, per_slot)
        return (
            remote(
                sided.at[3, these], sided.at[0, these], slot_send.at[0, slot], slot_recv.at[0, slot], mate
            ),
            remote(
                backs.at[4, these], backs.at[0, these], slot_send.at[1, slot], slot_recv.at[1, slot], mate
            ),
        )

    def far_copies(number):
        theirs = pl.ds(pl.multiple_of((1 - side) * column_half, column_half), column_half)
        return (
            remote(
                backs.at[5, number], backs.at[1, number], far_send.at[0, number], far_recv.at[0, number], opposite
            ),
            remote(
                backs.at[6, number], backs.at[2, number], far_send.at[1, number], far_recv.at[1, number], diagonal
            ),
            remote(
                cots.at[number, :, theirs],
                sided.at[1, number],
                far_send.at[2, number],
                far_recv.at[2, number],
                opposite,
            ),
        )

    def relay_copy(slot):
        these = pl.ds(slot * per_slot, per_slot)
        return remote(sided.at[1, these], sided.at[2, these], relay_send.at[slot], relay_recv.at[slot], mate)

    def send_slot(slot):
        for copy in slot_copies(slot):
            copy.start()

    def send_far(number):
        for copy in far_copies(number):
            copy.start()

    def backward(first, count, arriving):
        these = pl.ds(first, count)
        rows = count * unit
        back_active = None
        for piece in range(2):
            if arriving:
                cot_copy(first, piece).wait_recv()
            columns = slice(piece * column_half, (piece + 1) * column_half)
            part = matmul(cots[these, :, columns].reshape(rows, column_half), up[columns, :])
            back_active = part if back_active is None else back_active + part
        dot = jnp.zeros((rows, 1), F32)
        back_parts = []
        for part in range(2):
            columns = slice(part * half, (part + 1) * half)
            back = (back_active[:, columns] * slopes[part, these].reshape(rows, half)).astype(BF16)
            for of_side in range(2):
                role = lax.rem(core + part, 2) + 2 * lax.rem(side + of_side, 2)
                backs[3 + role, these] = back[:, of_side * quarter : (of_side + 1) * quarter].reshape(
                    count, unit, quarter
                )
            dot = dot + jnp.sum(
                back.astype(F32) * hiddens[part, these].reshape(rows, half), axis=-1, keepdims=True
            )
            back_parts.append(back)
        inverse = inverses[these].reshape(rows, 1)
        pull = inverse * inverse * dot * (1.0 / width)
        for piece in range(2):
            columns = slice(piece * column_half, (piece + 1) * column_half)
            back_normed = matmul(back_parts[0], down_turned[0:half, columns]) + matmul(
                back_parts[1], down_turned[half : 2 * half, columns]
            )
            grad = (
                cots[these, :, columns].astype(F32).reshape(rows, column_half)
                + inverse * (gain_ref[:, columns] * back_normed)
                - wide[these, :, columns].astype(F32).reshape(rows, column_half) * pull
            )
            grads[these, :, columns] = grad.astype(BF16).reshape(count, unit, column_half)

            @pl.when(not_first)
            def _():
                for number in range(count):
                    cot_copy(first + number, piece).start()

        ours = pl.ds(pl.multiple_of(side * column_half, column_half), column_half)
        sided[3, these] = cots[these, :, ours]

        @pl.when(streams)
        def _():
            for number in range(count):
                send_far(first + number)

    @pl.when(is_last)
    def _():
        def from_head(slot, unused):
            head_slot(slot)
            backward(slot * per_slot, per_slot, False)
            send_slot(slot)
            return unused

        lax.fori_loop(0, micro, from_head, 0)

    @pl.when(not_last)
    def _():
        def from_next(number, unused):
            backward(number, 1, True)

            @pl.when(lax.rem(number, per_slot) == per_slot - 1)
            def _():
                send_slot(lax.div(number, per_slot))

            return unused

        lax.fori_loop(0, units, from_next, 0)

    grads_copy = pltpu.make_async_copy(grads, grads_out, load_sem.at[3])
    grads_copy.start()

    @pl.when(jnp.logical_not(streams))
    def _():
        def send(number, unused):
            send_far(number)
            return unused

        lax.fori_loop(0, units, send, 0)

    row_step = min(256, column_half)
    tokens_all = 4 * rows_all

    def multiply(item):
        def block(number, unused):
            first = number * row_step
            rows = pl.ds(pl.multiple_of(first, row_step), row_step)
            if item < 2:
                of_side = 1 - side if item == 0 else side
                columns = pl.ds(pl.multiple_of(of_side * column_half + first, row_step), row_step)
                left, right = normed[:, :, :, columns], backs[0:4]
            else:
                left = sided[:, :, :, rows]
                right = active[0:4, :, :, (item - 2) * quarter : (item - 1) * quarter]
            products[item, rows] = matmul(
                left.reshape(tokens_all, row_step), right.reshape(tokens_all, quarter), TN
            ).astype(BF16)
            return unused

        lax.fori_loop(0, column_half // row_step, block, 0)

    longest = levels // 2

    def hops(item, way):
        return longest if item % 2 == way else longest - 1

    def rows_of(position):
        return pl.ds(pl.multiple_of(position * chunk, chunk), chunk)

    def ring_rows(item, way, hop):
        left = hops(item, way) - hop
        return rows_of(lax.rem(level + levels + (left if way == 0 else -left), levels))

    def ring_copy(item, way, hop):
        return remote(
            products.at[item, ring_rows(item, way, hop)],
            ring.at[item, way, hop],
            ring_send.at[item, way, hop],
            ring_recv.at[item, way, hop],
            ahead if way == 0 else behind,
        )

    def ways_of(item):
        return (0, 1) if item % 2 == 0 else (1, 0)

    def ring_start(item):
        for way in ways_of(item):
            ring_copy(item, way, 0).start()

    def ring_turn(item, hop):
        for way in ways_of(item):
            if hop < hops(item, way):
                ring_copy(item, way, hop - 1).wait_recv()
                rows = ring_rows(item, way, hop)
                total = products[item, rows].astype(F32) + ring[item, way, hop - 1].astype(F32)
                products[item, rows] = total.astype(BF16)
                ring_copy(item, way, hop).start()

    def ring_total(item):
        total = products[item, rows_of(level)].astype(F32)
        for way in reversed(ways_of(item)):
            last = hops(item, way) - 1
            ring_copy(item, way, last).wait_recv()
            total = total + ring[item, way, last].astype(F32)
        return total

    normed_far.wait_recv()
    normed_relay.start()

    def relay_slot(slot, unused):
        for number in range(per_slot):
            far_copies(slot * per_slot + number)[2].wait_recv()
        relay_copy(slot).start()
        return unused

    lax.fori_loop(0, micro, relay_slot, 0)

    def backs_arrived(slot, unused):
        slot_copies(slot)[1].wait_recv()
        for number in range(per_slot):
            for copy in far_copies(slot * per_slot + number)[:2]:
                copy.wait_recv()
        return unused

    lax.fori_loop(0, micro, backs_arrived, 0)
    normed_copy.wait_recv()
    normed_relay.wait_recv()
    multiply(0)
    ring_start(0)
    multiply(1)
    ring_start(1)

    def cots_arrived(slot, unused):
        slot_copies(slot)[0].wait_recv()
        relay_copy(slot).wait_recv()
        return unused

    lax.fori_loop(0, micro, cots_arrived, 0)
    for copy in (active_copy, active_far, active_cross):
        copy.wait_recv()
    multiply(2)
    ring_start(2)
    multiply(3)
    ring_start(3)

    def term_copy(offset):
        peer = lax.rem(me + offset, replicas)
        return remote(
            head_parts.at[peer], head_terms.at[me], term_send.at[offset], term_recv.at[me], (section, peer)
        )

    def term_wait(offset):
        peer = lax.rem(me + offset, replicas)
        remote(
            head_parts.at[peer], head_terms.at[peer], term_send.at[offset], term_recv.at[peer], (section, peer)
        ).wait_recv()

    def share_copy(number):
        block = sections * me + number
        target = (lax.div(block, replicas), lax.rem(block, replicas))
        return block, remote(head_sums.at[number], head_mine, share_send.at[number], share_recv, target)

    @pl.when(is_last)
    def _():
        part = matmul(
            head_ins[...].reshape(rows_all, width),
            head_slopes[...].reshape(rows_all, head_slopes.shape[2]),
            TN,
        )
        head_parts[...] = part.reshape(head_parts.shape)

        def send(offset, unused):
            term_copy(offset).start()
            return unused

        lax.fori_loop(1, replicas, send, 0)

    across_copy = remote(
        products.at[0, rows_of(level)], across, across_send.at[0], across_recv.at[0], opposite
    )
    for hop in range(1, longest):
        for item in range(4):
            ring_turn(item, hop)
    products[0, rows_of(level)] = ring_total(0).astype(BF16)
    across_copy.start()

    def mate_copy(matrix):
        return remote(
            halves.at[matrix, 1 - core], mates.at[matrix], mate_send.at[matrix], mate_recv.at[matrix], mate
        )

    mine = pl.ds(pl.multiple_of(core * half, half), half)
    theirs = pl.ds(pl.multiple_of((1 - core) * half, half), half)
    halves[0, :, :, pl.ds(pl.multiple_of(side * quarter, quarter), quarter)] = (
        ring_total(1) / LOSS_SCALE
    ).reshape(2, share, quarter)
    for item in (2, 3):
        halves[1, :, :, (item - 2) * quarter : (item - 1) * quarter] = (
            ring_total(item) / LOSS_SCALE
        ).reshape(2, share, quarter)
    mate_copy(1).start()
    up_out[:, mine] = halves[1, core]
    across_copy.wait_recv()
    halves[0, :, :, pl.ds(pl.multiple_of((1 - side) * quarter, quarter), quarter)] = (
        across[...].astype(F32) / LOSS_SCALE
    ).reshape(2, share, quarter)
    mate_copy(0).start()
    down_out[:, mine] = halves[0, core]

    @pl.when(is_last)
    def _():
        def add_term(offset, total):
            term_wait(offset)
            return total + head_terms[lax.rem(me + offset, replicas)]

        total = lax.fori_loop(1, replicas, add_term, head_parts[me]) / LOSS_SCALE
        for number in range(sections):
            head_sums[number] = total[number * final : (number + 1) * final]
        for number in range(sections):
            block, copy = share_copy(number)
            to_me = block == (sections - 1) * replicas + me

            @pl.when(to_me)
            def _():
                head_mine[...] = head_sums[number]

            @pl.when(jnp.logical_not(to_me))
            def _():
                copy.start()

    for matrix, result in ((1, up_out), (0, down_out)):
        mate_copy(matrix).wait_recv()
        result[:, theirs] = mates[matrix]

    @pl.when(jnp.logical_not(source_is_me))
    def _():
        share_copy(0)[1].wait_recv()

    head_out[...] = head_mine[...]

    grads_copy.wait()
    for copy in (
        normed_copy,
        normed_far,
        normed_relay,
        active_copy,
        active_far,
        active_cross,
        across_copy,
    ):
        copy.wait_send()

    def slot_left(slot, unused):
        for copy in slot_copies(slot):
            copy.wait_send()
        relay_copy(slot).wait_send()
        for number in range(per_slot):
            for copy in far_copies(slot * per_slot + number):
                copy.wait_send()
        return unused

    lax.fori_loop(0, micro, slot_left, 0)

    @pl.when(not_first)
    def _():
        def cot_left(slot, unused):
            cot_copy(slot, 0).wait_send()
            cot_copy(slot, 1).wait_send()
            return unused

        lax.fori_loop(0, units, cot_left, 0)

    for item in range(4):
        for way in range(2):
            for hop in range(hops(item, way)):
                ring_copy(item, way, hop).wait_send()
    for matrix in range(2):
        mate_copy(matrix).wait_send()

    @pl.when(is_last)
    def _():
        def head_left(offset, unused):
            term_copy(offset).wait_send()
            return unused

        lax.fori_loop(1, replicas, head_left, 0)

        def gather_left(offset, unused):
            gather_copy(offset).wait_send()
            return unused

        lax.fori_loop(1, positions, gather_left, 0)
        gather_mate(core).wait_send()
        for number in range(sections):
            block, copy = share_copy(number)

            @pl.when(block != (sections - 1) * replicas + me)
            def _():
                copy.wait_send()


def hand_out(*refs):
    sources, results, held, sem = refs[:4], refs[4:8], refs[8:12], refs[12]
    incoming = [
        pltpu.make_async_copy(source, middle, sem.at[0, number])
        for number, (source, middle) in enumerate(zip(sources, held))
    ]
    outgoing = [
        pltpu.make_async_copy(middle, result, sem.at[1, number])
        for number, (middle, result) in enumerate(zip(held, results))
    ]
    for copy in incoming:
        copy.start()
    for arrival, copy in zip(incoming, outgoing):
        arrival.wait()
        copy.start()
    for copy in outgoing:
        copy.wait()


def local(
    sections,
    replicas,
    saved_inputs,
    norm_gain,
    down_weight,
    up_weight,
    head_weight,
    head_gain,
    targets,
    levels,
    level_index,
    plan,
):
    micro, tokens, width = saved_inputs.shape[1:]
    units = down_weight.shape[2]
    half = units // 2
    cols = head_weight.shape[1]
    rings = replicas // 4
    chunk = width // (2 * rings)
    share = width // replicas
    final = share // sections
    unit = tokens // 2
    units_all = 2 * micro
    quarter = half // 2
    longest = rings // 2
    whole = pl.BlockSpec(memory_space=pltpu.VMEM)
    anywhere = pl.BlockSpec(memory_space=pl.ANY)
    dma = pltpu.SemaphoreType.DMA
    grads, down_grad, up_grad, head_grad = pl.pallas_call(
        functools.partial(body, sections, replicas),
        out_shape=(
            jax.ShapeDtypeStruct((units_all, unit, width), BF16),
            jax.ShapeDtypeStruct((share, units), F32),
            jax.ShapeDtypeStruct((share, units), F32),
            jax.ShapeDtypeStruct((final, cols), F32),
        ),
        in_specs=[
            pl.BlockSpec(memory_space=pltpu.SMEM),
            whole,
            anywhere,
            whole,
            anywhere,
            anywhere,
            whole,
            whole,
            whole,
            whole,
        ],
        out_specs=(anywhere, whole, whole, whole),
        scratch_shapes=[
            pltpu.VMEM((micro, tokens, width), BF16),
            pltpu.VMEM((width, units), BF16),
            pltpu.VMEM((width, units), BF16),
            pltpu.VMEM((units, width), BF16),
            pltpu.VMEM((units_all, unit, width), BF16),
            pltpu.VMEM((units_all, unit, 1), F32),
            pltpu.VMEM((4, units_all, unit, width), BF16),
            pltpu.VMEM((5, units_all, unit, half), BF16),
            pltpu.VMEM((2, units_all, unit, half), F32),
            pltpu.VMEM((2, units_all, unit, half), F32),
            pltpu.VMEM((units_all, unit, width), BF16),
            pltpu.VMEM((4, units_all, unit, width // 2), BF16),
            pltpu.VMEM((7, units_all, unit, quarter), BF16),
            pltpu.VMEM((units_all, unit, width), BF16),
            pltpu.VMEM((4, width // 2, quarter), BF16),
            pltpu.VMEM((4, 2, longest, chunk, quarter), BF16),
            pltpu.VMEM((chunk, quarter), BF16),
            pltpu.VMEM((2, 2, share, half), F32),
            pltpu.VMEM((2, share, half), F32),
            pltpu.VMEM((replicas // 2, 2, share, cols), BF16),
            pltpu.VMEM((units_all, unit, width), BF16),
            pltpu.VMEM((units_all, unit, width), BF16),
            pltpu.VMEM((units_all, unit, cols), BF16),
            pltpu.VMEM((replicas, share, cols), F32),
            pltpu.VMEM((replicas, share, cols), F32),
            pltpu.VMEM((sections, final, cols), F32),
            pltpu.VMEM((final, cols), F32),
            dma((4,)),
            dma((units_all, 2)),
            dma((units_all, 2)),
            dma((6,)),
            dma((6,)),
            dma((2, micro)),
            dma((2, micro)),
            dma((3, units_all)),
            dma((3, units_all)),
            dma((micro,)),
            dma((micro,)),
            dma((4, 2, longest)),
            dma((4, 2, longest)),
            dma((1,)),
            dma((1,)),
            dma((2,)),
            dma((2,)),
            dma((replicas // 2,)),
            dma((replicas // 2 + 1,)),
            dma((replicas,)),
            dma((replicas,)),
            dma((sections,)),
            dma(()),
        ],
        compiler_params=pltpu.CompilerParams(
            collective_id=0, has_side_effects=True, vmem_limit_bytes=56 * 1024 * 1024
        ),
    )(
        plan,
        level_index.reshape(1, -1),
        saved_inputs[0],
        norm_gain,
        down_weight[0],
        up_weight[0],
        head_weight,
        head_gain.reshape(1, -1),
        targets,
        levels.T,
    )
    grads, down_grad, up_grad, head_grad = pl.pallas_call(
        hand_out,
        out_shape=tuple(
            jax.ShapeDtypeStruct(value.shape, value.dtype)
            for value in (grads, down_grad, up_grad, head_grad)
        ),
        in_specs=[anywhere] * 4,
        out_specs=(anywhere,) * 4,
        scratch_shapes=[
            pltpu.VMEM(value.shape, value.dtype)
            for value in (grads, down_grad, up_grad, head_grad)
        ]
        + [dma((2, 4))],
    )(grads, down_grad, up_grad, head_grad)
    return grads.reshape(1, micro, tokens, width), down_grad[None], up_grad[None], head_grad


def solution(mesh):
    return jax.shard_map(
        functools.partial(local, mesh.shape["section"], mesh.shape["dp"]),
        mesh=mesh,
        in_specs=(
            P("section", None, "dp", None),
            P("section", None),
            P("section", None, None),
            P("section", None, None),
            P("dp", None),
            P(),
            P(None, "dp", None),
            P(),
            P(),
            P(),
        ),
        out_specs=(
            P("section", None, "dp", None),
            P("section", "dp", None),
            P("section", "dp", None),
            P(("section", "dp"), None),
        ),
        check_vma=False,
    )
```

```python
import functools

import jax
import jax.numpy as jnp
from jax import lax
from jax.experimental import pallas as pl
from jax.experimental.pallas import tpu as pltpu
from jax.sharding import PartitionSpec as P

EPS = 1e-06
DELTA = 0.25
BETA = 0.25
LOSS_SCALE = 64.0
SQRT_HALF = 0.7071067811865476
INV_SQRT_TAU = 0.3989422804014327
MESH = pl.DeviceIdType.MESH
F32 = jnp.float32
BF16 = jnp.bfloat16
NN = (((1,), (0,)), ((), ()))
NT = (((1,), (1,)), ((), ()))
TN = (((0,), (0,)), ((), ()))


def matmul(left, right, dims=NN):
    return lax.dot_general(left, right, dims, preferred_element_type=F32)


def inverse_rms(values):
    return lax.rsqrt(jnp.mean(values * values, axis=-1, keepdims=True) + EPS)


def norm_backward(values, inverse, scaling, upstream):
    weighted = upstream * scaling
    mean = jnp.mean(weighted * values, axis=-1, keepdims=True)
    return inverse * weighted - values * (inverse * inverse * inverse) * mean


def soft(values):
    return values * lax.rsqrt(values * values + DELTA * DELTA)


def chain(values, threshold):
    shifted = (values - threshold) / BETA
    softplus = jnp.maximum(shifted, 0.0) + jnp.log1p(jnp.exp(-jnp.abs(shifted)))
    return threshold + BETA * softplus


def chain_rate(values, threshold):
    shifted = (values - threshold) / BETA
    small = jnp.exp(-jnp.abs(shifted))
    return jnp.where(shifted >= 0.0, 1.0, small) / (1.0 + small)


def crps_slope(predicted, observed, threshold):
    variables = observed.shape[1]
    first, second = predicted[:, :variables], predicted[:, variables:]
    chain_first, chain_second = chain(first, threshold), chain(second, threshold)
    chain_obs = chain(observed, threshold)
    pair = soft(chain_first - chain_second)
    slope_first = soft(chain_first - chain_obs) / 2 - pair / 4
    slope_second = soft(chain_second - chain_obs) / 2 + pair / 4
    return jnp.concatenate(
        [
            LOSS_SCALE * chain_rate(first, threshold) * slope_first,
            LOSS_SCALE * chain_rate(second, threshold) * slope_second,
        ],
        axis=1,
    )


def body(
    sections,
    replicas,
    plan_ref,
    index_ref,
    saved_ref,
    gain_ref,
    down_ref,
    up_ref,
    head_ref,
    head_gain_ref,
    targets_ref,
    levels_ref,
    grads_out,
    down_out,
    up_out,
    head_out,
    saved,
    down,
    up,
    down_turned,
    wide,
    inverses,
    normed,
    active,
    slopes,
    hiddens,
    cots,
    sided,
    backs,
    grads,
    products,
    ring,
    across,
    halves,
    mates,
    full_head,
    outputs,
    head_ins,
    head_slopes,
    head_parts,
    head_terms,
    head_sums,
    head_mine,
    load_sem,
    cot_send,
    cot_recv,
    pair_send,
    pair_recv,
    slot_send,
    slot_recv,
    far_send,
    far_recv,
    relay_send,
    relay_recv,
    ring_send,
    ring_recv,
    across_send,
    across_recv,
    mate_send,
    mate_recv,
    gather_send,
    gather_recv,
    term_send,
    term_recv,
    share_send,
    share_recv,
):
    units, unit, width = wide.shape
    micro = saved.shape[0]
    per_slot = units // micro
    rows_all = units * unit
    half = active.shape[-1]
    levels = replicas // 4
    positions = replicas // 2
    chunk = width // (2 * levels)
    column_half = width // 2
    quarter = half // 2
    share = width // replicas
    final = head_mine.shape[0]

    section = lax.axis_index("section")
    me = lax.axis_index("dp")
    core = lax.rem(me, 2)
    level = lax.rem(lax.div(me, 2), levels)
    side = lax.div(me, 2 * levels)
    is_last = section == sections - 1
    not_last = section < sections - 1
    not_first = section > 0
    streams = section < max(sections // 2 - 1, 1)

    def member(side_of, level_of, core_of):
        return (section, (side_of * levels + level_of) * 2 + core_of)

    ahead = member(side, lax.rem(level + 1, levels), core)
    behind = member(side, lax.rem(level + levels - 1, levels), core)
    mate = member(side, level, 1 - core)
    opposite = member(1 - side, level, core)
    diagonal = member(1 - side, level, 1 - core)
    sender = (lax.rem(section + 1, sections), me)
    receiver = (lax.rem(section + sections - 1, sections), me)
    head_source = lax.div(section * replicas + me, sections)
    source_is_me = jnp.logical_and(is_last, head_source == me)

    def remote(src, dst, send, recv, device):
        return pltpu.make_async_remote_copy(
            src_ref=src,
            dst_ref=dst,
            send_sem=send,
            recv_sem=recv,
            device_id=device,
            device_id_type=MESH,
        )

    saved_load = pltpu.make_async_copy(saved_ref, saved, load_sem.at[0])
    down_load = pltpu.make_async_copy(down_ref, down, load_sem.at[1])
    up_load = pltpu.make_async_copy(up_ref, up, load_sem.at[2])
    saved_load.start()
    down_load.start()
    up_load.start()

    barrier = pltpu.get_barrier_semaphore()

    def greet(device):
        pl.semaphore_signal(barrier, inc=1, device_id=device, device_id_type=MESH)

    @pl.when(not_last)
    def _():
        greet(sender)
        for device in (ahead, behind, mate, opposite, diagonal):
            greet(device)

    @pl.when(is_last)
    def _():
        def greet_peer(offset, unused):
            greet((section, lax.rem(me + offset, replicas)))
            return unused

        lax.fori_loop(1, replicas, greet_peer, 0)

    @pl.when(jnp.logical_not(source_is_me))
    def _():
        greet((sections - 1, head_source))

    saved_load.wait()

    def norm_slot(slot, unused):
        values = saved[plan_ref[slot]]
        these = pl.ds(slot * per_slot, per_slot)
        wide[these] = values.reshape(per_slot, unit, width)
        values = values.astype(F32)
        inverse = inverse_rms(values)
        inverses[these] = inverse.reshape(per_slot, unit, 1)
        normed[3, these] = (
            (values * inverse * gain_ref[...]).astype(BF16).reshape(per_slot, unit, width)
        )
        return unused

    lax.fori_loop(0, micro, norm_slot, 0)

    heard = jnp.where(
        is_last,
        replicas + sections - jnp.where(me == replicas - 1, 1, 0),
        5 + jnp.where(not_first, 1, 0),
    )
    pl.semaphore_wait(barrier, heard)

    position = side * levels + level

    def gather_copy(offset):
        peer = lax.rem(position + offset, positions)
        return remote(
            head_ref,
            full_head.at[position, core],
            gather_send.at[offset],
            gather_recv.at[position],
            (section, peer * 2 + core),
        )

    def gather_wait(offset):
        peer = lax.rem(position + offset, positions)
        remote(
            head_ref,
            full_head.at[peer, core],
            gather_send.at[offset],
            gather_recv.at[peer],
            (section, peer * 2 + core),
        ).wait_recv()

    def gather_mate(which):
        return remote(
            full_head.at[:, which],
            full_head.at[:, which],
            gather_send.at[0],
            gather_recv.at[positions],
            mate,
        )

    @pl.when(is_last)
    def _():
        def send(offset, unused):
            gather_copy(offset).start()
            return unused

        lax.fori_loop(1, positions, send, 0)
        full_head[position, core] = head_ref[...]

    normed_copy = remote(normed.at[3], normed.at[0], pair_send.at[0], pair_recv.at[0], mate)
    normed_copy.start()
    normed_far = remote(normed.at[3], normed.at[1], pair_send.at[1], pair_recv.at[1], opposite)
    normed_relay = remote(normed.at[1], normed.at[2], pair_send.at[2], pair_recv.at[2], mate)
    active_copy = remote(active.at[4], active.at[0], pair_send.at[3], pair_recv.at[3], mate)
    active_far = remote(active.at[3], active.at[1], pair_send.at[4], pair_recv.at[4], opposite)
    active_cross = remote(active.at[4], active.at[2], pair_send.at[5], pair_recv.at[5], diagonal)

    normed_far.start()
    down_load.wait()
    step = min(256, half)
    all_normed = normed[3].reshape(rows_all, width)
    for part in range(2):
        where = 3 + lax.rem(core + part, 2)

        def forward(number, unused, part=part, where=where):
            columns = pl.ds(pl.multiple_of(part * half + number * step, step), step)
            inner = pl.ds(pl.multiple_of(number * step, step), step)
            hidden = matmul(all_normed, down[:, columns])
            bell = 0.5 * (1.0 + lax.erf(hidden * SQRT_HALF))
            active[where, :, :, inner] = (
                (hidden * bell).astype(BF16).reshape(units, unit, step)
            )
            slope = bell + hidden * jnp.exp(-0.5 * hidden * hidden) * INV_SQRT_TAU
            slopes[part, :, :, inner] = slope.reshape(units, unit, step)
            hiddens[part, :, :, inner] = hidden.reshape(units, unit, step)
            return unused

        lax.fori_loop(0, half // step, forward, 0)

    active_copy.start()
    active_far.start()
    active_cross.start()
    up_load.wait()

    @pl.when(is_last)
    def _():
        wide_step = min(256, width)

        def output_columns(number, unused):
            columns = pl.ds(pl.multiple_of(number * wide_step, wide_step), wide_step)
            total = wide[:, :, columns].astype(F32).reshape(rows_all, wide_step)
            for part in range(2):
                where = 3 + lax.rem(core + part, 2)
                total = total + matmul(
                    active[where].reshape(rows_all, half),
                    up[columns, part * half : (part + 1) * half],
                    NT,
                )
            outputs[:, :, columns] = total.astype(BF16).reshape(units, unit, wide_step)
            return unused

        lax.fori_loop(0, width // wide_step, output_columns, 0)

    turn_step = min(256, width)

    def turn_columns(number, unused):
        block = pl.ds(pl.multiple_of(number * turn_step, turn_step), turn_step)
        down_turned[block, :] = down[:, block].T
        return unused

    lax.fori_loop(0, 2 * half // turn_step, turn_columns, 0)

    @pl.when(is_last)
    def _():
        def arrive(offset, unused):
            gather_wait(offset)
            return unused

        lax.fori_loop(1, positions, arrive, 0)
        gather_mate(core).start()
        gather_mate(1 - core).wait_recv()

    def head_slot(slot):
        these = pl.ds(slot * per_slot, per_slot)
        rows = per_slot * unit
        choice = lax.broadcasted_iota(jnp.int32, levels_ref.shape, 0) == index_ref[...]
        threshold = jnp.sum(jnp.where(choice, levels_ref[...], 0.0), axis=0, keepdims=True)
        head = full_head[...].reshape(width, full_head.shape[3])
        values = outputs[these].astype(F32).reshape(rows, width)
        inverse = inverse_rms(values)
        head_in = (values * inverse * head_gain_ref[...]).astype(BF16)
        head_ins[these] = head_in.reshape(per_slot, unit, width)
        predicted = matmul(head_in, head)
        slope = crps_slope(predicted, targets_ref[plan_ref[slot]], threshold).astype(BF16)
        head_slopes[these] = slope.reshape(per_slot, unit, slope.shape[1])
        upstream = matmul(slope, head, NT)
        cotangent = norm_backward(values, inverse, head_gain_ref[...], upstream)
        cots[these] = cotangent.astype(BF16).reshape(per_slot, unit, width)

    def cot_copy(slot, piece):
        columns = slice(piece * column_half, (piece + 1) * column_half)
        return remote(
            grads.at[slot, :, columns],
            cots.at[slot, :, columns],
            cot_send.at[slot, piece],
            cot_recv.at[slot, piece],
            receiver,
        )

    def slot_copies(slot):
        these = pl.ds(slot * per_slot, per_slot)
        return (
            remote(
                sided.at[3, these], sided.at[0, these], slot_send.at[0, slot], slot_recv.at[0, slot], mate
            ),
            remote(
                backs.at[4, these], backs.at[0, these], slot_send.at[1, slot], slot_recv.at[1, slot], mate
            ),
        )

    def far_copies(number):
        theirs = pl.ds(pl.multiple_of((1 - side) * column_half, column_half), column_half)
        return (
            remote(
                backs.at[5, number], backs.at[1, number], far_send.at[0, number], far_recv.at[0, number], opposite
            ),
            remote(
                backs.at[6, number], backs.at[2, number], far_send.at[1, number], far_recv.at[1, number], diagonal
            ),
            remote(
                cots.at[number, :, theirs],
                sided.at[1, number],
                far_send.at[2, number],
                far_recv.at[2, number],
                opposite,
            ),
        )

    def relay_copy(slot):
        these = pl.ds(slot * per_slot, per_slot)
        return remote(sided.at[1, these], sided.at[2, these], relay_send.at[slot], relay_recv.at[slot], mate)

    def send_slot(slot):
        for copy in slot_copies(slot):
            copy.start()

    def send_far(number):
        for copy in far_copies(number):
            copy.start()

    def backward(first, count, arriving):
        these = pl.ds(first, count)
        rows = count * unit
        back_active = None
        for piece in range(2):
            if arriving:
                cot_copy(first, piece).wait_recv()
            columns = slice(piece * column_half, (piece + 1) * column_half)
            part = matmul(cots[these, :, columns].reshape(rows, column_half), up[columns, :])
            back_active = part if back_active is None else back_active + part
        dot = jnp.zeros((rows, 1), F32)
        back_parts = []
        for part in range(2):
            columns = slice(part * half, (part + 1) * half)
            back = (back_active[:, columns] * slopes[part, these].reshape(rows, half)).astype(BF16)
            for of_side in range(2):
                role = lax.rem(core + part, 2) + 2 * lax.rem(side + of_side, 2)
                backs[3 + role, these] = back[:, of_side * quarter : (of_side + 1) * quarter].reshape(
                    count, unit, quarter
                )
            dot = dot + jnp.sum(
                back.astype(F32) * hiddens[part, these].reshape(rows, half), axis=-1, keepdims=True
            )
            back_parts.append(back)
        inverse = inverses[these].reshape(rows, 1)
        pull = inverse * inverse * dot * (1.0 / width)
        for piece in range(2):
            columns = slice(piece * column_half, (piece + 1) * column_half)
            back_normed = matmul(back_parts[0], down_turned[0:half, columns]) + matmul(
                back_parts[1], down_turned[half : 2 * half, columns]
            )
            grad = (
                cots[these, :, columns].astype(F32).reshape(rows, column_half)
                + inverse * (gain_ref[:, columns] * back_normed)
                - wide[these, :, columns].astype(F32).reshape(rows, column_half) * pull
            )
            grads[these, :, columns] = grad.astype(BF16).reshape(count, unit, column_half)

            @pl.when(not_first)
            def _():
                for number in range(count):
                    cot_copy(first + number, piece).start()

        ours = pl.ds(pl.multiple_of(side * column_half, column_half), column_half)
        sided[3, these] = cots[these, :, ours]

        @pl.when(streams)
        def _():
            for number in range(count):
                send_far(first + number)

    @pl.when(is_last)
    def _():
        def from_head(slot, unused):
            head_slot(slot)
            backward(slot * per_slot, per_slot, False)
            send_slot(slot)
            return unused

        lax.fori_loop(0, micro, from_head, 0)

    @pl.when(not_last)
    def _():
        def from_next(number, unused):
            backward(number, 1, True)

            @pl.when(lax.rem(number, per_slot) == per_slot - 1)
            def _():
                send_slot(lax.div(number, per_slot))

            return unused

        lax.fori_loop(0, units, from_next, 0)

    grads_copy = pltpu.make_async_copy(grads, grads_out, load_sem.at[3])
    grads_copy.start()

    def term_copy(offset):
        peer = lax.rem(me + offset, replicas)
        return remote(
            head_parts.at[peer], head_terms.at[me], term_send.at[offset], term_recv.at[me], (section, peer)
        )

    def term_wait(offset):
        peer = lax.rem(me + offset, replicas)
        remote(
            head_parts.at[peer], head_terms.at[peer], term_send.at[offset], term_recv.at[peer], (section, peer)
        ).wait_recv()

    def share_copy(number):
        block = sections * me + number
        target = (lax.div(block, replicas), lax.rem(block, replicas))
        return block, remote(head_sums.at[number], head_mine, share_send.at[number], share_recv, target)

    @pl.when(is_last)
    def _():
        part = matmul(
            head_ins[...].reshape(rows_all, width),
            head_slopes[...].reshape(rows_all, head_slopes.shape[2]),
            TN,
        )
        head_parts[...] = part.reshape(head_parts.shape)

        def send(offset, unused):
            term_copy(offset).start()
            return unused

        lax.fori_loop(1, replicas, send, 0)

    @pl.when(jnp.logical_not(streams))
    def _():
        def send(number, unused):
            send_far(number)
            return unused

        lax.fori_loop(0, units, send, 0)

    row_step = min(256, column_half)
    tokens_all = 4 * rows_all

    def multiply(item):
        def block(number, unused):
            first = number * row_step
            rows = pl.ds(pl.multiple_of(first, row_step), row_step)
            if item < 2:
                of_side = 1 - side if item == 0 else side
                columns = pl.ds(pl.multiple_of(of_side * column_half + first, row_step), row_step)
                left, right = normed[:, :, :, columns], backs[0:4]
            else:
                left = sided[:, :, :, rows]
                right = active[0:4, :, :, (item - 2) * quarter : (item - 1) * quarter]
            products[item, rows] = matmul(
                left.reshape(tokens_all, row_step), right.reshape(tokens_all, quarter), TN
            ).astype(BF16)
            return unused

        lax.fori_loop(0, column_half // row_step, block, 0)

    longest = levels // 2

    def hops(item, way):
        return longest if item % 2 == way else longest - 1

    def rows_of(position):
        return pl.ds(pl.multiple_of(position * chunk, chunk), chunk)

    def ring_rows(item, way, hop):
        left = hops(item, way) - hop
        return rows_of(lax.rem(level + levels + (left if way == 0 else -left), levels))

    def ring_copy(item, way, hop):
        return remote(
            products.at[item, ring_rows(item, way, hop)],
            ring.at[item, way, hop],
            ring_send.at[item, way, hop],
            ring_recv.at[item, way, hop],
            ahead if way == 0 else behind,
        )

    def ways_of(item):
        return (0, 1) if item % 2 == 0 else (1, 0)

    def ring_start(item):
        for way in ways_of(item):
            ring_copy(item, way, 0).start()

    def ring_turn(item, hop):
        for way in ways_of(item):
            if hop < hops(item, way):
                ring_copy(item, way, hop - 1).wait_recv()
                rows = ring_rows(item, way, hop)
                total = products[item, rows].astype(F32) + ring[item, way, hop - 1].astype(F32)
                products[item, rows] = total.astype(BF16)
                ring_copy(item, way, hop).start()

    def ring_total(item):
        total = products[item, rows_of(level)].astype(F32)
        for way in reversed(ways_of(item)):
            last = hops(item, way) - 1
            ring_copy(item, way, last).wait_recv()
            total = total + ring[item, way, last].astype(F32)
        return total

    normed_far.wait_recv()
    normed_relay.start()

    def relay_slot(slot, unused):
        for number in range(per_slot):
            far_copies(slot * per_slot + number)[2].wait_recv()
        relay_copy(slot).start()
        return unused

    lax.fori_loop(0, micro, relay_slot, 0)

    def backs_arrived(slot, unused):
        slot_copies(slot)[1].wait_recv()
        for number in range(per_slot):
            for copy in far_copies(slot * per_slot + number)[:2]:
                copy.wait_recv()
        return unused

    lax.fori_loop(0, micro, backs_arrived, 0)
    normed_copy.wait_recv()
    normed_relay.wait_recv()
    multiply(0)
    ring_start(0)
    multiply(1)
    ring_start(1)

    def cots_arrived(slot, unused):
        slot_copies(slot)[0].wait_recv()
        relay_copy(slot).wait_recv()
        return unused

    lax.fori_loop(0, micro, cots_arrived, 0)
    for copy in (active_copy, active_far, active_cross):
        copy.wait_recv()
    multiply(2)
    ring_start(2)
    multiply(3)
    ring_start(3)

    @pl.when(is_last)
    def _():
        def add_term(offset, total):
            term_wait(offset)
            return total + head_terms[lax.rem(me + offset, replicas)]

        total = lax.fori_loop(1, replicas, add_term, head_parts[me]) / LOSS_SCALE
        for number in range(sections):
            head_sums[number] = total[number * final : (number + 1) * final]
        for number in range(sections):
            block, copy = share_copy(number)
            to_me = block == (sections - 1) * replicas + me

            @pl.when(to_me)
            def _():
                head_mine[...] = head_sums[number]

            @pl.when(jnp.logical_not(to_me))
            def _():
                copy.start()

    across_copy = remote(
        products.at[0, rows_of(level)], across, across_send.at[0], across_recv.at[0], opposite
    )
    for hop in range(1, longest):
        for item in range(4):
            ring_turn(item, hop)
    products[0, rows_of(level)] = ring_total(0).astype(BF16)
    across_copy.start()

    def mate_copy(matrix):
        return remote(
            halves.at[matrix, 1 - core], mates.at[matrix], mate_send.at[matrix], mate_recv.at[matrix], mate
        )

    mine = pl.ds(pl.multiple_of(core * half, half), half)
    theirs = pl.ds(pl.multiple_of((1 - core) * half, half), half)
    halves[0, :, :, pl.ds(pl.multiple_of(side * quarter, quarter), quarter)] = (
        ring_total(1) / LOSS_SCALE
    ).reshape(2, share, quarter)
    for item in (2, 3):
        halves[1, :, :, (item - 2) * quarter : (item - 1) * quarter] = (
            ring_total(item) / LOSS_SCALE
        ).reshape(2, share, quarter)
    mate_copy(1).start()
    up_out[:, mine] = halves[1, core]
    across_copy.wait_recv()
    halves[0, :, :, pl.ds(pl.multiple_of((1 - side) * quarter, quarter), quarter)] = (
        across[...].astype(F32) / LOSS_SCALE
    ).reshape(2, share, quarter)
    mate_copy(0).start()
    down_out[:, mine] = halves[0, core]

    for matrix, result in ((1, up_out), (0, down_out)):
        mate_copy(matrix).wait_recv()
        result[:, theirs] = mates[matrix]

    @pl.when(jnp.logical_not(source_is_me))
    def _():
        share_copy(0)[1].wait_recv()

    head_out[...] = head_mine[...]

    grads_copy.wait()
    for copy in (
        normed_copy,
        normed_far,
        normed_relay,
        active_copy,
        active_far,
        active_cross,
        across_copy,
    ):
        copy.wait_send()

    def slot_left(slot, unused):
        for copy in slot_copies(slot):
            copy.wait_send()
        relay_copy(slot).wait_send()
        for number in range(per_slot):
            for copy in far_copies(slot * per_slot + number):
                copy.wait_send()
        return unused

    lax.fori_loop(0, micro, slot_left, 0)

    @pl.when(not_first)
    def _():
        def cot_left(slot, unused):
            cot_copy(slot, 0).wait_send()
            cot_copy(slot, 1).wait_send()
            return unused

        lax.fori_loop(0, units, cot_left, 0)

    for item in range(4):
        for way in range(2):
            for hop in range(hops(item, way)):
                ring_copy(item, way, hop).wait_send()
    for matrix in range(2):
        mate_copy(matrix).wait_send()

    @pl.when(is_last)
    def _():
        def head_left(offset, unused):
            term_copy(offset).wait_send()
            return unused

        lax.fori_loop(1, replicas, head_left, 0)

        def gather_left(offset, unused):
            gather_copy(offset).wait_send()
            return unused

        lax.fori_loop(1, positions, gather_left, 0)
        gather_mate(core).wait_send()
        for number in range(sections):
            block, copy = share_copy(number)

            @pl.when(block != (sections - 1) * replicas + me)
            def _():
                copy.wait_send()


def hand_out(*refs):
    sources, results, held, sem = refs[:4], refs[4:8], refs[8:12], refs[12]
    incoming = [
        pltpu.make_async_copy(source, middle, sem.at[0, number])
        for number, (source, middle) in enumerate(zip(sources, held))
    ]
    outgoing = [
        pltpu.make_async_copy(middle, result, sem.at[1, number])
        for number, (middle, result) in enumerate(zip(held, results))
    ]
    for copy in incoming:
        copy.start()
    for arrival, copy in zip(incoming, outgoing):
        arrival.wait()
        copy.start()
    for copy in outgoing:
        copy.wait()


def local(
    sections,
    replicas,
    saved_inputs,
    norm_gain,
    down_weight,
    up_weight,
    head_weight,
    head_gain,
    targets,
    levels,
    level_index,
    plan,
):
    micro, tokens, width = saved_inputs.shape[1:]
    units = down_weight.shape[2]
    half = units // 2
    cols = head_weight.shape[1]
    rings = replicas // 4
    chunk = width // (2 * rings)
    share = width // replicas
    final = share // sections
    unit = tokens // 2
    units_all = 2 * micro
    quarter = half // 2
    longest = rings // 2
    whole = pl.BlockSpec(memory_space=pltpu.VMEM)
    anywhere = pl.BlockSpec(memory_space=pl.ANY)
    dma = pltpu.SemaphoreType.DMA
    grads, down_grad, up_grad, head_grad = pl.pallas_call(
        functools.partial(body, sections, replicas),
        out_shape=(
            jax.ShapeDtypeStruct((units_all, unit, width), BF16),
            jax.ShapeDtypeStruct((share, units), F32),
            jax.ShapeDtypeStruct((share, units), F32),
            jax.ShapeDtypeStruct((final, cols), F32),
        ),
        in_specs=[
            pl.BlockSpec(memory_space=pltpu.SMEM),
            whole,
            anywhere,
            whole,
            anywhere,
            anywhere,
            whole,
            whole,
            whole,
            whole,
        ],
        out_specs=(anywhere, whole, whole, whole),
        scratch_shapes=[
            pltpu.VMEM((micro, tokens, width), BF16),
            pltpu.VMEM((width, units), BF16),
            pltpu.VMEM((width, units), BF16),
            pltpu.VMEM((units, width), BF16),
            pltpu.VMEM((units_all, unit, width), BF16),
            pltpu.VMEM((units_all, unit, 1), F32),
            pltpu.VMEM((4, units_all, unit, width), BF16),
            pltpu.VMEM((5, units_all, unit, half), BF16),
            pltpu.VMEM((2, units_all, unit, half), F32),
            pltpu.VMEM((2, units_all, unit, half), F32),
            pltpu.VMEM((units_all, unit, width), BF16),
            pltpu.VMEM((4, units_all, unit, width // 2), BF16),
            pltpu.VMEM((7, units_all, unit, quarter), BF16),
            pltpu.VMEM((units_all, unit, width), BF16),
            pltpu.VMEM((4, width // 2, quarter), BF16),
            pltpu.VMEM((4, 2, longest, chunk, quarter), BF16),
            pltpu.VMEM((chunk, quarter), BF16),
            pltpu.VMEM((2, 2, share, half), F32),
            pltpu.VMEM((2, share, half), F32),
            pltpu.VMEM((replicas // 2, 2, share, cols), BF16),
            pltpu.VMEM((units_all, unit, width), BF16),
            pltpu.VMEM((units_all, unit, width), BF16),
            pltpu.VMEM((units_all, unit, cols), BF16),
            pltpu.VMEM((replicas, share, cols), F32),
            pltpu.VMEM((replicas, share, cols), F32),
            pltpu.VMEM((sections, final, cols), F32),
            pltpu.VMEM((final, cols), F32),
            dma((4,)),
            dma((units_all, 2)),
            dma((units_all, 2)),
            dma((6,)),
            dma((6,)),
            dma((2, micro)),
            dma((2, micro)),
            dma((3, units_all)),
            dma((3, units_all)),
            dma((micro,)),
            dma((micro,)),
            dma((4, 2, longest)),
            dma((4, 2, longest)),
            dma((1,)),
            dma((1,)),
            dma((2,)),
            dma((2,)),
            dma((replicas // 2,)),
            dma((replicas // 2 + 1,)),
            dma((replicas,)),
            dma((replicas,)),
            dma((sections,)),
            dma(()),
        ],
        compiler_params=pltpu.CompilerParams(
            collective_id=0, has_side_effects=True, vmem_limit_bytes=56 * 1024 * 1024
        ),
    )(
        plan,
        level_index.reshape(1, -1),
        saved_inputs[0],
        norm_gain,
        down_weight[0],
        up_weight[0],
        head_weight,
        head_gain.reshape(1, -1),
        targets,
        levels.T,
    )
    grads, down_grad, up_grad, head_grad = pl.pallas_call(
        hand_out,
        out_shape=tuple(
            jax.ShapeDtypeStruct(value.shape, value.dtype)
            for value in (grads, down_grad, up_grad, head_grad)
        ),
        in_specs=[anywhere] * 4,
        out_specs=(anywhere,) * 4,
        scratch_shapes=[
            pltpu.VMEM(value.shape, value.dtype)
            for value in (grads, down_grad, up_grad, head_grad)
        ]
        + [dma((2, 4))],
    )(grads, down_grad, up_grad, head_grad)
    return grads.reshape(1, micro, tokens, width), down_grad[None], up_grad[None], head_grad


def solution(mesh):
    return jax.shard_map(
        functools.partial(local, mesh.shape["section"], mesh.shape["dp"]),
        mesh=mesh,
        in_specs=(
            P("section", None, "dp", None),
            P("section", None),
            P("section", None, None),
            P("section", None, None),
            P("dp", None),
            P(),
            P(None, "dp", None),
            P(),
            P(),
            P(),
        ),
        out_specs=(
            P("section", None, "dp", None),
            P("section", "dp", None),
            P("section", "dp", None),
            P(("section", "dp"), None),
        ),
        check_vma=False,
    )
```

```python
import functools

import jax
import jax.numpy as jnp
from jax import lax
from jax.experimental import pallas as pl
from jax.experimental.pallas import tpu as pltpu
from jax.sharding import PartitionSpec as P

EPS = 1e-06
DELTA = 0.25
BETA = 0.25
LOSS_SCALE = 64.0
SQRT_HALF = 0.7071067811865476
INV_SQRT_TAU = 0.3989422804014327
MESH = pl.DeviceIdType.MESH
F32 = jnp.float32
BF16 = jnp.bfloat16
NN = (((1,), (0,)), ((), ()))
NT = (((1,), (1,)), ((), ()))
TN = (((0,), (0,)), ((), ()))


def matmul(left, right, dims=NN):
    return lax.dot_general(left, right, dims, preferred_element_type=F32)


def inverse_rms(values):
    return lax.rsqrt(jnp.mean(values * values, axis=-1, keepdims=True) + EPS)


def norm_backward(values, inverse, scaling, upstream):
    weighted = upstream * scaling
    mean = jnp.mean(weighted * values, axis=-1, keepdims=True)
    return inverse * weighted - values * (inverse * inverse * inverse) * mean


def soft(values):
    return values * lax.rsqrt(values * values + DELTA * DELTA)


def chain(values, threshold):
    shifted = (values - threshold) / BETA
    softplus = jnp.maximum(shifted, 0.0) + jnp.log1p(jnp.exp(-jnp.abs(shifted)))
    return threshold + BETA * softplus


def chain_rate(values, threshold):
    shifted = (values - threshold) / BETA
    small = jnp.exp(-jnp.abs(shifted))
    return jnp.where(shifted >= 0.0, 1.0, small) / (1.0 + small)


def crps_slope(predicted, observed, threshold):
    variables = observed.shape[1]
    first, second = predicted[:, :variables], predicted[:, variables:]
    chain_first, chain_second = chain(first, threshold), chain(second, threshold)
    chain_obs = chain(observed, threshold)
    pair = soft(chain_first - chain_second)
    slope_first = soft(chain_first - chain_obs) / 2 - pair / 4
    slope_second = soft(chain_second - chain_obs) / 2 + pair / 4
    return jnp.concatenate(
        [
            LOSS_SCALE * chain_rate(first, threshold) * slope_first,
            LOSS_SCALE * chain_rate(second, threshold) * slope_second,
        ],
        axis=1,
    )


def body(
    sections,
    replicas,
    plan_ref,
    index_ref,
    saved_ref,
    gain_ref,
    down_ref,
    up_ref,
    head_ref,
    head_gain_ref,
    targets_ref,
    levels_ref,
    grads_out,
    down_out,
    up_out,
    head_out,
    saved,
    down,
    up,
    down_turned,
    wide,
    inverses,
    normed,
    active,
    slopes,
    hiddens,
    cots,
    sided,
    backs,
    grads,
    products,
    ring,
    across,
    halves,
    mates,
    full_head,
    outputs,
    head_ins,
    head_slopes,
    head_parts,
    head_other,
    head_added,
    head_terms,
    head_sums,
    head_mine,
    load_sem,
    cot_send,
    cot_recv,
    pair_send,
    pair_recv,
    slot_send,
    slot_recv,
    far_send,
    far_recv,
    relay_send,
    relay_recv,
    ring_send,
    ring_recv,
    across_send,
    across_recv,
    mate_send,
    mate_recv,
    gather_send,
    gather_recv,
    term_send,
    term_recv,
    share_send,
    share_recv,
    other_send,
    other_recv,
    ready,
):
    units, unit, width = wide.shape
    micro = saved.shape[0]
    per_slot = units // micro
    rows_all = units * unit
    half = active.shape[-1]
    levels = replicas // 4
    positions = replicas // 2
    chunk = width // (2 * levels)
    column_half = width // 2
    quarter = half // 2
    share = width // replicas
    final = head_mine.shape[0]

    section = lax.axis_index("section")
    me = lax.axis_index("dp")
    core = lax.rem(me, 2)
    level = lax.rem(lax.div(me, 2), levels)
    side = lax.div(me, 2 * levels)
    is_last = section == sections - 1
    not_last = section < sections - 1
    not_first = section > 0
    streams = section < max(sections // 2 - 1, 1)

    def member(side_of, level_of, core_of):
        return (section, (side_of * levels + level_of) * 2 + core_of)

    ahead = member(side, lax.rem(level + 1, levels), core)
    behind = member(side, lax.rem(level + levels - 1, levels), core)
    mate = member(side, level, 1 - core)
    opposite = member(1 - side, level, core)
    diagonal = member(1 - side, level, 1 - core)
    sender = (lax.rem(section + 1, sections), me)
    receiver = (lax.rem(section + sections - 1, sections), me)
    head_source = lax.div(section * replicas + me, sections)
    source_is_me = jnp.logical_and(is_last, head_source == me)

    def remote(src, dst, send, recv, device):
        return pltpu.make_async_remote_copy(
            src_ref=src,
            dst_ref=dst,
            send_sem=send,
            recv_sem=recv,
            device_id=device,
            device_id_type=MESH,
        )

    saved_load = pltpu.make_async_copy(saved_ref, saved, load_sem.at[0])
    down_load = pltpu.make_async_copy(down_ref, down, load_sem.at[1])
    up_load = pltpu.make_async_copy(up_ref, up, load_sem.at[2])
    saved_load.start()
    down_load.start()
    up_load.start()

    barrier = pltpu.get_barrier_semaphore()

    def greet(device):
        pl.semaphore_signal(barrier, inc=1, device_id=device, device_id_type=MESH)

    @pl.when(not_last)
    def _():
        greet(sender)
        for device in (ahead, behind, mate, opposite, diagonal):
            greet(device)

    position = side * levels + level

    @pl.when(is_last)
    def _():
        def greet_peer(offset, unused):
            greet((section, lax.rem(position + offset, positions) * 2 + core))
            return unused

        lax.fori_loop(1, positions, greet_peer, 0)
        greet(mate)
        greet(diagonal)
        for number in range(sections):
            block = sections * me + number

            @pl.when(block != (sections - 1) * replicas + me)
            def _():
                greet((lax.div(block, replicas), lax.rem(block, replicas)))

    saved_load.wait()

    def norm_slot(slot, unused):
        values = saved[plan_ref[slot]]
        these = pl.ds(slot * per_slot, per_slot)
        wide[these] = values.reshape(per_slot, unit, width)
        values = values.astype(F32)
        inverse = inverse_rms(values)
        inverses[these] = inverse.reshape(per_slot, unit, 1)
        normed[3, these] = (
            (values * inverse * gain_ref[...]).astype(BF16).reshape(per_slot, unit, width)
        )
        return unused

    lax.fori_loop(0, micro, norm_slot, 0)

    heard = jnp.where(
        is_last,
        positions + 3 - jnp.where(me == replicas - 1, 1, 0),
        6 + jnp.where(not_first, 1, 0),
    )
    pl.semaphore_wait(barrier, heard)

    @pl.when(jnp.logical_not(source_is_me))
    def _():
        pl.semaphore_signal(
            ready, inc=1, device_id=(sections - 1, head_source), device_id_type=MESH
        )

    def gather_copy(offset):
        peer = lax.rem(position + offset, positions)
        return remote(
            head_ref,
            full_head.at[position, core],
            gather_send.at[offset],
            gather_recv.at[position],
            (section, peer * 2 + core),
        )

    def gather_wait(offset):
        peer = lax.rem(position + offset, positions)
        remote(
            head_ref,
            full_head.at[peer, core],
            gather_send.at[offset],
            gather_recv.at[peer],
            (section, peer * 2 + core),
        ).wait_recv()

    def gather_mate(which):
        return remote(
            full_head.at[:, which],
            full_head.at[:, which],
            gather_send.at[0],
            gather_recv.at[positions],
            mate,
        )

    @pl.when(is_last)
    def _():
        def send(offset, unused):
            gather_copy(offset).start()
            return unused

        lax.fori_loop(1, positions, send, 0)
        full_head[position, core] = head_ref[...]

    normed_copy = remote(normed.at[3], normed.at[0], pair_send.at[0], pair_recv.at[0], mate)
    normed_copy.start()
    normed_far = remote(normed.at[3], normed.at[1], pair_send.at[1], pair_recv.at[1], opposite)
    normed_relay = remote(normed.at[1], normed.at[2], pair_send.at[2], pair_recv.at[2], mate)
    active_copy = remote(active.at[4], active.at[0], pair_send.at[3], pair_recv.at[3], mate)
    active_far = remote(active.at[3], active.at[1], pair_send.at[4], pair_recv.at[4], opposite)
    active_cross = remote(active.at[4], active.at[2], pair_send.at[5], pair_recv.at[5], diagonal)

    normed_far.start()
    down_load.wait()
    step = min(256, half)
    all_normed = normed[3].reshape(rows_all, width)
    for part in range(2):
        where = 3 + lax.rem(core + part, 2)

        def forward(number, unused, part=part, where=where):
            columns = pl.ds(pl.multiple_of(part * half + number * step, step), step)
            inner = pl.ds(pl.multiple_of(number * step, step), step)
            hidden = matmul(all_normed, down[:, columns])
            bell = 0.5 * (1.0 + lax.erf(hidden * SQRT_HALF))
            active[where, :, :, inner] = (
                (hidden * bell).astype(BF16).reshape(units, unit, step)
            )
            slope = bell + hidden * jnp.exp(-0.5 * hidden * hidden) * INV_SQRT_TAU
            slopes[part, :, :, inner] = slope.reshape(units, unit, step)
            hiddens[part, :, :, inner] = hidden.reshape(units, unit, step)
            return unused

        lax.fori_loop(0, half // step, forward, 0)

    active_copy.start()
    active_far.start()
    active_cross.start()
    up_load.wait()

    @pl.when(is_last)
    def _():
        wide_step = min(256, width)

        def output_columns(number, unused):
            columns = pl.ds(pl.multiple_of(number * wide_step, wide_step), wide_step)
            total = wide[:, :, columns].astype(F32).reshape(rows_all, wide_step)
            for part in range(2):
                where = 3 + lax.rem(core + part, 2)
                total = total + matmul(
                    active[where].reshape(rows_all, half),
                    up[columns, part * half : (part + 1) * half],
                    NT,
                )
            outputs[:, :, columns] = total.astype(BF16).reshape(units, unit, wide_step)
            return unused

        lax.fori_loop(0, width // wide_step, output_columns, 0)

    turn_step = min(256, width)

    def turn_columns(number, unused):
        block = pl.ds(pl.multiple_of(number * turn_step, turn_step), turn_step)
        down_turned[block, :] = down[:, block].T
        return unused

    lax.fori_loop(0, 2 * half // turn_step, turn_columns, 0)

    @pl.when(is_last)
    def _():
        def arrive(offset, unused):
            gather_wait(offset)
            return unused

        lax.fori_loop(1, positions, arrive, 0)
        gather_mate(core).start()
        gather_mate(1 - core).wait_recv()

    def head_slot(slot):
        these = pl.ds(slot * per_slot, per_slot)
        rows = per_slot * unit
        choice = lax.broadcasted_iota(jnp.int32, levels_ref.shape, 0) == index_ref[...]
        threshold = jnp.sum(jnp.where(choice, levels_ref[...], 0.0), axis=0, keepdims=True)
        head = full_head[...].reshape(width, full_head.shape[3])
        values = outputs[these].astype(F32).reshape(rows, width)
        inverse = inverse_rms(values)
        head_in = (values * inverse * head_gain_ref[...]).astype(BF16)
        head_ins[these] = head_in.reshape(per_slot, unit, width)
        predicted = matmul(head_in, head)
        slope = crps_slope(predicted, targets_ref[plan_ref[slot]], threshold).astype(BF16)
        head_slopes[these] = slope.reshape(per_slot, unit, slope.shape[1])
        upstream = matmul(slope, head, NT)
        cotangent = norm_backward(values, inverse, head_gain_ref[...], upstream)
        cots[these] = cotangent.astype(BF16).reshape(per_slot, unit, width)

    def cot_copy(slot, piece):
        columns = slice(piece * column_half, (piece + 1) * column_half)
        return remote(
            grads.at[slot, :, columns],
            cots.at[slot, :, columns],
            cot_send.at[slot, piece],
            cot_recv.at[slot, piece],
            receiver,
        )

    def slot_copies(slot):
        these = pl.ds(slot * per_slot, per_slot)
        return (
            remote(
                sided.at[3, these], sided.at[0, these], slot_send.at[0, slot], slot_recv.at[0, slot], mate
            ),
            remote(
                backs.at[4, these], backs.at[0, these], slot_send.at[1, slot], slot_recv.at[1, slot], mate
            ),
        )

    def far_copies(number):
        theirs = pl.ds(pl.multiple_of((1 - side) * column_half, column_half), column_half)
        return (
            remote(
                backs.at[5, number], backs.at[1, number], far_send.at[0, number], far_recv.at[0, number], opposite
            ),
            remote(
                backs.at[6, number], backs.at[2, number], far_send.at[1, number], far_recv.at[1, number], diagonal
            ),
            remote(
                cots.at[number, :, theirs],
                sided.at[1, number],
                far_send.at[2, number],
                far_recv.at[2, number],
                opposite,
            ),
        )

    def relay_copy(slot):
        these = pl.ds(slot * per_slot, per_slot)
        return remote(sided.at[1, these], sided.at[2, these], relay_send.at[slot], relay_recv.at[slot], mate)

    def send_slot(slot):
        for copy in slot_copies(slot):
            copy.start()

    def send_far(number):
        for copy in far_copies(number):
            copy.start()

    def backward(first, count, arriving, passing, far):
        these = pl.ds(first, count)
        rows = count * unit
        back_active = None
        for piece in range(2):
            if arriving:
                cot_copy(first, piece).wait_recv()
            columns = slice(piece * column_half, (piece + 1) * column_half)
            part = matmul(cots[these, :, columns].reshape(rows, column_half), up[columns, :])
            back_active = part if back_active is None else back_active + part
        dot = jnp.zeros((rows, 1), F32)
        back_parts = []
        for part in range(2):
            columns = slice(part * half, (part + 1) * half)
            back = (back_active[:, columns] * slopes[part, these].reshape(rows, half)).astype(BF16)
            for of_side in range(2):
                role = lax.rem(core + part, 2) + 2 * lax.rem(side + of_side, 2)
                backs[3 + role, these] = back[:, of_side * quarter : (of_side + 1) * quarter].reshape(
                    count, unit, quarter
                )
            dot = dot + jnp.sum(
                back.astype(F32) * hiddens[part, these].reshape(rows, half), axis=-1, keepdims=True
            )
            back_parts.append(back)
        inverse = inverses[these].reshape(rows, 1)
        pull = inverse * inverse * dot * (1.0 / width)
        for piece in range(2):
            columns = slice(piece * column_half, (piece + 1) * column_half)
            back_normed = matmul(back_parts[0], down_turned[0:half, columns]) + matmul(
                back_parts[1], down_turned[half : 2 * half, columns]
            )
            grad = (
                cots[these, :, columns].astype(F32).reshape(rows, column_half)
                + inverse * (gain_ref[:, columns] * back_normed)
                - wide[these, :, columns].astype(F32).reshape(rows, column_half) * pull
            )
            grads[these, :, columns] = grad.astype(BF16).reshape(count, unit, column_half)

            if passing:
                for number in range(count):
                    cot_copy(first + number, piece).start()

        ours = pl.ds(pl.multiple_of(side * column_half, column_half), column_half)
        sided[3, these] = cots[these, :, ours]

        if far:

            @pl.when(streams)
            def _():
                for number in range(count):
                    send_far(first + number)

    @pl.when(is_last)
    def _():
        def from_head(slot, unused):
            head_slot(slot)
            backward(slot * per_slot, per_slot, False, True, False)
            send_slot(slot)
            return unused

        lax.fori_loop(0, micro, from_head, 0)

    def receive(passing):
        def from_next(number, unused):
            backward(number, 1, True, passing, True)

            @pl.when(lax.rem(number, per_slot) == per_slot - 1)
            def _():
                send_slot(lax.div(number, per_slot))

            return unused

        lax.fori_loop(0, units, from_next, 0)

    @pl.when(jnp.logical_and(not_first, not_last))
    def _():
        receive(True)

    @pl.when(jnp.logical_not(not_first))
    def _():
        receive(False)

    grads_copy = pltpu.make_async_copy(grads, grads_out, load_sem.at[3])
    grads_copy.start()

    other_copy = remote(
        head_parts.at[:, 1 - core], head_other, other_send, other_recv, mate
    )

    def term_copy(offset):
        peer = lax.rem(position + offset, positions)
        return remote(
            head_added.at[peer],
            head_terms.at[position],
            term_send.at[offset],
            term_recv.at[position],
            (section, peer * 2 + core),
        )

    def term_wait(offset):
        peer = lax.rem(position + offset, positions)
        remote(
            head_added.at[peer],
            head_terms.at[peer],
            term_send.at[offset],
            term_recv.at[peer],
            (section, peer * 2 + core),
        ).wait_recv()

    def share_copy(number):
        block = sections * me + number
        target = (lax.div(block, replicas), lax.rem(block, replicas))
        return block, remote(head_sums.at[number], head_mine, share_send.at[number], share_recv, target)

    @pl.when(is_last)
    def _():
        part = matmul(
            head_ins[...].reshape(rows_all, width),
            head_slopes[...].reshape(rows_all, head_slopes.shape[2]),
            TN,
        )
        head_parts[...] = part.reshape(head_parts.shape)
        other_copy.start()
        other_copy.wait_recv()
        head_added[...] = head_parts[:, core] + head_other[...]

        def send(offset, unused):
            term_copy(offset).start()
            return unused

        lax.fori_loop(1, positions, send, 0)

    @pl.when(jnp.logical_not(streams))
    def _():
        def send(number, unused):
            send_far(number)
            return unused

        lax.fori_loop(0, units, send, 0)

    row_step = min(256, column_half)
    tokens_all = 4 * rows_all

    def multiply(item):
        def block(number, unused):
            first = number * row_step
            rows = pl.ds(pl.multiple_of(first, row_step), row_step)
            if item < 2:
                of_side = 1 - side if item == 0 else side
                columns = pl.ds(pl.multiple_of(of_side * column_half + first, row_step), row_step)
                left, right = normed[:, :, :, columns], backs[0:4]
            else:
                left = sided[:, :, :, rows]
                right = active[0:4, :, :, (item - 2) * quarter : (item - 1) * quarter]
            products[item, rows] = matmul(
                left.reshape(tokens_all, row_step), right.reshape(tokens_all, quarter), TN
            ).astype(BF16)
            return unused

        lax.fori_loop(0, column_half // row_step, block, 0)

    longest = levels // 2

    def hops(item, way):
        return longest if item % 2 == way else longest - 1

    def rows_of(position):
        return pl.ds(pl.multiple_of(position * chunk, chunk), chunk)

    def ring_rows(item, way, hop):
        left = hops(item, way) - hop
        return rows_of(lax.rem(level + levels + (left if way == 0 else -left), levels))

    def ring_copy(item, way, hop):
        return remote(
            products.at[item, ring_rows(item, way, hop)],
            ring.at[item, way, hop],
            ring_send.at[item, way, hop],
            ring_recv.at[item, way, hop],
            ahead if way == 0 else behind,
        )

    def ways_of(item):
        return (0, 1) if item % 2 == 0 else (1, 0)

    def ring_start(item):
        for way in ways_of(item):
            ring_copy(item, way, 0).start()

    def ring_turn(item, hop):
        for way in ways_of(item):
            if hop < hops(item, way):
                ring_copy(item, way, hop - 1).wait_recv()
                rows = ring_rows(item, way, hop)
                total = products[item, rows].astype(F32) + ring[item, way, hop - 1].astype(F32)
                products[item, rows] = total.astype(BF16)
                ring_copy(item, way, hop).start()

    def ring_total(item):
        total = products[item, rows_of(level)].astype(F32)
        for way in reversed(ways_of(item)):
            last = hops(item, way) - 1
            ring_copy(item, way, last).wait_recv()
            total = total + ring[item, way, last].astype(F32)
        return total

    normed_far.wait_recv()
    normed_relay.start()

    def relay_slot(slot, unused):
        for number in range(per_slot):
            far_copies(slot * per_slot + number)[2].wait_recv()
        relay_copy(slot).start()
        return unused

    lax.fori_loop(0, micro, relay_slot, 0)

    def backs_arrived(slot, unused):
        slot_copies(slot)[1].wait_recv()
        for number in range(per_slot):
            for copy in far_copies(slot * per_slot + number)[:2]:
                copy.wait_recv()
        return unused

    lax.fori_loop(0, micro, backs_arrived, 0)
    normed_copy.wait_recv()
    normed_relay.wait_recv()
    multiply(0)
    ring_start(0)
    multiply(1)
    ring_start(1)

    def cots_arrived(slot, unused):
        slot_copies(slot)[0].wait_recv()
        relay_copy(slot).wait_recv()
        return unused

    lax.fori_loop(0, micro, cots_arrived, 0)
    for copy in (active_copy, active_far, active_cross):
        copy.wait_recv()
    multiply(2)
    ring_start(2)
    multiply(3)
    ring_start(3)

    @pl.when(is_last)
    def _():
        def add_term(offset, total):
            term_wait(offset)
            return total + head_terms[lax.rem(position + offset, positions)]

        total = lax.fori_loop(1, positions, add_term, head_added[position]) / LOSS_SCALE
        pl.semaphore_wait(ready, sections - jnp.where(me == replicas - 1, 1, 0))
        for number in range(sections):
            head_sums[number] = total[number * final : (number + 1) * final]
        for number in range(sections):
            block, copy = share_copy(number)
            to_me = block == (sections - 1) * replicas + me

            @pl.when(to_me)
            def _():
                head_mine[...] = head_sums[number]

            @pl.when(jnp.logical_not(to_me))
            def _():
                copy.start()

    across_copy = remote(
        products.at[0, rows_of(level)], across, across_send.at[0], across_recv.at[0], opposite
    )
    turns = (
        ((0, 1), (1, 1), (2, 1), (0, 2), (3, 1), (1, 2), (0, 3), (2, 2), (3, 2), (1, 3), (2, 3), (3, 3))
        if longest == 4
        else tuple((item, hop) for hop in range(1, longest) for item in range(4))
    )
    for number, (item, hop) in enumerate(turns):
        ring_turn(item, hop)
        if number == len(turns) - 2:
            products[0, rows_of(level)] = ring_total(0).astype(BF16)
            across_copy.start()
    if not turns:
        products[0, rows_of(level)] = ring_total(0).astype(BF16)
        across_copy.start()

    def mate_copy(matrix):
        return remote(
            halves.at[matrix, 1 - core], mates.at[matrix], mate_send.at[matrix], mate_recv.at[matrix], mate
        )

    mine = pl.ds(pl.multiple_of(core * half, half), half)
    theirs = pl.ds(pl.multiple_of((1 - core) * half, half), half)
    halves[0, :, :, pl.ds(pl.multiple_of(side * quarter, quarter), quarter)] = (
        ring_total(1) / LOSS_SCALE
    ).reshape(2, share, quarter)
    for item in (2, 3):
        halves[1, :, :, (item - 2) * quarter : (item - 1) * quarter] = (
            ring_total(item) / LOSS_SCALE
        ).reshape(2, share, quarter)
    mate_copy(1).start()
    up_out[:, mine] = halves[1, core]
    across_copy.wait_recv()
    halves[0, :, :, pl.ds(pl.multiple_of((1 - side) * quarter, quarter), quarter)] = (
        across[...].astype(F32) / LOSS_SCALE
    ).reshape(2, share, quarter)
    mate_copy(0).start()
    down_out[:, mine] = halves[0, core]

    for matrix, result in ((1, up_out), (0, down_out)):
        mate_copy(matrix).wait_recv()
        result[:, theirs] = mates[matrix]

    @pl.when(jnp.logical_not(source_is_me))
    def _():
        share_copy(0)[1].wait_recv()

    head_out[...] = head_mine[...]

    grads_copy.wait()
    for copy in (
        normed_copy,
        normed_far,
        normed_relay,
        active_copy,
        active_far,
        active_cross,
        across_copy,
    ):
        copy.wait_send()

    def slot_left(slot, unused):
        for copy in slot_copies(slot):
            copy.wait_send()
        relay_copy(slot).wait_send()
        for number in range(per_slot):
            for copy in far_copies(slot * per_slot + number):
                copy.wait_send()
        return unused

    lax.fori_loop(0, micro, slot_left, 0)

    @pl.when(not_first)
    def _():
        def cot_left(slot, unused):
            cot_copy(slot, 0).wait_send()
            cot_copy(slot, 1).wait_send()
            return unused

        lax.fori_loop(0, units, cot_left, 0)

    for item in range(4):
        for way in range(2):
            for hop in range(hops(item, way)):
                ring_copy(item, way, hop).wait_send()
    for matrix in range(2):
        mate_copy(matrix).wait_send()

    @pl.when(is_last)
    def _():
        def head_left(offset, unused):
            term_copy(offset).wait_send()
            gather_copy(offset).wait_send()
            return unused

        lax.fori_loop(1, positions, head_left, 0)
        other_copy.wait_send()
        gather_mate(core).wait_send()
        for number in range(sections):
            block, copy = share_copy(number)

            @pl.when(block != (sections - 1) * replicas + me)
            def _():
                copy.wait_send()


def hand_out(*refs):
    sources, results, held, sem = refs[:4], refs[4:8], refs[8:12], refs[12]
    incoming = [
        pltpu.make_async_copy(source, middle, sem.at[0, number])
        for number, (source, middle) in enumerate(zip(sources, held))
    ]
    outgoing = [
        pltpu.make_async_copy(middle, result, sem.at[1, number])
        for number, (middle, result) in enumerate(zip(held, results))
    ]
    for copy in incoming:
        copy.start()
    for arrival, copy in zip(incoming, outgoing):
        arrival.wait()
        copy.start()
    for copy in outgoing:
        copy.wait()


def local(
    sections,
    replicas,
    saved_inputs,
    norm_gain,
    down_weight,
    up_weight,
    head_weight,
    head_gain,
    targets,
    levels,
    level_index,
    plan,
):
    micro, tokens, width = saved_inputs.shape[1:]
    units = down_weight.shape[2]
    half = units // 2
    cols = head_weight.shape[1]
    rings = replicas // 4
    chunk = width // (2 * rings)
    share = width // replicas
    final = share // sections
    unit = tokens // 2
    units_all = 2 * micro
    quarter = half // 2
    longest = rings // 2
    whole = pl.BlockSpec(memory_space=pltpu.VMEM)
    anywhere = pl.BlockSpec(memory_space=pl.ANY)
    dma = pltpu.SemaphoreType.DMA
    grads, down_grad, up_grad, head_grad = pl.pallas_call(
        functools.partial(body, sections, replicas),
        out_shape=(
            jax.ShapeDtypeStruct((units_all, unit, width), BF16),
            jax.ShapeDtypeStruct((share, units), F32),
            jax.ShapeDtypeStruct((share, units), F32),
            jax.ShapeDtypeStruct((final, cols), F32),
        ),
        in_specs=[
            pl.BlockSpec(memory_space=pltpu.SMEM),
            whole,
            anywhere,
            whole,
            anywhere,
            anywhere,
            whole,
            whole,
            whole,
            whole,
        ],
        out_specs=(anywhere, whole, whole, whole),
        scratch_shapes=[
            pltpu.VMEM((micro, tokens, width), BF16),
            pltpu.VMEM((width, units), BF16),
            pltpu.VMEM((width, units), BF16),
            pltpu.VMEM((units, width), BF16),
            pltpu.VMEM((units_all, unit, width), BF16),
            pltpu.VMEM((units_all, unit, 1), F32),
            pltpu.VMEM((4, units_all, unit, width), BF16),
            pltpu.VMEM((5, units_all, unit, half), BF16),
            pltpu.VMEM((2, units_all, unit, half), F32),
            pltpu.VMEM((2, units_all, unit, half), F32),
            pltpu.VMEM((units_all, unit, width), BF16),
            pltpu.VMEM((4, units_all, unit, width // 2), BF16),
            pltpu.VMEM((7, units_all, unit, quarter), BF16),
            pltpu.VMEM((units_all, unit, width), BF16),
            pltpu.VMEM((4, width // 2, quarter), BF16),
            pltpu.VMEM((4, 2, longest, chunk, quarter), BF16),
            pltpu.VMEM((chunk, quarter), BF16),
            pltpu.VMEM((2, 2, share, half), F32),
            pltpu.VMEM((2, share, half), F32),
            pltpu.VMEM((replicas // 2, 2, share, cols), BF16),
            pltpu.VMEM((units_all, unit, width), BF16),
            pltpu.VMEM((units_all, unit, width), BF16),
            pltpu.VMEM((units_all, unit, cols), BF16),
            pltpu.VMEM((replicas // 2, 2, share, cols), F32),
            pltpu.VMEM((replicas // 2, share, cols), F32),
            pltpu.VMEM((replicas // 2, share, cols), F32),
            pltpu.VMEM((replicas // 2, share, cols), F32),
            pltpu.VMEM((sections, final, cols), F32),
            pltpu.VMEM((final, cols), F32),
            dma((4,)),
            dma((units_all, 2)),
            dma((units_all, 2)),
            dma((6,)),
            dma((6,)),
            dma((2, micro)),
            dma((2, micro)),
            dma((3, units_all)),
            dma((3, units_all)),
            dma((micro,)),
            dma((micro,)),
            dma((4, 2, longest)),
            dma((4, 2, longest)),
            dma((1,)),
            dma((1,)),
            dma((2,)),
            dma((2,)),
            dma((replicas // 2,)),
            dma((replicas // 2 + 1,)),
            dma((replicas // 2,)),
            dma((replicas // 2,)),
            dma((sections,)),
            dma(()),
            dma(()),
            dma(()),
            pltpu.SemaphoreType.REGULAR,
        ],
        compiler_params=pltpu.CompilerParams(
            collective_id=0, has_side_effects=True, vmem_limit_bytes=56 * 1024 * 1024
        ),
    )(
        plan,
        level_index.reshape(1, -1),
        saved_inputs[0],
        norm_gain,
        down_weight[0],
        up_weight[0],
        head_weight,
        head_gain.reshape(1, -1),
        targets,
        levels.T,
    )
    grads, down_grad, up_grad, head_grad = pl.pallas_call(
        hand_out,
        out_shape=tuple(
            jax.ShapeDtypeStruct(value.shape, value.dtype)
            for value in (grads, down_grad, up_grad, head_grad)
        ),
        in_specs=[anywhere] * 4,
        out_specs=(anywhere,) * 4,
        scratch_shapes=[
            pltpu.VMEM(value.shape, value.dtype)
            for value in (grads, down_grad, up_grad, head_grad)
        ]
        + [dma((2, 4))],
    )(grads, down_grad, up_grad, head_grad)
    return grads.reshape(1, micro, tokens, width), down_grad[None], up_grad[None], head_grad


def solution(mesh):
    return jax.shard_map(
        functools.partial(local, mesh.shape["section"], mesh.shape["dp"]),
        mesh=mesh,
        in_specs=(
            P("section", None, "dp", None),
            P("section", None),
            P("section", None, None),
            P("section", None, None),
            P("dp", None),
            P(),
            P(None, "dp", None),
            P(),
            P(),
            P(),
        ),
        out_specs=(
            P("section", None, "dp", None),
            P("section", "dp", None),
            P("section", "dp", None),
            P(("section", "dp"), None),
        ),
        check_vma=False,
    )
```

```python
import functools

import jax
import jax.numpy as jnp
from jax import lax
from jax.experimental import pallas as pl
from jax.experimental.pallas import tpu as pltpu
from jax.sharding import PartitionSpec as P

EPS = 1e-06
DELTA = 0.25
BETA = 0.25
LOSS_SCALE = 64.0
SQRT_HALF = 0.7071067811865476
INV_SQRT_TAU = 0.3989422804014327
MESH = pl.DeviceIdType.MESH
F32 = jnp.float32
BF16 = jnp.bfloat16
NN = (((1,), (0,)), ((), ()))
NT = (((1,), (1,)), ((), ()))
TN = (((0,), (0,)), ((), ()))


def matmul(left, right, dims=NN):
    return lax.dot_general(left, right, dims, preferred_element_type=F32)


def inverse_rms(values):
    return lax.rsqrt(jnp.mean(values * values, axis=-1, keepdims=True) + EPS)


def norm_backward(values, inverse, scaling, upstream):
    weighted = upstream * scaling
    mean = jnp.mean(weighted * values, axis=-1, keepdims=True)
    return inverse * weighted - values * (inverse * inverse * inverse) * mean


def soft(values):
    return values * lax.rsqrt(values * values + DELTA * DELTA)


def chain(values, threshold):
    shifted = (values - threshold) / BETA
    softplus = jnp.maximum(shifted, 0.0) + jnp.log1p(jnp.exp(-jnp.abs(shifted)))
    return threshold + BETA * softplus


def chain_rate(values, threshold):
    shifted = (values - threshold) / BETA
    small = jnp.exp(-jnp.abs(shifted))
    return jnp.where(shifted >= 0.0, 1.0, small) / (1.0 + small)


def crps_slope(predicted, observed, threshold):
    variables = observed.shape[1]
    first, second = predicted[:, :variables], predicted[:, variables:]
    chain_first, chain_second = chain(first, threshold), chain(second, threshold)
    chain_obs = chain(observed, threshold)
    pair = soft(chain_first - chain_second)
    slope_first = soft(chain_first - chain_obs) / 2 - pair / 4
    slope_second = soft(chain_second - chain_obs) / 2 + pair / 4
    return jnp.concatenate(
        [
            LOSS_SCALE * chain_rate(first, threshold) * slope_first,
            LOSS_SCALE * chain_rate(second, threshold) * slope_second,
        ],
        axis=1,
    )


def body(
    sections,
    replicas,
    plan_in,
    index_in,
    saved_ref,
    gain_in,
    down_ref,
    up_ref,
    head_in_ref,
    head_gain_in,
    targets_in,
    levels_in,
    grads_out,
    down_out,
    up_out,
    head_out,
    plan_ref,
    index_ref,
    gain_ref,
    head_ref,
    head_gain_ref,
    targets_ref,
    levels_ref,
    saved,
    down,
    up,
    down_turned,
    wide,
    inverses,
    normed,
    active,
    slopes,
    hiddens,
    cots,
    sided,
    backs,
    grads,
    products,
    ring,
    across,
    halves,
    mates,
    full_head,
    outputs,
    head_ins,
    head_slopes,
    head_parts,
    head_other,
    head_added,
    head_terms,
    head_sums,
    head_mine,
    load_sem,
    cot_send,
    cot_recv,
    pair_send,
    pair_recv,
    slot_send,
    slot_recv,
    far_send,
    far_recv,
    relay_send,
    relay_recv,
    ring_send,
    ring_recv,
    across_send,
    across_recv,
    mate_send,
    mate_recv,
    gather_send,
    gather_recv,
    term_send,
    term_recv,
    share_send,
    share_recv,
    other_send,
    other_recv,
    ready,
    small_sem,
    out_sem,
):
    units, unit, width = wide.shape
    micro = saved.shape[0]
    per_slot = units // micro
    rows_all = units * unit
    half = active.shape[-1]
    levels = replicas // 4
    positions = replicas // 2
    chunk = width // (2 * levels)
    column_half = width // 2
    quarter = half // 2
    share = width // replicas
    final = head_mine.shape[0]

    section = lax.axis_index("section")
    me = lax.axis_index("dp")
    core = lax.rem(me, 2)
    level = lax.rem(lax.div(me, 2), levels)
    side = lax.div(me, 2 * levels)
    is_last = section == sections - 1
    not_last = section < sections - 1
    not_first = section > 0
    streams = section < max(sections // 2 - 1, 1)

    def member(side_of, level_of, core_of):
        return (section, (side_of * levels + level_of) * 2 + core_of)

    ahead = member(side, lax.rem(level + 1, levels), core)
    behind = member(side, lax.rem(level + levels - 1, levels), core)
    mate = member(side, level, 1 - core)
    opposite = member(1 - side, level, core)
    diagonal = member(1 - side, level, 1 - core)
    sender = (lax.rem(section + 1, sections), me)
    receiver = (lax.rem(section + sections - 1, sections), me)
    head_source = lax.div(section * replicas + me, sections)
    source_is_me = jnp.logical_and(is_last, head_source == me)

    def remote(src, dst, send, recv, device):
        return pltpu.make_async_remote_copy(
            src_ref=src,
            dst_ref=dst,
            send_sem=send,
            recv_sem=recv,
            device_id=device,
            device_id_type=MESH,
        )

    saved_load = pltpu.make_async_copy(saved_ref, saved, load_sem.at[0])
    down_load = pltpu.make_async_copy(down_ref, down, load_sem.at[1])
    up_load = pltpu.make_async_copy(up_ref, up, load_sem.at[2])
    small_loads = [
        pltpu.make_async_copy(source, held, small_sem.at[number])
        for number, (source, held) in enumerate(
            (
                (plan_in, plan_ref),
                (gain_in, gain_ref),
                (head_in_ref, head_ref),
                (index_in, index_ref),
                (head_gain_in, head_gain_ref),
                (targets_in, targets_ref),
                (levels_in, levels_ref),
            )
        )
    ]

    barrier = pltpu.get_barrier_semaphore()

    def greet(device):
        pl.semaphore_signal(barrier, inc=1, device_id=device, device_id_type=MESH)

    @pl.when(not_last)
    def _():
        greet(sender)
        for device in (ahead, behind, mate, opposite, diagonal):
            greet(device)

    position = side * levels + level

    @pl.when(is_last)
    def _():
        def greet_peer(offset, unused):
            greet((section, lax.rem(position + offset, positions) * 2 + core))
            return unused

        lax.fori_loop(1, positions, greet_peer, 0)
        greet(mate)
        greet(diagonal)
        for number in range(sections):
            block = sections * me + number

            @pl.when(block != (sections - 1) * replicas + me)
            def _():
                greet((lax.div(block, replicas), lax.rem(block, replicas)))

    saved_load.start()
    for load in small_loads[:3]:
        load.start()
    down_load.start()
    up_load.start()
    for load in small_loads[3:]:
        load.start()
    for load in small_loads:
        load.wait()
    saved_load.wait()

    def norm_slot(slot, unused):
        values = saved[plan_ref[slot]]
        these = pl.ds(slot * per_slot, per_slot)
        wide[these] = values.reshape(per_slot, unit, width)
        values = values.astype(F32)
        inverse = inverse_rms(values)
        inverses[these] = inverse.reshape(per_slot, unit, 1)
        normed[3, these] = (
            (values * inverse * gain_ref[...]).astype(BF16).reshape(per_slot, unit, width)
        )
        return unused

    lax.fori_loop(0, micro, norm_slot, 0)

    heard = jnp.where(
        is_last,
        positions + 3 - jnp.where(me == replicas - 1, 1, 0),
        6 + jnp.where(not_first, 1, 0),
    )
    pl.semaphore_wait(barrier, heard)

    @pl.when(jnp.logical_not(source_is_me))
    def _():
        pl.semaphore_signal(
            ready, inc=1, device_id=(sections - 1, head_source), device_id_type=MESH
        )

    def gather_copy(offset):
        peer = lax.rem(position + offset, positions)
        return remote(
            head_ref,
            full_head.at[position, core],
            gather_send.at[offset],
            gather_recv.at[position],
            (section, peer * 2 + core),
        )

    def gather_wait(offset):
        peer = lax.rem(position + offset, positions)
        remote(
            head_ref,
            full_head.at[peer, core],
            gather_send.at[offset],
            gather_recv.at[peer],
            (section, peer * 2 + core),
        ).wait_recv()

    def gather_mate(which):
        return remote(
            full_head.at[:, which],
            full_head.at[:, which],
            gather_send.at[0],
            gather_recv.at[positions],
            mate,
        )

    @pl.when(is_last)
    def _():
        def send(offset, unused):
            gather_copy(offset).start()
            return unused

        lax.fori_loop(1, positions, send, 0)
        full_head[position, core] = head_ref[...]

    normed_copy = remote(normed.at[3], normed.at[0], pair_send.at[0], pair_recv.at[0], mate)
    normed_copy.start()
    normed_far = remote(normed.at[3], normed.at[1], pair_send.at[1], pair_recv.at[1], opposite)
    normed_relay = remote(normed.at[1], normed.at[2], pair_send.at[2], pair_recv.at[2], mate)
    active_copy = remote(active.at[4], active.at[0], pair_send.at[3], pair_recv.at[3], mate)
    active_far = remote(active.at[3], active.at[1], pair_send.at[4], pair_recv.at[4], opposite)
    active_cross = remote(active.at[4], active.at[2], pair_send.at[5], pair_recv.at[5], diagonal)

    normed_far.start()
    down_load.wait()
    step = min(256, half)
    all_normed = normed[3].reshape(rows_all, width)
    for part in range(2):
        where = 3 + lax.rem(core + part, 2)

        def forward(number, unused, part=part, where=where):
            columns = pl.ds(pl.multiple_of(part * half + number * step, step), step)
            inner = pl.ds(pl.multiple_of(number * step, step), step)
            hidden = matmul(all_normed, down[:, columns])
            bell = 0.5 * (1.0 + lax.erf(hidden * SQRT_HALF))
            active[where, :, :, inner] = (
                (hidden * bell).astype(BF16).reshape(units, unit, step)
            )
            slope = bell + hidden * jnp.exp(-0.5 * hidden * hidden) * INV_SQRT_TAU
            slopes[part, :, :, inner] = slope.reshape(units, unit, step)
            hiddens[part, :, :, inner] = hidden.reshape(units, unit, step)
            return unused

        lax.fori_loop(0, half // step, forward, 0)

    active_copy.start()
    active_far.start()
    active_cross.start()
    up_load.wait()

    @pl.when(is_last)
    def _():
        wide_step = min(256, width)

        def output_columns(number, unused):
            columns = pl.ds(pl.multiple_of(number * wide_step, wide_step), wide_step)
            total = wide[:, :, columns].astype(F32).reshape(rows_all, wide_step)
            for part in range(2):
                where = 3 + lax.rem(core + part, 2)
                total = total + matmul(
                    active[where].reshape(rows_all, half),
                    up[columns, part * half : (part + 1) * half],
                    NT,
                )
            outputs[:, :, columns] = total.astype(BF16).reshape(units, unit, wide_step)
            return unused

        lax.fori_loop(0, width // wide_step, output_columns, 0)

    turn_step = min(256, width)

    def turn_columns(number, unused):
        block = pl.ds(pl.multiple_of(number * turn_step, turn_step), turn_step)
        down_turned[block, :] = down[:, block].T
        return unused

    lax.fori_loop(0, 2 * half // turn_step, turn_columns, 0)

    @pl.when(is_last)
    def _():
        def arrive(offset, unused):
            gather_wait(offset)
            return unused

        lax.fori_loop(1, positions, arrive, 0)
        gather_mate(core).start()
        gather_mate(1 - core).wait_recv()

    def head_slot(slot):
        these = pl.ds(slot * per_slot, per_slot)
        rows = per_slot * unit
        choice = lax.broadcasted_iota(jnp.int32, levels_ref.shape, 0) == index_ref[...]
        threshold = jnp.sum(jnp.where(choice, levels_ref[...], 0.0), axis=0, keepdims=True)
        head = full_head[...].reshape(width, full_head.shape[3])
        values = outputs[these].astype(F32).reshape(rows, width)
        inverse = inverse_rms(values)
        head_in = (values * inverse * head_gain_ref[...]).astype(BF16)
        head_ins[these] = head_in.reshape(per_slot, unit, width)
        predicted = matmul(head_in, head)
        slope = crps_slope(predicted, targets_ref[plan_ref[slot]], threshold).astype(BF16)
        head_slopes[these] = slope.reshape(per_slot, unit, slope.shape[1])
        upstream = matmul(slope, head, NT)
        cotangent = norm_backward(values, inverse, head_gain_ref[...], upstream)
        cots[these] = cotangent.astype(BF16).reshape(per_slot, unit, width)

    def cot_copy(slot, piece):
        columns = slice(piece * column_half, (piece + 1) * column_half)
        return remote(
            grads.at[slot, :, columns],
            cots.at[slot, :, columns],
            cot_send.at[slot, piece],
            cot_recv.at[slot, piece],
            receiver,
        )

    def slot_copies(slot):
        these = pl.ds(slot * per_slot, per_slot)
        return (
            remote(
                sided.at[3, these], sided.at[0, these], slot_send.at[0, slot], slot_recv.at[0, slot], mate
            ),
            remote(
                backs.at[4, these], backs.at[0, these], slot_send.at[1, slot], slot_recv.at[1, slot], mate
            ),
        )

    def far_copies(number):
        theirs = pl.ds(pl.multiple_of((1 - side) * column_half, column_half), column_half)
        return (
            remote(
                backs.at[5, number], backs.at[1, number], far_send.at[0, number], far_recv.at[0, number], opposite
            ),
            remote(
                backs.at[6, number], backs.at[2, number], far_send.at[1, number], far_recv.at[1, number], diagonal
            ),
            remote(
                cots.at[number, :, theirs],
                sided.at[1, number],
                far_send.at[2, number],
                far_recv.at[2, number],
                opposite,
            ),
        )

    def relay_copy(slot):
        these = pl.ds(slot * per_slot, per_slot)
        return remote(sided.at[1, these], sided.at[2, these], relay_send.at[slot], relay_recv.at[slot], mate)

    def send_slot(slot):
        for copy in slot_copies(slot):
            copy.start()

    def send_far(number):
        for copy in far_copies(number):
            copy.start()

    def backward(first, count, arriving, passing, far):
        these = pl.ds(first, count)
        rows = count * unit
        back_active = None
        for piece in range(2):
            if arriving:
                cot_copy(first, piece).wait_recv()
            columns = slice(piece * column_half, (piece + 1) * column_half)
            part = matmul(cots[these, :, columns].reshape(rows, column_half), up[columns, :])
            back_active = part if back_active is None else back_active + part
        dot = jnp.zeros((rows, 1), F32)
        back_parts = []
        for part in range(2):
            columns = slice(part * half, (part + 1) * half)
            back = (back_active[:, columns] * slopes[part, these].reshape(rows, half)).astype(BF16)
            for of_side in range(2):
                role = lax.rem(core + part, 2) + 2 * lax.rem(side + of_side, 2)
                backs[3 + role, these] = back[:, of_side * quarter : (of_side + 1) * quarter].reshape(
                    count, unit, quarter
                )
            dot = dot + jnp.sum(
                back.astype(F32) * hiddens[part, these].reshape(rows, half), axis=-1, keepdims=True
            )
            back_parts.append(back)
        inverse = inverses[these].reshape(rows, 1)
        pull = inverse * inverse * dot * (1.0 / width)
        for piece in range(2):
            columns = slice(piece * column_half, (piece + 1) * column_half)
            back_normed = matmul(back_parts[0], down_turned[0:half, columns]) + matmul(
                back_parts[1], down_turned[half : 2 * half, columns]
            )
            grad = (
                cots[these, :, columns].astype(F32).reshape(rows, column_half)
                + inverse * (gain_ref[:, columns] * back_normed)
                - wide[these, :, columns].astype(F32).reshape(rows, column_half) * pull
            )
            grads[these, :, columns] = grad.astype(BF16).reshape(count, unit, column_half)

            if passing:
                for number in range(count):
                    cot_copy(first + number, piece).start()

        ours = pl.ds(pl.multiple_of(side * column_half, column_half), column_half)
        sided[3, these] = cots[these, :, ours]

        if far:

            @pl.when(streams)
            def _():
                for number in range(count):
                    send_far(first + number)

    @pl.when(is_last)
    def _():
        def from_head(slot, unused):
            head_slot(slot)
            backward(slot * per_slot, per_slot, False, True, False)
            send_slot(slot)
            return unused

        lax.fori_loop(0, micro, from_head, 0)

    def receive(passing):
        def from_next(number, unused):
            backward(number, 1, True, passing, True)

            @pl.when(lax.rem(number, per_slot) == per_slot - 1)
            def _():
                send_slot(lax.div(number, per_slot))

            return unused

        lax.fori_loop(0, units, from_next, 0)

    @pl.when(jnp.logical_and(not_first, not_last))
    def _():
        receive(True)

    @pl.when(jnp.logical_not(not_first))
    def _():
        receive(False)

    grads_copy = pltpu.make_async_copy(grads, grads_out, load_sem.at[3])
    grads_copy.start()

    other_copy = remote(
        head_parts.at[:, 1 - core], head_other, other_send, other_recv, mate
    )

    def term_copy(offset):
        peer = lax.rem(position + offset, positions)
        return remote(
            head_added.at[peer],
            head_terms.at[position],
            term_send.at[offset],
            term_recv.at[position],
            (section, peer * 2 + core),
        )

    def term_wait(offset):
        peer = lax.rem(position + offset, positions)
        remote(
            head_added.at[peer],
            head_terms.at[peer],
            term_send.at[offset],
            term_recv.at[peer],
            (section, peer * 2 + core),
        ).wait_recv()

    def share_copy(number):
        block = sections * me + number
        target = (lax.div(block, replicas), lax.rem(block, replicas))
        return block, remote(head_sums.at[number], head_mine, share_send.at[number], share_recv, target)

    @pl.when(is_last)
    def _():
        part = matmul(
            head_ins[...].reshape(rows_all, width),
            head_slopes[...].reshape(rows_all, head_slopes.shape[2]),
            TN,
        )
        head_parts[...] = part.reshape(head_parts.shape)
        other_copy.start()
        other_copy.wait_recv()
        head_added[...] = head_parts[:, core] + head_other[...]

        def send(offset, unused):
            term_copy(offset).start()
            return unused

        lax.fori_loop(1, positions, send, 0)

    @pl.when(jnp.logical_not(streams))
    def _():
        def send(number, unused):
            send_far(number)
            return unused

        lax.fori_loop(0, units, send, 0)

    row_step = min(256, column_half)
    tokens_all = 4 * rows_all

    def multiply(item):
        def block(number, unused):
            first = number * row_step
            rows = pl.ds(pl.multiple_of(first, row_step), row_step)
            if item < 2:
                of_side = 1 - side if item == 0 else side
                columns = pl.ds(pl.multiple_of(of_side * column_half + first, row_step), row_step)
                left, right = normed[:, :, :, columns], backs[0:4]
            else:
                left = sided[:, :, :, rows]
                right = active[0:4, :, :, (item - 2) * quarter : (item - 1) * quarter]
            products[item, rows] = matmul(
                left.reshape(tokens_all, row_step), right.reshape(tokens_all, quarter), TN
            ).astype(BF16)
            return unused

        lax.fori_loop(0, column_half // row_step, block, 0)

    longest = levels // 2

    def hops(item, way):
        return longest if item % 2 == way else longest - 1

    def rows_of(position):
        return pl.ds(pl.multiple_of(position * chunk, chunk), chunk)

    def ring_rows(item, way, hop):
        left = hops(item, way) - hop
        return rows_of(lax.rem(level + levels + (left if way == 0 else -left), levels))

    def ring_copy(item, way, hop):
        return remote(
            products.at[item, ring_rows(item, way, hop)],
            ring.at[item, way, hop],
            ring_send.at[item, way, hop],
            ring_recv.at[item, way, hop],
            ahead if way == 0 else behind,
        )

    def ways_of(item):
        return (0, 1) if item % 2 == 0 else (1, 0)

    def ring_start(item):
        for way in ways_of(item):
            ring_copy(item, way, 0).start()

    def ring_turn(item, hop):
        for way in ways_of(item):
            if hop < hops(item, way):
                ring_copy(item, way, hop - 1).wait_recv()
                rows = ring_rows(item, way, hop)
                total = products[item, rows].astype(F32) + ring[item, way, hop - 1].astype(F32)
                products[item, rows] = total.astype(BF16)
                ring_copy(item, way, hop).start()

    def ring_total(item):
        total = products[item, rows_of(level)].astype(F32)
        for way in reversed(ways_of(item)):
            last = hops(item, way) - 1
            ring_copy(item, way, last).wait_recv()
            total = total + ring[item, way, last].astype(F32)
        return total

    normed_far.wait_recv()
    normed_relay.start()

    def backs_arrived(slot, unused):
        slot_copies(slot)[1].wait_recv()
        for number in range(per_slot):
            for copy in far_copies(slot * per_slot + number)[:2]:
                copy.wait_recv()
        return unused

    lax.fori_loop(0, micro, backs_arrived, 0)
    normed_copy.wait_recv()
    normed_relay.wait_recv()
    multiply(0)
    ring_start(0)

    def relay_slot(slot, unused):
        for number in range(per_slot):
            far_copies(slot * per_slot + number)[2].wait_recv()
        relay_copy(slot).start()
        return unused

    lax.fori_loop(0, micro, relay_slot, 0)

    multiply(1)
    ring_start(1)

    def cots_arrived(slot, unused):
        slot_copies(slot)[0].wait_recv()
        relay_copy(slot).wait_recv()
        return unused

    lax.fori_loop(0, micro, cots_arrived, 0)
    for copy in (active_copy, active_far, active_cross):
        copy.wait_recv()
    multiply(2)
    ring_start(2)
    multiply(3)
    ring_start(3)

    @pl.when(is_last)
    def _():
        def add_term(offset, total):
            term_wait(offset)
            return total + head_terms[lax.rem(position + offset, positions)]

        total = lax.fori_loop(1, positions, add_term, head_added[position]) / LOSS_SCALE
        pl.semaphore_wait(ready, sections - jnp.where(me == replicas - 1, 1, 0))
        for number in range(sections):
            head_sums[number] = total[number * final : (number + 1) * final]
        for number in range(sections):
            block, copy = share_copy(number)
            to_me = block == (sections - 1) * replicas + me

            @pl.when(to_me)
            def _():
                head_mine[...] = head_sums[number]

            @pl.when(jnp.logical_not(to_me))
            def _():
                copy.start()

    across_copy = remote(
        products.at[0, rows_of(level)], across, across_send.at[0], across_recv.at[0], opposite
    )
    turns = (
        ((0, 1), (1, 1), (2, 1), (0, 2), (3, 1), (1, 2), (0, 3), (2, 2), (3, 2), (1, 3), (2, 3), (3, 3))
        if longest == 4
        else tuple((item, hop) for hop in range(1, longest) for item in range(4))
    )
    for number, (item, hop) in enumerate(turns):
        ring_turn(item, hop)
        if number == len(turns) - 2:
            products[0, rows_of(level)] = ring_total(0).astype(BF16)
            across_copy.start()
    if not turns:
        products[0, rows_of(level)] = ring_total(0).astype(BF16)
        across_copy.start()

    def mate_copy(matrix):
        return remote(
            halves.at[matrix, 1 - core], mates.at[matrix], mate_send.at[matrix], mate_recv.at[matrix], mate
        )

    mine = pl.ds(pl.multiple_of(core * half, half), half)
    theirs = pl.ds(pl.multiple_of((1 - core) * half, half), half)
    results = (down_out, up_out)

    def own_out(matrix):
        return pltpu.make_async_copy(
            halves.at[matrix, core], results[matrix].at[:, mine], out_sem.at[matrix]
        )

    def mate_out(matrix):
        return pltpu.make_async_copy(
            mates.at[matrix], results[matrix].at[:, theirs], out_sem.at[2 + matrix]
        )

    halves[0, :, :, pl.ds(pl.multiple_of(side * quarter, quarter), quarter)] = (
        ring_total(1) / LOSS_SCALE
    ).reshape(2, share, quarter)
    for item in (2, 3):
        halves[1, :, :, (item - 2) * quarter : (item - 1) * quarter] = (
            ring_total(item) / LOSS_SCALE
        ).reshape(2, share, quarter)
    mate_copy(1).start()
    own_out(1).start()
    across_copy.wait_recv()
    halves[0, :, :, pl.ds(pl.multiple_of((1 - side) * quarter, quarter), quarter)] = (
        across[...].astype(F32) / LOSS_SCALE
    ).reshape(2, share, quarter)
    mate_copy(0).start()
    own_out(0).start()

    for matrix in (1, 0):
        mate_copy(matrix).wait_recv()
        mate_out(matrix).start()

    @pl.when(jnp.logical_not(source_is_me))
    def _():
        share_copy(0)[1].wait_recv()

    head_write = pltpu.make_async_copy(head_mine, head_out, out_sem.at[4])
    head_write.start()

    grads_copy.wait()
    for matrix in range(2):
        own_out(matrix).wait()
        mate_out(matrix).wait()
    head_write.wait()
    for copy in (
        normed_copy,
        normed_far,
        normed_relay,
        active_copy,
        active_far,
        active_cross,
        across_copy,
    ):
        copy.wait_send()

    def slot_left(slot, unused):
        for copy in slot_copies(slot):
            copy.wait_send()
        relay_copy(slot).wait_send()
        for number in range(per_slot):
            for copy in far_copies(slot * per_slot + number):
                copy.wait_send()
        return unused

    lax.fori_loop(0, micro, slot_left, 0)

    @pl.when(not_first)
    def _():
        def cot_left(slot, unused):
            cot_copy(slot, 0).wait_send()
            cot_copy(slot, 1).wait_send()
            return unused

        lax.fori_loop(0, units, cot_left, 0)

    for item in range(4):
        for way in range(2):
            for hop in range(hops(item, way)):
                ring_copy(item, way, hop).wait_send()
    for matrix in range(2):
        mate_copy(matrix).wait_send()

    @pl.when(is_last)
    def _():
        def head_left(offset, unused):
            term_copy(offset).wait_send()
            gather_copy(offset).wait_send()
            return unused

        lax.fori_loop(1, positions, head_left, 0)
        other_copy.wait_send()
        gather_mate(core).wait_send()
        for number in range(sections):
            block, copy = share_copy(number)

            @pl.when(block != (sections - 1) * replicas + me)
            def _():
                copy.wait_send()


def hand_out(*refs):
    sources, results, held, sem = refs[:4], refs[4:8], refs[8:12], refs[12]
    incoming = [
        pltpu.make_async_copy(source, middle, sem.at[0, number])
        for number, (source, middle) in enumerate(zip(sources, held))
    ]
    outgoing = [
        pltpu.make_async_copy(middle, result, sem.at[1, number])
        for number, (middle, result) in enumerate(zip(held, results))
    ]
    for copy in incoming:
        copy.start()
    for arrival, copy in zip(incoming, outgoing):
        arrival.wait()
        copy.start()
    for copy in outgoing:
        copy.wait()


def local(
    sections,
    replicas,
    saved_inputs,
    norm_gain,
    down_weight,
    up_weight,
    head_weight,
    head_gain,
    targets,
    levels,
    level_index,
    plan,
):
    micro, tokens, width = saved_inputs.shape[1:]
    units = down_weight.shape[2]
    half = units // 2
    cols = head_weight.shape[1]
    rings = replicas // 4
    chunk = width // (2 * rings)
    share = width // replicas
    final = share // sections
    unit = tokens // 2
    units_all = 2 * micro
    quarter = half // 2
    longest = rings // 2
    anywhere = pl.BlockSpec(memory_space=pl.ANY)
    dma = pltpu.SemaphoreType.DMA
    grads, down_grad, up_grad, head_grad = pl.pallas_call(
        functools.partial(body, sections, replicas),
        out_shape=(
            jax.ShapeDtypeStruct((units_all, unit, width), BF16),
            jax.ShapeDtypeStruct((share, units), F32),
            jax.ShapeDtypeStruct((share, units), F32),
            jax.ShapeDtypeStruct((final, cols), F32),
        ),
        in_specs=[anywhere] * 10,
        out_specs=(anywhere,) * 4,
        scratch_shapes=[
            pltpu.SMEM(plan.shape, jnp.int32),
            pltpu.VMEM((1, level_index.shape[0]), jnp.int32),
            pltpu.VMEM(norm_gain.shape, F32),
            pltpu.VMEM(head_weight.shape, BF16),
            pltpu.VMEM((1, width), F32),
            pltpu.VMEM(targets.shape, F32),
            pltpu.VMEM(levels.T.shape, F32),
            pltpu.VMEM((micro, tokens, width), BF16),
            pltpu.VMEM((width, units), BF16),
            pltpu.VMEM((width, units), BF16),
            pltpu.VMEM((units, width), BF16),
            pltpu.VMEM((units_all, unit, width), BF16),
            pltpu.VMEM((units_all, unit, 1), F32),
            pltpu.VMEM((4, units_all, unit, width), BF16),
            pltpu.VMEM((5, units_all, unit, half), BF16),
            pltpu.VMEM((2, units_all, unit, half), F32),
            pltpu.VMEM((2, units_all, unit, half), F32),
            pltpu.VMEM((units_all, unit, width), BF16),
            pltpu.VMEM((4, units_all, unit, width // 2), BF16),
            pltpu.VMEM((7, units_all, unit, quarter), BF16),
            pltpu.VMEM((units_all, unit, width), BF16),
            pltpu.VMEM((4, width // 2, quarter), BF16),
            pltpu.VMEM((4, 2, longest, chunk, quarter), BF16),
            pltpu.VMEM((chunk, quarter), BF16),
            pltpu.VMEM((2, 2, share, half), F32),
            pltpu.VMEM((2, share, half), F32),
            pltpu.VMEM((replicas // 2, 2, share, cols), BF16),
            pltpu.VMEM((units_all, unit, width), BF16),
            pltpu.VMEM((units_all, unit, width), BF16),
            pltpu.VMEM((units_all, unit, cols), BF16),
            pltpu.VMEM((replicas // 2, 2, share, cols), F32),
            pltpu.VMEM((replicas // 2, share, cols), F32),
            pltpu.VMEM((replicas // 2, share, cols), F32),
            pltpu.VMEM((replicas // 2, share, cols), F32),
            pltpu.VMEM((sections, final, cols), F32),
            pltpu.VMEM((final, cols), F32),
            dma((4,)),
            dma((units_all, 2)),
            dma((units_all, 2)),
            dma((6,)),
            dma((6,)),
            dma((2, micro)),
            dma((2, micro)),
            dma((3, units_all)),
            dma((3, units_all)),
            dma((micro,)),
            dma((micro,)),
            dma((4, 2, longest)),
            dma((4, 2, longest)),
            dma((1,)),
            dma((1,)),
            dma((2,)),
            dma((2,)),
            dma((replicas // 2,)),
            dma((replicas // 2 + 1,)),
            dma((replicas // 2,)),
            dma((replicas // 2,)),
            dma((sections,)),
            dma(()),
            dma(()),
            dma(()),
            pltpu.SemaphoreType.REGULAR,
            dma((7,)),
            dma((5,)),
        ],
        compiler_params=pltpu.CompilerParams(
            collective_id=0, has_side_effects=True, vmem_limit_bytes=56 * 1024 * 1024
        ),
    )(
        plan,
        level_index.reshape(1, -1),
        saved_inputs[0],
        norm_gain,
        down_weight[0],
        up_weight[0],
        head_weight,
        head_gain.reshape(1, -1),
        targets,
        levels.T,
    )
    grads, down_grad, up_grad, head_grad = pl.pallas_call(
        hand_out,
        out_shape=tuple(
            jax.ShapeDtypeStruct(value.shape, value.dtype)
            for value in (grads, down_grad, up_grad, head_grad)
        ),
        in_specs=[anywhere] * 4,
        out_specs=(anywhere,) * 4,
        scratch_shapes=[
            pltpu.VMEM(value.shape, value.dtype)
            for value in (grads, down_grad, up_grad, head_grad)
        ]
        + [dma((2, 4))],
    )(grads, down_grad, up_grad, head_grad)
    return grads.reshape(1, micro, tokens, width), down_grad[None], up_grad[None], head_grad


def solution(mesh):
    return jax.shard_map(
        functools.partial(local, mesh.shape["section"], mesh.shape["dp"]),
        mesh=mesh,
        in_specs=(
            P("section", None, "dp", None),
            P("section", None),
            P("section", None, None),
            P("section", None, None),
            P("dp", None),
            P(),
            P(None, "dp", None),
            P(),
            P(),
            P(),
        ),
        out_specs=(
            P("section", None, "dp", None),
            P("section", "dp", None),
            P("section", "dp", None),
            P(("section", "dp"), None),
        ),
        check_vma=False,
    )
```

```python
import functools

import jax
import jax.numpy as jnp
from jax import lax
from jax.experimental import pallas as pl
from jax.experimental.pallas import tpu as pltpu
from jax.sharding import PartitionSpec as P

EPS = 1e-06
DELTA = 0.25
BETA = 0.25
LOSS_SCALE = 64.0
SQRT_HALF = 0.7071067811865476
INV_SQRT_TAU = 0.3989422804014327
MESH = pl.DeviceIdType.MESH
F32 = jnp.float32
BF16 = jnp.bfloat16
NN = (((1,), (0,)), ((), ()))
NT = (((1,), (1,)), ((), ()))
TN = (((0,), (0,)), ((), ()))


def matmul(left, right, dims=NN):
    return lax.dot_general(left, right, dims, preferred_element_type=F32)


def inverse_rms(values):
    return lax.rsqrt(jnp.mean(values * values, axis=-1, keepdims=True) + EPS)


def norm_backward(values, inverse, scaling, upstream):
    weighted = upstream * scaling
    mean = jnp.mean(weighted * values, axis=-1, keepdims=True)
    return inverse * weighted - values * (inverse * inverse * inverse) * mean


def soft(values):
    return values * lax.rsqrt(values * values + DELTA * DELTA)


def chain(values, threshold):
    shifted = (values - threshold) / BETA
    softplus = jnp.maximum(shifted, 0.0) + jnp.log1p(jnp.exp(-jnp.abs(shifted)))
    return threshold + BETA * softplus


def chain_rate(values, threshold):
    shifted = (values - threshold) / BETA
    small = jnp.exp(-jnp.abs(shifted))
    return jnp.where(shifted >= 0.0, 1.0, small) / (1.0 + small)


def crps_slope(predicted, observed, threshold):
    variables = observed.shape[1]
    first, second = predicted[:, :variables], predicted[:, variables:]
    chain_first, chain_second = chain(first, threshold), chain(second, threshold)
    chain_obs = chain(observed, threshold)
    pair = soft(chain_first - chain_second)
    slope_first = soft(chain_first - chain_obs) / 2 - pair / 4
    slope_second = soft(chain_second - chain_obs) / 2 + pair / 4
    return jnp.concatenate(
        [
            LOSS_SCALE * chain_rate(first, threshold) * slope_first,
            LOSS_SCALE * chain_rate(second, threshold) * slope_second,
        ],
        axis=1,
    )


def body(
    sections,
    replicas,
    plan_in,
    index_in,
    saved_ref,
    gain_in,
    down_ref,
    up_ref,
    head_in_ref,
    head_gain_in,
    targets_in,
    levels_in,
    grads_out,
    down_out,
    up_out,
    head_out,
    plan_ref,
    index_ref,
    gain_ref,
    head_ref,
    head_gain_ref,
    targets_ref,
    levels_ref,
    saved,
    down,
    up,
    down_turned,
    wide,
    inverses,
    normed,
    active,
    slopes,
    hiddens,
    cots,
    sided,
    backs,
    grads,
    products,
    ring,
    across,
    halves,
    mates,
    full_head,
    outputs,
    head_ins,
    head_slopes,
    head_parts,
    head_other,
    head_added,
    head_terms,
    head_sums,
    head_mine,
    load_sem,
    cot_send,
    cot_recv,
    pair_send,
    pair_recv,
    slot_send,
    slot_recv,
    far_send,
    far_recv,
    relay_send,
    relay_recv,
    ring_send,
    ring_recv,
    across_send,
    across_recv,
    mate_send,
    mate_recv,
    gather_send,
    gather_recv,
    term_send,
    term_recv,
    share_send,
    share_recv,
    other_send,
    other_recv,
    ready,
    small_sem,
    out_sem,
):
    units, unit, width = wide.shape
    micro = saved.shape[0]
    per_slot = units // micro
    rows_all = units * unit
    half = active.shape[-1]
    levels = replicas // 4
    positions = replicas // 2
    chunk = width // (2 * levels)
    column_half = width // 2
    quarter = half // 2
    share = width // replicas
    final = head_mine.shape[0]

    section = lax.axis_index("section")
    me = lax.axis_index("dp")
    core = lax.rem(me, 2)
    level = lax.rem(lax.div(me, 2), levels)
    side = lax.div(me, 2 * levels)
    is_last = section == sections - 1
    not_last = section < sections - 1
    not_first = section > 0
    streams = section < max(sections // 2 - 1, 1)

    def member(side_of, level_of, core_of):
        return (section, (side_of * levels + level_of) * 2 + core_of)

    ahead = member(side, lax.rem(level + 1, levels), core)
    behind = member(side, lax.rem(level + levels - 1, levels), core)
    mate = member(side, level, 1 - core)
    opposite = member(1 - side, level, core)
    diagonal = member(1 - side, level, 1 - core)
    sender = (lax.rem(section + 1, sections), me)
    receiver = (lax.rem(section + sections - 1, sections), me)
    head_source = lax.div(section * replicas + me, sections)
    source_is_me = jnp.logical_and(is_last, head_source == me)

    def remote(src, dst, send, recv, device):
        return pltpu.make_async_remote_copy(
            src_ref=src,
            dst_ref=dst,
            send_sem=send,
            recv_sem=recv,
            device_id=device,
            device_id_type=MESH,
        )

    saved_load = pltpu.make_async_copy(saved_ref, saved, load_sem.at[0])
    down_load = pltpu.make_async_copy(down_ref, down, load_sem.at[1])
    up_load = pltpu.make_async_copy(up_ref, up, load_sem.at[2])
    small_loads = [
        pltpu.make_async_copy(source, held, small_sem.at[number])
        for number, (source, held) in enumerate(
            (
                (plan_in, plan_ref),
                (gain_in, gain_ref),
                (head_in_ref, head_ref),
                (index_in, index_ref),
                (head_gain_in, head_gain_ref),
                (targets_in, targets_ref),
                (levels_in, levels_ref),
            )
        )
    ]

    barrier = pltpu.get_barrier_semaphore()

    def greet(device):
        pl.semaphore_signal(barrier, inc=1, device_id=device, device_id_type=MESH)

    @pl.when(not_last)
    def _():
        greet(sender)
        for device in (ahead, behind, mate, opposite, diagonal):
            greet(device)

    position = side * levels + level

    @pl.when(is_last)
    def _():
        def greet_peer(offset, unused):
            greet((section, lax.rem(position + offset, positions) * 2 + core))
            return unused

        lax.fori_loop(1, positions, greet_peer, 0)
        greet(mate)
        greet(diagonal)
        for number in range(sections):
            block = sections * me + number

            @pl.when(block != (sections - 1) * replicas + me)
            def _():
                greet((lax.div(block, replicas), lax.rem(block, replicas)))

    saved_load.start()
    for load in small_loads[:3]:
        load.start()
    down_load.start()
    up_load.start()
    for load in small_loads[3:]:
        load.start()
    for load in small_loads:
        load.wait()
    saved_load.wait()

    def norm_slot(slot, unused):
        values = saved[plan_ref[slot]]
        these = pl.ds(slot * per_slot, per_slot)
        wide[these] = values.reshape(per_slot, unit, width)
        values = values.astype(F32)
        inverse = inverse_rms(values)
        inverses[these] = inverse.reshape(per_slot, unit, 1)
        normed[3, these] = (
            (values * inverse * gain_ref[...]).astype(BF16).reshape(per_slot, unit, width)
        )
        return unused

    lax.fori_loop(0, micro, norm_slot, 0)

    heard = jnp.where(
        is_last,
        positions + 3 - jnp.where(me == replicas - 1, 1, 0),
        6 + jnp.where(not_first, 1, 0),
    )
    pl.semaphore_wait(barrier, heard)

    @pl.when(jnp.logical_not(source_is_me))
    def _():
        pl.semaphore_signal(
            ready, inc=1, device_id=(sections - 1, head_source), device_id_type=MESH
        )

    def gather_copy(offset):
        peer = lax.rem(position + offset, positions)
        return remote(
            head_ref,
            full_head.at[position, core],
            gather_send.at[offset],
            gather_recv.at[position],
            (section, peer * 2 + core),
        )

    def gather_wait(offset):
        peer = lax.rem(position + offset, positions)
        remote(
            head_ref,
            full_head.at[peer, core],
            gather_send.at[offset],
            gather_recv.at[peer],
            (section, peer * 2 + core),
        ).wait_recv()

    def gather_mate(which):
        return remote(
            full_head.at[:, which],
            full_head.at[:, which],
            gather_send.at[0],
            gather_recv.at[positions],
            mate,
        )

    @pl.when(is_last)
    def _():
        def send(offset, unused):
            gather_copy(offset).start()
            return unused

        lax.fori_loop(1, positions, send, 0)
        full_head[position, core] = head_ref[...]

    normed_copy = remote(normed.at[3], normed.at[0], pair_send.at[0], pair_recv.at[0], mate)
    normed_copy.start()
    normed_far = remote(normed.at[3], normed.at[1], pair_send.at[1], pair_recv.at[1], opposite)
    normed_relay = remote(normed.at[1], normed.at[2], pair_send.at[2], pair_recv.at[2], mate)
    active_copy = remote(active.at[4], active.at[0], pair_send.at[3], pair_recv.at[3], mate)
    active_far = remote(active.at[3], active.at[1], pair_send.at[4], pair_recv.at[4], opposite)
    active_cross = remote(active.at[4], active.at[2], pair_send.at[5], pair_recv.at[5], diagonal)

    normed_far.start()
    down_load.wait()
    step = min(256, half)
    all_normed = normed[3].reshape(rows_all, width)
    for part in range(2):
        where = 3 + lax.rem(core + part, 2)

        def forward(number, unused, part=part, where=where):
            columns = pl.ds(pl.multiple_of(part * half + number * step, step), step)
            inner = pl.ds(pl.multiple_of(number * step, step), step)
            hidden = matmul(all_normed, down[:, columns])
            bell = 0.5 * (1.0 + lax.erf(hidden * SQRT_HALF))
            active[where, :, :, inner] = (
                (hidden * bell).astype(BF16).reshape(units, unit, step)
            )
            slope = bell + hidden * jnp.exp(-0.5 * hidden * hidden) * INV_SQRT_TAU
            slopes[part, :, :, inner] = slope.reshape(units, unit, step)
            hiddens[part, :, :, inner] = hidden.reshape(units, unit, step)
            return unused

        lax.fori_loop(0, half // step, forward, 0)

    active_copy.start()
    active_far.start()
    active_cross.start()
    up_load.wait()

    @pl.when(is_last)
    def _():
        wide_step = min(256, width)

        def output_columns(number, unused):
            columns = pl.ds(pl.multiple_of(number * wide_step, wide_step), wide_step)
            total = wide[:, :, columns].astype(F32).reshape(rows_all, wide_step)
            for part in range(2):
                where = 3 + lax.rem(core + part, 2)
                total = total + matmul(
                    active[where].reshape(rows_all, half),
                    up[columns, part * half : (part + 1) * half],
                    NT,
                )
            outputs[:, :, columns] = total.astype(BF16).reshape(units, unit, wide_step)
            return unused

        lax.fori_loop(0, width // wide_step, output_columns, 0)

    turn_step = min(256, width)

    def turn_columns(number, unused):
        block = pl.ds(pl.multiple_of(number * turn_step, turn_step), turn_step)
        down_turned[block, :] = down[:, block].T
        return unused

    lax.fori_loop(0, 2 * half // turn_step, turn_columns, 0)

    @pl.when(is_last)
    def _():
        def arrive(offset, unused):
            gather_wait(offset)
            return unused

        lax.fori_loop(1, positions, arrive, 0)
        gather_mate(core).start()
        gather_mate(1 - core).wait_recv()

    def head_slot(slot):
        these = pl.ds(slot * per_slot, per_slot)
        rows = per_slot * unit
        choice = lax.broadcasted_iota(jnp.int32, levels_ref.shape, 0) == index_ref[...]
        threshold = jnp.sum(jnp.where(choice, levels_ref[...], 0.0), axis=0, keepdims=True)
        head = full_head[...].reshape(width, full_head.shape[3])
        values = outputs[these].astype(F32).reshape(rows, width)
        inverse = inverse_rms(values)
        head_in = (values * inverse * head_gain_ref[...]).astype(BF16)
        head_ins[these] = head_in.reshape(per_slot, unit, width)
        predicted = matmul(head_in, head)
        slope = crps_slope(predicted, targets_ref[plan_ref[slot]], threshold).astype(BF16)
        head_slopes[these] = slope.reshape(per_slot, unit, slope.shape[1])
        upstream = matmul(slope, head, NT)
        cotangent = norm_backward(values, inverse, head_gain_ref[...], upstream)
        cots[these] = cotangent.astype(BF16).reshape(per_slot, unit, width)

    def cot_copy(slot, piece):
        columns = slice(piece * column_half, (piece + 1) * column_half)
        return remote(
            grads.at[slot, :, columns],
            cots.at[slot, :, columns],
            cot_send.at[slot, piece],
            cot_recv.at[slot, piece],
            receiver,
        )

    def slot_copies(slot):
        these = pl.ds(slot * per_slot, per_slot)
        return (
            remote(
                sided.at[3, these], sided.at[0, these], slot_send.at[0, slot], slot_recv.at[0, slot], mate
            ),
            remote(
                backs.at[4, these], backs.at[0, these], slot_send.at[1, slot], slot_recv.at[1, slot], mate
            ),
        )

    def far_copies(number):
        theirs = pl.ds(pl.multiple_of((1 - side) * column_half, column_half), column_half)
        return (
            remote(
                backs.at[5, number], backs.at[1, number], far_send.at[0, number], far_recv.at[0, number], opposite
            ),
            remote(
                backs.at[6, number], backs.at[2, number], far_send.at[1, number], far_recv.at[1, number], diagonal
            ),
            remote(
                cots.at[number, :, theirs],
                sided.at[1, number],
                far_send.at[2, number],
                far_recv.at[2, number],
                opposite,
            ),
        )

    def relay_copy(slot):
        these = pl.ds(slot * per_slot, per_slot)
        return remote(sided.at[1, these], sided.at[2, these], relay_send.at[slot], relay_recv.at[slot], mate)

    def send_slot(slot):
        for copy in slot_copies(slot):
            copy.start()

    def send_far(number):
        for copy in far_copies(number):
            copy.start()

    def backward(first, count, arriving, passing, far):
        these = pl.ds(first, count)
        rows = count * unit
        back_active = None
        for piece in range(2):
            if arriving:
                cot_copy(first, piece).wait_recv()
            columns = slice(piece * column_half, (piece + 1) * column_half)
            part = matmul(cots[these, :, columns].reshape(rows, column_half), up[columns, :])
            back_active = part if back_active is None else back_active + part
        dot = jnp.zeros((rows, 1), F32)
        back_parts = []
        for part in range(2):
            columns = slice(part * half, (part + 1) * half)
            back = (back_active[:, columns] * slopes[part, these].reshape(rows, half)).astype(BF16)
            for of_side in range(2):
                role = lax.rem(core + part, 2) + 2 * lax.rem(side + of_side, 2)
                backs[3 + role, these] = back[:, of_side * quarter : (of_side + 1) * quarter].reshape(
                    count, unit, quarter
                )
            dot = dot + jnp.sum(
                back.astype(F32) * hiddens[part, these].reshape(rows, half), axis=-1, keepdims=True
            )
            back_parts.append(back)
        inverse = inverses[these].reshape(rows, 1)
        pull = inverse * inverse * dot * (1.0 / width)
        for piece in range(2):
            columns = slice(piece * column_half, (piece + 1) * column_half)
            back_normed = matmul(back_parts[0], down_turned[0:half, columns]) + matmul(
                back_parts[1], down_turned[half : 2 * half, columns]
            )
            grad = (
                cots[these, :, columns].astype(F32).reshape(rows, column_half)
                + inverse * (gain_ref[:, columns] * back_normed)
                - wide[these, :, columns].astype(F32).reshape(rows, column_half) * pull
            )
            grads[these, :, columns] = grad.astype(BF16).reshape(count, unit, column_half)

            if passing:
                for number in range(count):
                    cot_copy(first + number, piece).start()

        ours = pl.ds(pl.multiple_of(side * column_half, column_half), column_half)
        sided[3, these] = cots[these, :, ours]

        if far:

            @pl.when(streams)
            def _():
                for number in range(count):
                    send_far(first + number)

    @pl.when(is_last)
    def _():
        def from_head(slot, unused):
            head_slot(slot)
            backward(slot * per_slot, per_slot, False, True, False)
            send_slot(slot)
            return unused

        lax.fori_loop(0, micro, from_head, 0)

    def receive(passing):
        def from_next(number, unused):
            backward(number, 1, True, passing, True)

            @pl.when(lax.rem(number, per_slot) == per_slot - 1)
            def _():
                send_slot(lax.div(number, per_slot))

            return unused

        lax.fori_loop(0, units, from_next, 0)

    @pl.when(jnp.logical_and(not_first, not_last))
    def _():
        receive(True)

    @pl.when(jnp.logical_not(not_first))
    def _():
        receive(False)

    grads_copy = pltpu.make_async_copy(grads, grads_out, load_sem.at[3])
    grads_copy.start()

    other_copy = remote(
        head_parts.at[:, 1 - core], head_other, other_send, other_recv, mate
    )

    def term_copy(offset):
        peer = lax.rem(position + offset, positions)
        return remote(
            head_added.at[peer],
            head_terms.at[position],
            term_send.at[offset],
            term_recv.at[position],
            (section, peer * 2 + core),
        )

    def term_wait(offset):
        peer = lax.rem(position + offset, positions)
        remote(
            head_added.at[peer],
            head_terms.at[peer],
            term_send.at[offset],
            term_recv.at[peer],
            (section, peer * 2 + core),
        ).wait_recv()

    def share_copy(number):
        block = sections * me + number
        target = (lax.div(block, replicas), lax.rem(block, replicas))
        return block, remote(head_sums.at[number], head_mine, share_send.at[number], share_recv, target)

    @pl.when(is_last)
    def _():
        part = matmul(
            head_ins[...].reshape(rows_all, width),
            head_slopes[...].reshape(rows_all, head_slopes.shape[2]),
            TN,
        )
        head_parts[...] = part.reshape(head_parts.shape)
        other_copy.start()
        other_copy.wait_recv()
        head_added[...] = head_parts[:, core] + head_other[...]

        def send(offset, unused):
            term_copy(offset).start()
            return unused

        lax.fori_loop(1, positions, send, 0)

    @pl.when(jnp.logical_not(streams))
    def _():
        def send_cots(number, unused):
            far_copies(number)[2].start()
            return unused

        def send_backs(number, unused):
            for copy in far_copies(number)[:2]:
                copy.start()
            return unused

        lax.fori_loop(0, units, send_cots, 0)
        lax.fori_loop(0, units, send_backs, 0)

    row_step = min(256, column_half)
    tokens_all = 4 * rows_all

    def multiply(item):
        def block(number, unused):
            first = number * row_step
            rows = pl.ds(pl.multiple_of(first, row_step), row_step)
            if item < 2:
                of_side = 1 - side if item == 0 else side
                columns = pl.ds(pl.multiple_of(of_side * column_half + first, row_step), row_step)
                left, right = normed[:, :, :, columns], backs[0:4]
            else:
                left = sided[:, :, :, rows]
                right = active[0:4, :, :, (item - 2) * quarter : (item - 1) * quarter]
            products[item, rows] = matmul(
                left.reshape(tokens_all, row_step), right.reshape(tokens_all, quarter), TN
            ).astype(BF16)
            return unused

        lax.fori_loop(0, column_half // row_step, block, 0)

    longest = levels // 2

    def hops(item, way):
        return longest if item % 2 == way else longest - 1

    def rows_of(position):
        return pl.ds(pl.multiple_of(position * chunk, chunk), chunk)

    def ring_rows(item, way, hop):
        left = hops(item, way) - hop
        return rows_of(lax.rem(level + levels + (left if way == 0 else -left), levels))

    def ring_copy(item, way, hop):
        return remote(
            products.at[item, ring_rows(item, way, hop)],
            ring.at[item, way, hop],
            ring_send.at[item, way, hop],
            ring_recv.at[item, way, hop],
            ahead if way == 0 else behind,
        )

    def ways_of(item):
        return (0, 1) if item % 2 == 0 else (1, 0)

    def ring_start(item):
        for way in ways_of(item):
            ring_copy(item, way, 0).start()

    def ring_turn(item, hop):
        for way in ways_of(item):
            if hop < hops(item, way):
                ring_copy(item, way, hop - 1).wait_recv()
                rows = ring_rows(item, way, hop)
                total = products[item, rows].astype(F32) + ring[item, way, hop - 1].astype(F32)
                products[item, rows] = total.astype(BF16)
                ring_copy(item, way, hop).start()

    def ring_total(item):
        total = products[item, rows_of(level)].astype(F32)
        for way in reversed(ways_of(item)):
            last = hops(item, way) - 1
            ring_copy(item, way, last).wait_recv()
            total = total + ring[item, way, last].astype(F32)
        return total

    def backs_arrived(slot, unused):
        slot_copies(slot)[1].wait_recv()
        for number in range(per_slot):
            for copy in far_copies(slot * per_slot + number)[:2]:
                copy.wait_recv()
        return unused

    def relay_slot(slot, unused):
        for number in range(per_slot):
            far_copies(slot * per_slot + number)[2].wait_recv()
        relay_copy(slot).start()
        return unused

    def cots_arrived(slot, unused):
        slot_copies(slot)[0].wait_recv()
        relay_copy(slot).wait_recv()
        return unused

    across_copy = remote(
        products.at[0, rows_of(level)], across, across_send.at[0], across_recv.at[0], opposite
    )
    def trade_across():
        products[0, rows_of(level)] = ring_total(0).astype(BF16)
        across_copy.start()

    def down_arrived():
        lax.fori_loop(0, micro, backs_arrived, 0)
        normed_copy.wait_recv()
        normed_relay.wait_recv()

    def up_arrived():
        lax.fori_loop(0, micro, cots_arrived, 0)
        for copy in (active_copy, active_far, active_cross):
            copy.wait_recv()

    def make(item):
        multiply(item)
        ring_start(item)

    normed_far.wait_recv()
    normed_relay.start()

    @pl.when(streams)
    def _():
        down_arrived()
        make(0)
        lax.fori_loop(0, micro, relay_slot, 0)
        make(1)
        up_arrived()
        make(2)
        make(3)
        turns = (
            ((0, 1), (1, 1), (2, 1), (0, 2), (3, 1), (1, 2), (0, 3), (2, 2), (3, 2), (1, 3), (2, 3), (3, 3))
            if longest == 4
            else tuple((item, hop) for hop in range(1, longest) for item in range(4))
        )
        for item, hop in turns[:-1]:
            ring_turn(item, hop)
        trade_across()
        for item, hop in turns[-1:]:
            ring_turn(item, hop)

    @pl.when(jnp.logical_not(streams))
    def _():
        lax.fori_loop(0, micro, relay_slot, 0)
        up_arrived()
        make(2)
        make(3)
        @pl.when(is_last)
        def _():
            def add_term(offset, total):
                term_wait(offset)
                return total + head_terms[lax.rem(position + offset, positions)]

            total = lax.fori_loop(1, positions, add_term, head_added[position]) / LOSS_SCALE
            pl.semaphore_wait(ready, sections - jnp.where(me == replicas - 1, 1, 0))
            for number in range(sections):
                head_sums[number] = total[number * final : (number + 1) * final]
            for number in range(sections):
                block, copy = share_copy(number)
                to_me = block == (sections - 1) * replicas + me

                @pl.when(to_me)
                def _():
                    head_mine[...] = head_sums[number]

                @pl.when(jnp.logical_not(to_me))
                def _():
                    copy.start()

        for hop in range(1, longest - 1):
            ring_turn(2, hop)
            ring_turn(3, hop)
        down_arrived()
        make(0)
        make(1)
        for hop in range(1, longest):
            ring_turn(0, hop)
            ring_turn(1, hop)
            if hop == 1:
                ring_turn(2, longest - 1)
                ring_turn(3, longest - 1)
        trade_across()

    def mate_copy(matrix):
        return remote(
            halves.at[matrix, 1 - core], mates.at[matrix], mate_send.at[matrix], mate_recv.at[matrix], mate
        )

    mine = pl.ds(pl.multiple_of(core * half, half), half)
    theirs = pl.ds(pl.multiple_of((1 - core) * half, half), half)
    results = (down_out, up_out)

    def own_out(matrix):
        return pltpu.make_async_copy(
            halves.at[matrix, core], results[matrix].at[:, mine], out_sem.at[matrix]
        )

    def mate_out(matrix):
        return pltpu.make_async_copy(
            mates.at[matrix], results[matrix].at[:, theirs], out_sem.at[2 + matrix]
        )

    halves[0, :, :, pl.ds(pl.multiple_of(side * quarter, quarter), quarter)] = (
        ring_total(1) / LOSS_SCALE
    ).reshape(2, share, quarter)
    for item in (2, 3):
        halves[1, :, :, (item - 2) * quarter : (item - 1) * quarter] = (
            ring_total(item) / LOSS_SCALE
        ).reshape(2, share, quarter)
    mate_copy(1).start()
    own_out(1).start()
    across_copy.wait_recv()
    halves[0, :, :, pl.ds(pl.multiple_of((1 - side) * quarter, quarter), quarter)] = (
        across[...].astype(F32) / LOSS_SCALE
    ).reshape(2, share, quarter)
    mate_copy(0).start()
    own_out(0).start()

    for matrix in (1, 0):
        mate_copy(matrix).wait_recv()
        mate_out(matrix).start()

    @pl.when(jnp.logical_not(source_is_me))
    def _():
        share_copy(0)[1].wait_recv()

    head_write = pltpu.make_async_copy(head_mine, head_out, out_sem.at[4])
    head_write.start()

    grads_copy.wait()
    for matrix in range(2):
        own_out(matrix).wait()
        mate_out(matrix).wait()
    head_write.wait()
    for copy in (
        normed_copy,
        normed_far,
        normed_relay,
        active_copy,
        active_far,
        active_cross,
        across_copy,
    ):
        copy.wait_send()

    def slot_left(slot, unused):
        for copy in slot_copies(slot):
            copy.wait_send()
        relay_copy(slot).wait_send()
        for number in range(per_slot):
            for copy in far_copies(slot * per_slot + number):
                copy.wait_send()
        return unused

    lax.fori_loop(0, micro, slot_left, 0)

    @pl.when(not_first)
    def _():
        def cot_left(slot, unused):
            cot_copy(slot, 0).wait_send()
            cot_copy(slot, 1).wait_send()
            return unused

        lax.fori_loop(0, units, cot_left, 0)

    for item in range(4):
        for way in range(2):
            for hop in range(hops(item, way)):
                ring_copy(item, way, hop).wait_send()
    for matrix in range(2):
        mate_copy(matrix).wait_send()

    @pl.when(is_last)
    def _():
        def head_left(offset, unused):
            term_copy(offset).wait_send()
            gather_copy(offset).wait_send()
            return unused

        lax.fori_loop(1, positions, head_left, 0)
        other_copy.wait_send()
        gather_mate(core).wait_send()
        for number in range(sections):
            block, copy = share_copy(number)

            @pl.when(block != (sections - 1) * replicas + me)
            def _():
                copy.wait_send()


def hand_out(*refs):
    sources, results, held, sem = refs[:4], refs[4:8], refs[8:12], refs[12]
    incoming = [
        pltpu.make_async_copy(source, middle, sem.at[0, number])
        for number, (source, middle) in enumerate(zip(sources, held))
    ]
    outgoing = [
        pltpu.make_async_copy(middle, result, sem.at[1, number])
        for number, (middle, result) in enumerate(zip(held, results))
    ]
    for copy in incoming:
        copy.start()
    for arrival, copy in zip(incoming, outgoing):
        arrival.wait()
        copy.start()
    for copy in outgoing:
        copy.wait()


def local(
    sections,
    replicas,
    saved_inputs,
    norm_gain,
    down_weight,
    up_weight,
    head_weight,
    head_gain,
    targets,
    levels,
    level_index,
    plan,
):
    micro, tokens, width = saved_inputs.shape[1:]
    units = down_weight.shape[2]
    half = units // 2
    cols = head_weight.shape[1]
    rings = replicas // 4
    chunk = width // (2 * rings)
    share = width // replicas
    final = share // sections
    unit = tokens // 2
    units_all = 2 * micro
    quarter = half // 2
    longest = rings // 2
    anywhere = pl.BlockSpec(memory_space=pl.ANY)
    dma = pltpu.SemaphoreType.DMA
    grads, down_grad, up_grad, head_grad = pl.pallas_call(
        functools.partial(body, sections, replicas),
        out_shape=(
            jax.ShapeDtypeStruct((units_all, unit, width), BF16),
            jax.ShapeDtypeStruct((share, units), F32),
            jax.ShapeDtypeStruct((share, units), F32),
            jax.ShapeDtypeStruct((final, cols), F32),
        ),
        in_specs=[anywhere] * 10,
        out_specs=(anywhere,) * 4,
        scratch_shapes=[
            pltpu.SMEM(plan.shape, jnp.int32),
            pltpu.VMEM((1, level_index.shape[0]), jnp.int32),
            pltpu.VMEM(norm_gain.shape, F32),
            pltpu.VMEM(head_weight.shape, BF16),
            pltpu.VMEM((1, width), F32),
            pltpu.VMEM(targets.shape, F32),
            pltpu.VMEM(levels.T.shape, F32),
            pltpu.VMEM((micro, tokens, width), BF16),
            pltpu.VMEM((width, units), BF16),
            pltpu.VMEM((width, units), BF16),
            pltpu.VMEM((units, width), BF16),
            pltpu.VMEM((units_all, unit, width), BF16),
            pltpu.VMEM((units_all, unit, 1), F32),
            pltpu.VMEM((4, units_all, unit, width), BF16),
            pltpu.VMEM((5, units_all, unit, half), BF16),
            pltpu.VMEM((2, units_all, unit, half), F32),
            pltpu.VMEM((2, units_all, unit, half), F32),
            pltpu.VMEM((units_all, unit, width), BF16),
            pltpu.VMEM((4, units_all, unit, width // 2), BF16),
            pltpu.VMEM((7, units_all, unit, quarter), BF16),
            pltpu.VMEM((units_all, unit, width), BF16),
            pltpu.VMEM((4, width // 2, quarter), BF16),
            pltpu.VMEM((4, 2, longest, chunk, quarter), BF16),
            pltpu.VMEM((chunk, quarter), BF16),
            pltpu.VMEM((2, 2, share, half), F32),
            pltpu.VMEM((2, share, half), F32),
            pltpu.VMEM((replicas // 2, 2, share, cols), BF16),
            pltpu.VMEM((units_all, unit, width), BF16),
            pltpu.VMEM((units_all, unit, width), BF16),
            pltpu.VMEM((units_all, unit, cols), BF16),
            pltpu.VMEM((replicas // 2, 2, share, cols), F32),
            pltpu.VMEM((replicas // 2, share, cols), F32),
            pltpu.VMEM((replicas // 2, share, cols), F32),
            pltpu.VMEM((replicas // 2, share, cols), F32),
            pltpu.VMEM((sections, final, cols), F32),
            pltpu.VMEM((final, cols), F32),
            dma((4,)),
            dma((units_all, 2)),
            dma((units_all, 2)),
            dma((6,)),
            dma((6,)),
            dma((2, micro)),
            dma((2, micro)),
            dma((3, units_all)),
            dma((3, units_all)),
            dma((micro,)),
            dma((micro,)),
            dma((4, 2, longest)),
            dma((4, 2, longest)),
            dma((1,)),
            dma((1,)),
            dma((2,)),
            dma((2,)),
            dma((replicas // 2,)),
            dma((replicas // 2 + 1,)),
            dma((replicas // 2,)),
            dma((replicas // 2,)),
            dma((sections,)),
            dma(()),
            dma(()),
            dma(()),
            pltpu.SemaphoreType.REGULAR,
            dma((7,)),
            dma((5,)),
        ],
        compiler_params=pltpu.CompilerParams(
            collective_id=0, has_side_effects=True, vmem_limit_bytes=56 * 1024 * 1024
        ),
    )(
        plan,
        level_index.reshape(1, -1),
        saved_inputs[0],
        norm_gain,
        down_weight[0],
        up_weight[0],
        head_weight,
        head_gain.reshape(1, -1),
        targets,
        levels.T,
    )
    grads, down_grad, up_grad, head_grad = pl.pallas_call(
        hand_out,
        out_shape=tuple(
            jax.ShapeDtypeStruct(value.shape, value.dtype)
            for value in (grads, down_grad, up_grad, head_grad)
        ),
        in_specs=[anywhere] * 4,
        out_specs=(anywhere,) * 4,
        scratch_shapes=[
            pltpu.VMEM(value.shape, value.dtype)
            for value in (grads, down_grad, up_grad, head_grad)
        ]
        + [dma((2, 4))],
    )(grads, down_grad, up_grad, head_grad)
    return grads.reshape(1, micro, tokens, width), down_grad[None], up_grad[None], head_grad


def solution(mesh):
    return jax.shard_map(
        functools.partial(local, mesh.shape["section"], mesh.shape["dp"]),
        mesh=mesh,
        in_specs=(
            P("section", None, "dp", None),
            P("section", None),
            P("section", None, None),
            P("section", None, None),
            P("dp", None),
            P(),
            P(None, "dp", None),
            P(),
            P(),
            P(),
        ),
        out_specs=(
            P("section", None, "dp", None),
            P("section", "dp", None),
            P("section", "dp", None),
            P(("section", "dp"), None),
        ),
        check_vma=False,
    )
```

```python
import functools

import jax
import jax.numpy as jnp
from jax import lax
from jax.experimental import pallas as pl
from jax.experimental.pallas import tpu as pltpu
from jax.sharding import PartitionSpec as P

EPS = 1e-06
DELTA = 0.25
BETA = 0.25
LOSS_SCALE = 64.0
SQRT_HALF = 0.7071067811865476
INV_SQRT_TAU = 0.3989422804014327
MESH = pl.DeviceIdType.MESH
F32 = jnp.float32
BF16 = jnp.bfloat16
NN = (((1,), (0,)), ((), ()))
NT = (((1,), (1,)), ((), ()))
TN = (((0,), (0,)), ((), ()))


def matmul(left, right, dims=NN):
    return lax.dot_general(left, right, dims, preferred_element_type=F32)


def inverse_rms(values):
    return lax.rsqrt(jnp.mean(values * values, axis=-1, keepdims=True) + EPS)


def norm_backward(values, inverse, scaling, upstream):
    weighted = upstream * scaling
    mean = jnp.mean(weighted * values, axis=-1, keepdims=True)
    return inverse * weighted - values * (inverse * inverse * inverse) * mean


def soft(values):
    return values * lax.rsqrt(values * values + DELTA * DELTA)


def chain(values, threshold):
    shifted = (values - threshold) / BETA
    softplus = jnp.maximum(shifted, 0.0) + jnp.log1p(jnp.exp(-jnp.abs(shifted)))
    return threshold + BETA * softplus


def chain_rate(values, threshold):
    shifted = (values - threshold) / BETA
    small = jnp.exp(-jnp.abs(shifted))
    return jnp.where(shifted >= 0.0, 1.0, small) / (1.0 + small)


def crps_slope(predicted, observed, threshold):
    variables = observed.shape[1]
    first, second = predicted[:, :variables], predicted[:, variables:]
    chain_first, chain_second = chain(first, threshold), chain(second, threshold)
    chain_obs = chain(observed, threshold)
    pair = soft(chain_first - chain_second)
    slope_first = soft(chain_first - chain_obs) / 2 - pair / 4
    slope_second = soft(chain_second - chain_obs) / 2 + pair / 4
    return jnp.concatenate(
        [
            LOSS_SCALE * chain_rate(first, threshold) * slope_first,
            LOSS_SCALE * chain_rate(second, threshold) * slope_second,
        ],
        axis=1,
    )


def body(
    sections,
    replicas,
    plan_in,
    index_in,
    saved_ref,
    gain_in,
    down_ref,
    up_ref,
    head_in_ref,
    head_gain_in,
    targets_in,
    levels_in,
    grads_out,
    down_out,
    up_out,
    head_out,
    plan_ref,
    index_ref,
    gain_ref,
    head_ref,
    head_gain_ref,
    targets_ref,
    levels_ref,
    saved,
    down,
    up,
    down_turned,
    wide,
    inverses,
    normed,
    active,
    slopes,
    hiddens,
    cots,
    sided,
    backs,
    grads,
    products,
    ring,
    across,
    halves,
    mates,
    full_head,
    outputs,
    head_ins,
    head_slopes,
    head_parts,
    head_other,
    head_added,
    head_terms,
    head_sums,
    head_mine,
    load_sem,
    cot_send,
    cot_recv,
    pair_send,
    pair_recv,
    slot_send,
    slot_recv,
    far_send,
    far_recv,
    relay_send,
    relay_recv,
    ring_send,
    ring_recv,
    across_send,
    across_recv,
    mate_send,
    mate_recv,
    gather_send,
    gather_recv,
    term_send,
    term_recv,
    share_send,
    share_recv,
    other_send,
    other_recv,
    ready,
    small_sem,
    out_sem,
):
    units, unit, width = wide.shape
    micro = saved.shape[0]
    per_slot = units // micro
    rows_all = units * unit
    half = active.shape[-1]
    levels = replicas // 4
    positions = replicas // 2
    chunk = width // (2 * levels)
    column_half = width // 2
    quarter = half // 2
    share = width // replicas
    final = head_mine.shape[0]

    section = lax.axis_index("section")
    me = lax.axis_index("dp")
    core = lax.rem(me, 2)
    level = lax.rem(lax.div(me, 2), levels)
    side = lax.div(me, 2 * levels)
    is_last = section == sections - 1
    not_last = section < sections - 1
    not_first = section > 0
    streams = section < max(sections // 2 - 1, 1)

    def member(side_of, level_of, core_of):
        return (section, (side_of * levels + level_of) * 2 + core_of)

    ahead = member(side, lax.rem(level + 1, levels), core)
    behind = member(side, lax.rem(level + levels - 1, levels), core)
    mate = member(side, level, 1 - core)
    opposite = member(1 - side, level, core)
    diagonal = member(1 - side, level, 1 - core)
    sender = (lax.rem(section + 1, sections), me)
    receiver = (lax.rem(section + sections - 1, sections), me)
    head_source = lax.div(section * replicas + me, sections)
    source_is_me = jnp.logical_and(is_last, head_source == me)

    def remote(src, dst, send, recv, device):
        return pltpu.make_async_remote_copy(
            src_ref=src,
            dst_ref=dst,
            send_sem=send,
            recv_sem=recv,
            device_id=device,
            device_id_type=MESH,
        )

    saved_load = pltpu.make_async_copy(saved_ref, saved, load_sem.at[0])
    down_load = pltpu.make_async_copy(down_ref, down, load_sem.at[1])
    up_load = pltpu.make_async_copy(up_ref, up, load_sem.at[2])
    small_loads = [
        pltpu.make_async_copy(source, held, small_sem.at[number])
        for number, (source, held) in enumerate(
            (
                (plan_in, plan_ref),
                (gain_in, gain_ref),
                (head_in_ref, head_ref),
                (index_in, index_ref),
                (head_gain_in, head_gain_ref),
                (targets_in, targets_ref),
                (levels_in, levels_ref),
            )
        )
    ]

    barrier = pltpu.get_barrier_semaphore()

    def greet(device):
        pl.semaphore_signal(barrier, inc=1, device_id=device, device_id_type=MESH)

    @pl.when(not_last)
    def _():
        greet(sender)
        for device in (ahead, behind, mate, opposite, diagonal):
            greet(device)

    position = side * levels + level
    farthest_first = sorted(
        range(1, positions), key=lambda offset: -min(offset % levels, levels - offset % levels)
    )

    @pl.when(is_last)
    def _():
        for offset in farthest_first:
            greet((section, lax.rem(position + offset, positions) * 2 + core))
        greet(mate)
        greet(diagonal)
        for number in range(sections):
            block = sections * me + number

            @pl.when(block != (sections - 1) * replicas + me)
            def _():
                greet((lax.div(block, replicas), lax.rem(block, replicas)))

    saved_load.start()
    for load in small_loads[:3]:
        load.start()
    down_load.start()
    up_load.start()
    for load in small_loads[3:]:
        load.start()
    for load in small_loads:
        load.wait()
    saved_load.wait()

    def norm_slot(slot, unused):
        values = saved[plan_ref[slot]]
        these = pl.ds(slot * per_slot, per_slot)
        wide[these] = values.reshape(per_slot, unit, width)
        values = values.astype(F32)
        inverse = inverse_rms(values)
        inverses[these] = inverse.reshape(per_slot, unit, 1)
        normed[3, these] = (
            (values * inverse * gain_ref[...]).astype(BF16).reshape(per_slot, unit, width)
        )
        return unused

    lax.fori_loop(0, micro, norm_slot, 0)

    heard = jnp.where(
        is_last,
        positions + 3 - jnp.where(me == replicas - 1, 1, 0),
        6 + jnp.where(not_first, 1, 0),
    )
    pl.semaphore_wait(barrier, heard)


    def gather_copy(offset):
        peer = lax.rem(position + offset, positions)
        return remote(
            head_ref,
            full_head.at[position, core],
            gather_send.at[offset],
            gather_recv.at[position],
            (section, peer * 2 + core),
        )

    def gather_wait(offset):
        peer = lax.rem(position + offset, positions)
        remote(
            head_ref,
            full_head.at[peer, core],
            gather_send.at[offset],
            gather_recv.at[peer],
            (section, peer * 2 + core),
        ).wait_recv()

    def gather_mate(which):
        return remote(
            full_head.at[:, which],
            full_head.at[:, which],
            gather_send.at[0],
            gather_recv.at[positions],
            mate,
        )

    @pl.when(is_last)
    def _():
        for offset in farthest_first:
            gather_copy(offset).start()
        full_head[position, core] = head_ref[...]

    @pl.when(jnp.logical_not(source_is_me))
    def _():
        pl.semaphore_signal(
            ready, inc=1, device_id=(sections - 1, head_source), device_id_type=MESH
        )

    normed_copy = remote(normed.at[3], normed.at[0], pair_send.at[0], pair_recv.at[0], mate)
    normed_copy.start()
    normed_far = remote(normed.at[3], normed.at[1], pair_send.at[1], pair_recv.at[1], opposite)
    normed_relay = remote(normed.at[1], normed.at[2], pair_send.at[2], pair_recv.at[2], mate)
    active_copy = remote(active.at[4], active.at[0], pair_send.at[3], pair_recv.at[3], mate)
    active_far = remote(active.at[3], active.at[1], pair_send.at[4], pair_recv.at[4], opposite)
    active_cross = remote(active.at[4], active.at[2], pair_send.at[5], pair_recv.at[5], diagonal)

    normed_far.start()
    down_load.wait()
    step = min(256, half)
    all_normed = normed[3].reshape(rows_all, width)
    for part in range(2):
        where = 3 + lax.rem(core + part, 2)

        def forward(number, unused, part=part, where=where):
            columns = pl.ds(pl.multiple_of(part * half + number * step, step), step)
            inner = pl.ds(pl.multiple_of(number * step, step), step)
            hidden = matmul(all_normed, down[:, columns])
            bell = 0.5 * (1.0 + lax.erf(hidden * SQRT_HALF))
            active[where, :, :, inner] = (
                (hidden * bell).astype(BF16).reshape(units, unit, step)
            )
            slope = bell + hidden * jnp.exp(-0.5 * hidden * hidden) * INV_SQRT_TAU
            slopes[part, :, :, inner] = slope.reshape(units, unit, step)
            hiddens[part, :, :, inner] = hidden.reshape(units, unit, step)
            return unused

        lax.fori_loop(0, half // step, forward, 0)

    active_copy.start()
    active_far.start()
    active_cross.start()
    up_load.wait()

    @pl.when(is_last)
    def _():
        wide_step = min(256, width)

        def output_columns(number, unused):
            columns = pl.ds(pl.multiple_of(number * wide_step, wide_step), wide_step)
            total = wide[:, :, columns].astype(F32).reshape(rows_all, wide_step)
            for part in range(2):
                where = 3 + lax.rem(core + part, 2)
                total = total + matmul(
                    active[where].reshape(rows_all, half),
                    up[columns, part * half : (part + 1) * half],
                    NT,
                )
            outputs[:, :, columns] = total.astype(BF16).reshape(units, unit, wide_step)
            return unused

        lax.fori_loop(0, width // wide_step, output_columns, 0)

    turn_step = min(256, width)

    def turn_columns(number, unused):
        block = pl.ds(pl.multiple_of(number * turn_step, turn_step), turn_step)
        down_turned[block, :] = down[:, block].T
        return unused

    lax.fori_loop(0, 2 * half // turn_step, turn_columns, 0)

    @pl.when(is_last)
    def _():
        def arrive(offset, unused):
            gather_wait(offset)
            return unused

        lax.fori_loop(1, positions, arrive, 0)
        gather_mate(core).start()
        gather_mate(1 - core).wait_recv()

    def head_slot(slot):
        these = pl.ds(slot * per_slot, per_slot)
        rows = per_slot * unit
        choice = lax.broadcasted_iota(jnp.int32, levels_ref.shape, 0) == index_ref[...]
        threshold = jnp.sum(jnp.where(choice, levels_ref[...], 0.0), axis=0, keepdims=True)
        head = full_head[...].reshape(width, full_head.shape[3])
        values = outputs[these].astype(F32).reshape(rows, width)
        inverse = inverse_rms(values)
        head_in = (values * inverse * head_gain_ref[...]).astype(BF16)
        head_ins[these] = head_in.reshape(per_slot, unit, width)
        predicted = matmul(head_in, head)
        slope = crps_slope(predicted, targets_ref[plan_ref[slot]], threshold).astype(BF16)
        head_slopes[these] = slope.reshape(per_slot, unit, slope.shape[1])
        upstream = matmul(slope, head, NT)
        cotangent = norm_backward(values, inverse, head_gain_ref[...], upstream)
        cots[these] = cotangent.astype(BF16).reshape(per_slot, unit, width)

    def cot_copy(slot, piece):
        columns = slice(piece * column_half, (piece + 1) * column_half)
        return remote(
            grads.at[slot, :, columns],
            cots.at[slot, :, columns],
            cot_send.at[slot, piece],
            cot_recv.at[slot, piece],
            receiver,
        )

    def slot_copies(slot):
        these = pl.ds(slot * per_slot, per_slot)
        return (
            remote(
                sided.at[3, these], sided.at[0, these], slot_send.at[0, slot], slot_recv.at[0, slot], mate
            ),
            remote(
                backs.at[4, these], backs.at[0, these], slot_send.at[1, slot], slot_recv.at[1, slot], mate
            ),
        )

    def far_copies(number):
        theirs = pl.ds(pl.multiple_of((1 - side) * column_half, column_half), column_half)
        return (
            remote(
                backs.at[5, number], backs.at[1, number], far_send.at[0, number], far_recv.at[0, number], opposite
            ),
            remote(
                backs.at[6, number], backs.at[2, number], far_send.at[1, number], far_recv.at[1, number], diagonal
            ),
            remote(
                cots.at[number, :, theirs],
                sided.at[1, number],
                far_send.at[2, number],
                far_recv.at[2, number],
                opposite,
            ),
        )

    def relay_copy(slot):
        these = pl.ds(slot * per_slot, per_slot)
        return remote(sided.at[1, these], sided.at[2, these], relay_send.at[slot], relay_recv.at[slot], mate)

    def send_slot(slot):
        for copy in slot_copies(slot):
            copy.start()

    def send_far(number):
        for copy in far_copies(number):
            copy.start()

    def backward(first, count, arriving, passing, far):
        these = pl.ds(first, count)
        rows = count * unit
        back_active = None
        for piece in range(2):
            if arriving:
                cot_copy(first, piece).wait_recv()
            columns = slice(piece * column_half, (piece + 1) * column_half)
            if not passing and piece == 1:
                for number in range(count):
                    far_copies(first + number)[2].start()
            part = matmul(cots[these, :, columns].reshape(rows, column_half), up[columns, :])
            back_active = part if back_active is None else back_active + part
        dot = jnp.zeros((rows, 1), F32)
        back_parts = []
        for part in range(2):
            columns = slice(part * half, (part + 1) * half)
            back = (back_active[:, columns] * slopes[part, these].reshape(rows, half)).astype(BF16)
            for of_side in range(2):
                role = lax.rem(core + part, 2) + 2 * lax.rem(side + of_side, 2)
                backs[3 + role, these] = back[:, of_side * quarter : (of_side + 1) * quarter].reshape(
                    count, unit, quarter
                )
            dot = dot + jnp.sum(
                back.astype(F32) * hiddens[part, these].reshape(rows, half), axis=-1, keepdims=True
            )
            back_parts.append(back)
        if not passing:
            for number in range(count):
                for copy in far_copies(first + number)[:2]:
                    copy.start()
        inverse = inverses[these].reshape(rows, 1)
        pull = inverse * inverse * dot * (1.0 / width)
        for piece in range(2):
            columns = slice(piece * column_half, (piece + 1) * column_half)
            back_normed = matmul(back_parts[0], down_turned[0:half, columns]) + matmul(
                back_parts[1], down_turned[half : 2 * half, columns]
            )
            grad = (
                cots[these, :, columns].astype(F32).reshape(rows, column_half)
                + inverse * (gain_ref[:, columns] * back_normed)
                - wide[these, :, columns].astype(F32).reshape(rows, column_half) * pull
            )
            grads[these, :, columns] = grad.astype(BF16).reshape(count, unit, column_half)

            if passing:
                for number in range(count):
                    cot_copy(first + number, piece).start()

        ours = pl.ds(pl.multiple_of(side * column_half, column_half), column_half)
        sided[3, these] = cots[these, :, ours]

        if far and passing:

            @pl.when(streams)
            def _():
                for number in range(count):
                    send_far(first + number)

    @pl.when(is_last)
    def _():
        def from_head(slot, unused):
            head_slot(slot)
            backward(slot * per_slot, per_slot, False, True, False)
            send_slot(slot)
            return unused

        lax.fori_loop(0, micro, from_head, 0)

    def receive(passing):
        def from_next(number, unused):
            backward(number, 1, True, passing, True)

            @pl.when(lax.rem(number, per_slot) == per_slot - 1)
            def _():
                send_slot(lax.div(number, per_slot))

            return unused

        lax.fori_loop(0, units, from_next, 0)

    @pl.when(jnp.logical_and(not_first, not_last))
    def _():
        receive(True)

    @pl.when(jnp.logical_not(not_first))
    def _():
        receive(False)

    grads_copy = pltpu.make_async_copy(grads, grads_out, load_sem.at[3])
    grads_copy.start()

    other_copy = remote(
        head_parts.at[:, 1 - core], head_other, other_send, other_recv, mate
    )

    def term_copy(offset):
        peer = lax.rem(position + offset, positions)
        return remote(
            head_added.at[peer],
            head_terms.at[position],
            term_send.at[offset],
            term_recv.at[position],
            (section, peer * 2 + core),
        )

    def term_wait(offset):
        peer = lax.rem(position + offset, positions)
        remote(
            head_added.at[peer],
            head_terms.at[peer],
            term_send.at[offset],
            term_recv.at[peer],
            (section, peer * 2 + core),
        ).wait_recv()

    def share_copy(number):
        block = sections * me + number
        target = (lax.div(block, replicas), lax.rem(block, replicas))
        return block, remote(head_sums.at[number], head_mine, share_send.at[number], share_recv, target)

    @pl.when(is_last)
    def _():
        part = matmul(
            head_ins[...].reshape(rows_all, width),
            head_slopes[...].reshape(rows_all, head_slopes.shape[2]),
            TN,
        )
        head_parts[...] = part.reshape(head_parts.shape)
        other_copy.start()
        other_copy.wait_recv()
        head_added[...] = head_parts[:, core] + head_other[...]

        def send(offset, unused):
            term_copy(offset).start()
            return unused

        lax.fori_loop(1, positions, send, 0)

    @pl.when(jnp.logical_not(streams))
    def _():
        def send_cots(number, unused):
            far_copies(number)[2].start()
            return unused

        def send_backs(number, unused):
            for copy in far_copies(number)[:2]:
                copy.start()
            return unused

        lax.fori_loop(0, units, send_cots, 0)
        lax.fori_loop(0, units, send_backs, 0)

    row_step = min(256, column_half)
    tokens_all = 4 * rows_all

    def multiply(item):
        def block(number, unused):
            first = number * row_step
            rows = pl.ds(pl.multiple_of(first, row_step), row_step)
            if item < 2:
                of_side = 1 - side if item == 0 else side
                columns = pl.ds(pl.multiple_of(of_side * column_half + first, row_step), row_step)
                left, right = normed[:, :, :, columns], backs[0:4]
            else:
                left = sided[:, :, :, rows]
                right = active[0:4, :, :, (item - 2) * quarter : (item - 1) * quarter]
            products[item, rows] = matmul(
                left.reshape(tokens_all, row_step), right.reshape(tokens_all, quarter), TN
            ).astype(BF16)
            return unused

        lax.fori_loop(0, column_half // row_step, block, 0)

    longest = levels // 2

    def hops(item, way):
        return longest if item % 2 == way else longest - 1

    def rows_of(position):
        return pl.ds(pl.multiple_of(position * chunk, chunk), chunk)

    def ring_rows(item, way, hop):
        left = hops(item, way) - hop
        return rows_of(lax.rem(level + levels + (left if way == 0 else -left), levels))

    def ring_copy(item, way, hop):
        return remote(
            products.at[item, ring_rows(item, way, hop)],
            ring.at[item, way, hop],
            ring_send.at[item, way, hop],
            ring_recv.at[item, way, hop],
            ahead if way == 0 else behind,
        )

    def ways_of(item):
        return (0, 1) if item % 2 == 0 else (1, 0)

    def ring_start(item):
        for way in ways_of(item):
            ring_copy(item, way, 0).start()

    def ring_turn(item, hop):
        for way in ways_of(item):
            if hop < hops(item, way):
                ring_copy(item, way, hop - 1).wait_recv()
                rows = ring_rows(item, way, hop)
                total = products[item, rows].astype(F32) + ring[item, way, hop - 1].astype(F32)
                products[item, rows] = total.astype(BF16)
                ring_copy(item, way, hop).start()

    def ring_total(item):
        total = products[item, rows_of(level)].astype(F32)
        for way in reversed(ways_of(item)):
            last = hops(item, way) - 1
            ring_copy(item, way, last).wait_recv()
            total = total + ring[item, way, last].astype(F32)
        return total

    def backs_arrived(slot, unused):
        slot_copies(slot)[1].wait_recv()
        for number in range(per_slot):
            for copy in far_copies(slot * per_slot + number)[:2]:
                copy.wait_recv()
        return unused

    def relay_slot(slot, unused):
        for number in range(per_slot):
            far_copies(slot * per_slot + number)[2].wait_recv()
        relay_copy(slot).start()
        return unused

    def cots_arrived(slot, unused):
        slot_copies(slot)[0].wait_recv()
        relay_copy(slot).wait_recv()
        return unused

    across_copy = remote(
        products.at[0, rows_of(level)], across, across_send.at[0], across_recv.at[0], opposite
    )
    def trade_across():
        products[0, rows_of(level)] = ring_total(0).astype(BF16)
        across_copy.start()

    def down_arrived():
        lax.fori_loop(0, micro, backs_arrived, 0)
        normed_copy.wait_recv()
        normed_relay.wait_recv()

    def up_arrived():
        lax.fori_loop(0, micro, cots_arrived, 0)
        for copy in (active_copy, active_far, active_cross):
            copy.wait_recv()

    def make(item):
        multiply(item)
        ring_start(item)

    normed_far.wait_recv()
    normed_relay.start()

    @pl.when(streams)
    def _():
        down_arrived()
        make(0)
        lax.fori_loop(0, micro, relay_slot, 0)
        make(1)
        up_arrived()
        make(2)
        make(3)
        turns = (
            ((0, 1), (1, 1), (2, 1), (0, 2), (3, 1), (1, 2), (0, 3), (2, 2), (3, 2), (1, 3), (2, 3), (3, 3))
            if longest == 4
            else tuple((item, hop) for hop in range(1, longest) for item in range(4))
        )
        for item, hop in turns[:-1]:
            ring_turn(item, hop)
        trade_across()
        for item, hop in turns[-1:]:
            ring_turn(item, hop)

    @pl.when(jnp.logical_not(streams))
    def _():
        lax.fori_loop(0, micro, relay_slot, 0)
        up_arrived()
        make(2)
        make(3)
        @pl.when(is_last)
        def _():
            def add_term(offset, total):
                term_wait(offset)
                return total + head_terms[lax.rem(position + offset, positions)]

            total = lax.fori_loop(1, positions, add_term, head_added[position]) / LOSS_SCALE
            pl.semaphore_wait(ready, sections - jnp.where(me == replicas - 1, 1, 0))
            for number in range(sections):
                head_sums[number] = total[number * final : (number + 1) * final]
            for number in range(sections):
                block, copy = share_copy(number)
                to_me = block == (sections - 1) * replicas + me

                @pl.when(to_me)
                def _():
                    head_mine[...] = head_sums[number]

                @pl.when(jnp.logical_not(to_me))
                def _():
                    copy.start()

        for hop in range(1, longest - 1):
            ring_turn(2, hop)
            ring_turn(3, hop)
        down_arrived()
        make(0)
        make(1)
        for hop in range(1, longest):
            ring_turn(0, hop)
            ring_turn(1, hop)
            if hop == 1:
                ring_turn(2, longest - 1)
                ring_turn(3, longest - 1)
        trade_across()

    def mate_copy(matrix):
        return remote(
            halves.at[matrix, 1 - core], mates.at[matrix], mate_send.at[matrix], mate_recv.at[matrix], mate
        )

    mine = pl.ds(pl.multiple_of(core * half, half), half)
    theirs = pl.ds(pl.multiple_of((1 - core) * half, half), half)
    results = (down_out, up_out)

    def own_out(matrix):
        return pltpu.make_async_copy(
            halves.at[matrix, core], results[matrix].at[:, mine], out_sem.at[matrix]
        )

    def mate_out(matrix):
        return pltpu.make_async_copy(
            mates.at[matrix], results[matrix].at[:, theirs], out_sem.at[2 + matrix]
        )

    halves[0, :, :, pl.ds(pl.multiple_of(side * quarter, quarter), quarter)] = (
        ring_total(1) / LOSS_SCALE
    ).reshape(2, share, quarter)
    for item in (2, 3):
        halves[1, :, :, (item - 2) * quarter : (item - 1) * quarter] = (
            ring_total(item) / LOSS_SCALE
        ).reshape(2, share, quarter)
    mate_copy(1).start()
    own_out(1).start()
    across_copy.wait_recv()
    halves[0, :, :, pl.ds(pl.multiple_of((1 - side) * quarter, quarter), quarter)] = (
        across[...].astype(F32) / LOSS_SCALE
    ).reshape(2, share, quarter)
    mate_copy(0).start()
    own_out(0).start()

    for matrix in (1, 0):
        mate_copy(matrix).wait_recv()
        mate_out(matrix).start()

    @pl.when(jnp.logical_not(source_is_me))
    def _():
        share_copy(0)[1].wait_recv()

    head_write = pltpu.make_async_copy(head_mine, head_out, out_sem.at[4])
    head_write.start()

    grads_copy.wait()
    for matrix in range(2):
        own_out(matrix).wait()
        mate_out(matrix).wait()
    head_write.wait()
    for copy in (
        normed_copy,
        normed_far,
        normed_relay,
        active_copy,
        active_far,
        active_cross,
        across_copy,
    ):
        copy.wait_send()

    def slot_left(slot, unused):
        for copy in slot_copies(slot):
            copy.wait_send()
        relay_copy(slot).wait_send()
        for number in range(per_slot):
            for copy in far_copies(slot * per_slot + number):
                copy.wait_send()
        return unused

    lax.fori_loop(0, micro, slot_left, 0)

    @pl.when(not_first)
    def _():
        def cot_left(slot, unused):
            cot_copy(slot, 0).wait_send()
            cot_copy(slot, 1).wait_send()
            return unused

        lax.fori_loop(0, units, cot_left, 0)

    for item in range(4):
        for way in range(2):
            for hop in range(hops(item, way)):
                ring_copy(item, way, hop).wait_send()
    for matrix in range(2):
        mate_copy(matrix).wait_send()

    @pl.when(is_last)
    def _():
        def head_left(offset, unused):
            term_copy(offset).wait_send()
            gather_copy(offset).wait_send()
            return unused

        lax.fori_loop(1, positions, head_left, 0)
        other_copy.wait_send()
        gather_mate(core).wait_send()
        for number in range(sections):
            block, copy = share_copy(number)

            @pl.when(block != (sections - 1) * replicas + me)
            def _():
                copy.wait_send()


def hand_out(*refs):
    sources, results, held, sem = refs[:4], refs[4:8], refs[8:12], refs[12]
    incoming = [
        pltpu.make_async_copy(source, middle, sem.at[0, number])
        for number, (source, middle) in enumerate(zip(sources, held))
    ]
    outgoing = [
        pltpu.make_async_copy(middle, result, sem.at[1, number])
        for number, (middle, result) in enumerate(zip(held, results))
    ]
    for copy in incoming:
        copy.start()
    for arrival, copy in zip(incoming, outgoing):
        arrival.wait()
        copy.start()
    for copy in outgoing:
        copy.wait()


def local(
    sections,
    replicas,
    saved_inputs,
    norm_gain,
    down_weight,
    up_weight,
    head_weight,
    head_gain,
    targets,
    levels,
    level_index,
    plan,
):
    micro, tokens, width = saved_inputs.shape[1:]
    units = down_weight.shape[2]
    half = units // 2
    cols = head_weight.shape[1]
    rings = replicas // 4
    chunk = width // (2 * rings)
    share = width // replicas
    final = share // sections
    unit = tokens // 2
    units_all = 2 * micro
    quarter = half // 2
    longest = rings // 2
    anywhere = pl.BlockSpec(memory_space=pl.ANY)
    dma = pltpu.SemaphoreType.DMA
    grads, down_grad, up_grad, head_grad = pl.pallas_call(
        functools.partial(body, sections, replicas),
        out_shape=(
            jax.ShapeDtypeStruct((units_all, unit, width), BF16),
            jax.ShapeDtypeStruct((share, units), F32),
            jax.ShapeDtypeStruct((share, units), F32),
            jax.ShapeDtypeStruct((final, cols), F32),
        ),
        in_specs=[anywhere] * 10,
        out_specs=(anywhere,) * 4,
        scratch_shapes=[
            pltpu.SMEM(plan.shape, jnp.int32),
            pltpu.VMEM((1, level_index.shape[0]), jnp.int32),
            pltpu.VMEM(norm_gain.shape, F32),
            pltpu.VMEM(head_weight.shape, BF16),
            pltpu.VMEM((1, width), F32),
            pltpu.VMEM(targets.shape, F32),
            pltpu.VMEM(levels.T.shape, F32),
            pltpu.VMEM((micro, tokens, width), BF16),
            pltpu.VMEM((width, units), BF16),
            pltpu.VMEM((width, units), BF16),
            pltpu.VMEM((units, width), BF16),
            pltpu.VMEM((units_all, unit, width), BF16),
            pltpu.VMEM((units_all, unit, 1), F32),
            pltpu.VMEM((4, units_all, unit, width), BF16),
            pltpu.VMEM((5, units_all, unit, half), BF16),
            pltpu.VMEM((2, units_all, unit, half), F32),
            pltpu.VMEM((2, units_all, unit, half), F32),
            pltpu.VMEM((units_all, unit, width), BF16),
            pltpu.VMEM((4, units_all, unit, width // 2), BF16),
            pltpu.VMEM((7, units_all, unit, quarter), BF16),
            pltpu.VMEM((units_all, unit, width), BF16),
            pltpu.VMEM((4, width // 2, quarter), BF16),
            pltpu.VMEM((4, 2, longest, chunk, quarter), BF16),
            pltpu.VMEM((chunk, quarter), BF16),
            pltpu.VMEM((2, 2, share, half), F32),
            pltpu.VMEM((2, share, half), F32),
            pltpu.VMEM((replicas // 2, 2, share, cols), BF16),
            pltpu.VMEM((units_all, unit, width), BF16),
            pltpu.VMEM((units_all, unit, width), BF16),
            pltpu.VMEM((units_all, unit, cols), BF16),
            pltpu.VMEM((replicas // 2, 2, share, cols), F32),
            pltpu.VMEM((replicas // 2, share, cols), F32),
            pltpu.VMEM((replicas // 2, share, cols), F32),
            pltpu.VMEM((replicas // 2, share, cols), F32),
            pltpu.VMEM((sections, final, cols), F32),
            pltpu.VMEM((final, cols), F32),
            dma((4,)),
            dma((units_all, 2)),
            dma((units_all, 2)),
            dma((6,)),
            dma((6,)),
            dma((2, micro)),
            dma((2, micro)),
            dma((3, units_all)),
            dma((3, units_all)),
            dma((micro,)),
            dma((micro,)),
            dma((4, 2, longest)),
            dma((4, 2, longest)),
            dma((1,)),
            dma((1,)),
            dma((2,)),
            dma((2,)),
            dma((replicas // 2,)),
            dma((replicas // 2 + 1,)),
            dma((replicas // 2,)),
            dma((replicas // 2,)),
            dma((sections,)),
            dma(()),
            dma(()),
            dma(()),
            pltpu.SemaphoreType.REGULAR,
            dma((7,)),
            dma((5,)),
        ],
        compiler_params=pltpu.CompilerParams(
            collective_id=0, has_side_effects=True, vmem_limit_bytes=56 * 1024 * 1024
        ),
    )(
        plan,
        level_index.reshape(1, -1),
        saved_inputs[0],
        norm_gain,
        down_weight[0],
        up_weight[0],
        head_weight,
        head_gain.reshape(1, -1),
        targets,
        levels.T,
    )
    grads, down_grad, up_grad, head_grad = pl.pallas_call(
        hand_out,
        out_shape=tuple(
            jax.ShapeDtypeStruct(value.shape, value.dtype)
            for value in (grads, down_grad, up_grad, head_grad)
        ),
        in_specs=[anywhere] * 4,
        out_specs=(anywhere,) * 4,
        scratch_shapes=[
            pltpu.VMEM(value.shape, value.dtype)
            for value in (grads, down_grad, up_grad, head_grad)
        ]
        + [dma((2, 4))],
    )(grads, down_grad, up_grad, head_grad)
    return grads.reshape(1, micro, tokens, width), down_grad[None], up_grad[None], head_grad


def solution(mesh):
    return jax.shard_map(
        functools.partial(local, mesh.shape["section"], mesh.shape["dp"]),
        mesh=mesh,
        in_specs=(
            P("section", None, "dp", None),
            P("section", None),
            P("section", None, None),
            P("section", None, None),
            P("dp", None),
            P(),
            P(None, "dp", None),
            P(),
            P(),
            P(),
        ),
        out_specs=(
            P("section", None, "dp", None),
            P("section", "dp", None),
            P("section", "dp", None),
            P(("section", "dp"), None),
        ),
        check_vma=False,
    )
```

```python
import functools

import jax
import jax.numpy as jnp
from jax import lax
from jax.experimental import pallas as pl
from jax.experimental.pallas import tpu as pltpu
from jax.sharding import PartitionSpec as P

EPS = 1e-06
DELTA = 0.25
BETA = 0.25
LOSS_SCALE = 64.0
SQRT_HALF = 0.7071067811865476
INV_SQRT_TAU = 0.3989422804014327
MESH = pl.DeviceIdType.MESH
F32 = jnp.float32
BF16 = jnp.bfloat16
NN = (((1,), (0,)), ((), ()))
NT = (((1,), (1,)), ((), ()))
TN = (((0,), (0,)), ((), ()))


def matmul(left, right, dims=NN):
    return lax.dot_general(left, right, dims, preferred_element_type=F32)


def inverse_rms(values):
    return lax.rsqrt(jnp.mean(values * values, axis=-1, keepdims=True) + EPS)


def norm_backward(values, inverse, scaling, upstream):
    weighted = upstream * scaling
    mean = jnp.mean(weighted * values, axis=-1, keepdims=True)
    return inverse * weighted - values * (inverse * inverse * inverse) * mean


def soft(values):
    return values * lax.rsqrt(values * values + DELTA * DELTA)


def chain(values, threshold):
    shifted = (values - threshold) / BETA
    softplus = jnp.maximum(shifted, 0.0) + jnp.log1p(jnp.exp(-jnp.abs(shifted)))
    return threshold + BETA * softplus


def chain_rate(values, threshold):
    shifted = (values - threshold) / BETA
    small = jnp.exp(-jnp.abs(shifted))
    return jnp.where(shifted >= 0.0, 1.0, small) / (1.0 + small)


def crps_slope(predicted, observed, threshold):
    variables = observed.shape[1]
    first, second = predicted[:, :variables], predicted[:, variables:]
    chain_first, chain_second = chain(first, threshold), chain(second, threshold)
    chain_obs = chain(observed, threshold)
    pair = soft(chain_first - chain_second)
    slope_first = soft(chain_first - chain_obs) / 2 - pair / 4
    slope_second = soft(chain_second - chain_obs) / 2 + pair / 4
    return jnp.concatenate(
        [
            LOSS_SCALE * chain_rate(first, threshold) * slope_first,
            LOSS_SCALE * chain_rate(second, threshold) * slope_second,
        ],
        axis=1,
    )


def body(
    sections,
    replicas,
    plan_in,
    index_in,
    saved_ref,
    gain_in,
    down_ref,
    up_ref,
    head_in_ref,
    head_gain_in,
    targets_in,
    levels_in,
    grads_out,
    down_out,
    up_out,
    head_out,
    plan_ref,
    index_ref,
    gain_ref,
    head_ref,
    head_gain_ref,
    targets_ref,
    levels_ref,
    saved,
    down,
    up,
    down_turned,
    wide,
    inverses,
    normed,
    active,
    slopes,
    hiddens,
    cots,
    sided,
    backs,
    grads,
    products,
    ring,
    across,
    halves,
    mates,
    full_head,
    outputs,
    head_ins,
    head_slopes,
    head_parts,
    head_other,
    head_added,
    head_terms,
    head_sums,
    head_mine,
    load_sem,
    cot_send,
    cot_recv,
    pair_send,
    pair_recv,
    slot_send,
    slot_recv,
    far_send,
    far_recv,
    relay_send,
    relay_recv,
    ring_send,
    ring_recv,
    across_send,
    across_recv,
    mate_send,
    mate_recv,
    gather_send,
    gather_recv,
    term_send,
    term_recv,
    share_send,
    share_recv,
    other_send,
    other_recv,
    ready,
    small_sem,
    out_sem,
):
    units, unit, width = wide.shape
    micro = saved.shape[0]
    per_slot = units // micro
    rows_all = units * unit
    half = active.shape[-1]
    levels = replicas // 4
    positions = replicas // 2
    chunk = width // (2 * levels)
    column_half = width // 2
    quarter = half // 2
    share = width // replicas
    final = head_mine.shape[0]

    section = lax.axis_index("section")
    me = lax.axis_index("dp")
    core = lax.rem(me, 2)
    level = lax.rem(lax.div(me, 2), levels)
    side = lax.div(me, 2 * levels)
    is_last = section == sections - 1
    not_last = section < sections - 1
    not_first = section > 0
    streams = section < max(sections // 2 - 1, 1)

    def member(side_of, level_of, core_of):
        return (section, (side_of * levels + level_of) * 2 + core_of)

    ahead = member(side, lax.rem(level + 1, levels), core)
    behind = member(side, lax.rem(level + levels - 1, levels), core)
    mate = member(side, level, 1 - core)
    opposite = member(1 - side, level, core)
    diagonal = member(1 - side, level, 1 - core)
    sender = (lax.rem(section + 1, sections), me)
    receiver = (lax.rem(section + sections - 1, sections), me)
    head_source = lax.div(section * replicas + me, sections)
    source_is_me = jnp.logical_and(is_last, head_source == me)

    def remote(src, dst, send, recv, device):
        return pltpu.make_async_remote_copy(
            src_ref=src,
            dst_ref=dst,
            send_sem=send,
            recv_sem=recv,
            device_id=device,
            device_id_type=MESH,
        )

    saved_load = pltpu.make_async_copy(saved_ref, saved, load_sem.at[0])
    down_load = pltpu.make_async_copy(down_ref, down, load_sem.at[1])
    up_load = pltpu.make_async_copy(up_ref, up, load_sem.at[2])
    small_loads = [
        pltpu.make_async_copy(source, held, small_sem.at[number])
        for number, (source, held) in enumerate(
            (
                (plan_in, plan_ref),
                (gain_in, gain_ref),
                (head_in_ref, head_ref),
                (index_in, index_ref),
                (head_gain_in, head_gain_ref),
                (targets_in, targets_ref),
                (levels_in, levels_ref),
            )
        )
    ]

    barrier = pltpu.get_barrier_semaphore()

    def greet(device):
        pl.semaphore_signal(barrier, inc=1, device_id=device, device_id_type=MESH)

    @pl.when(not_last)
    def _():
        greet(sender)
        for device in (ahead, behind, mate, opposite, diagonal):
            greet(device)

    position = side * levels + level
    farthest_first = sorted(
        range(1, positions), key=lambda offset: -min(offset % levels, levels - offset % levels)
    )

    @pl.when(is_last)
    def _():
        for offset in farthest_first:
            greet((section, lax.rem(position + offset, positions) * 2 + core))
        greet(mate)
        greet(diagonal)
        for number in range(sections):
            block = sections * me + number

            @pl.when(block != (sections - 1) * replicas + me)
            def _():
                greet((lax.div(block, replicas), lax.rem(block, replicas)))

    saved_load.start()
    for load in small_loads[:3]:
        load.start()
    down_load.start()
    up_load.start()
    for load in small_loads[3:]:
        load.start()
    for load in small_loads:
        load.wait()
    saved_load.wait()

    def norm_slot(slot, unused):
        values = saved[plan_ref[slot]]
        these = pl.ds(slot * per_slot, per_slot)
        wide[these] = values.reshape(per_slot, unit, width)
        values = values.astype(F32)
        inverse = inverse_rms(values)
        inverses[these] = inverse.reshape(per_slot, unit, 1)
        normed[3, these] = (
            (values * inverse * gain_ref[...]).astype(BF16).reshape(per_slot, unit, width)
        )
        return unused

    lax.fori_loop(0, micro, norm_slot, 0)

    heard = jnp.where(
        is_last,
        positions + 3 - jnp.where(me == replicas - 1, 1, 0),
        6 + jnp.where(not_first, 1, 0),
    )
    pl.semaphore_wait(barrier, heard)


    def gather_copy(offset):
        peer = lax.rem(position + offset, positions)
        return remote(
            head_ref,
            full_head.at[position, core],
            gather_send.at[offset],
            gather_recv.at[position],
            (section, peer * 2 + core),
        )

    def gather_wait(offset):
        peer = lax.rem(position + offset, positions)
        remote(
            head_ref,
            full_head.at[peer, core],
            gather_send.at[offset],
            gather_recv.at[peer],
            (section, peer * 2 + core),
        ).wait_recv()

    def gather_mate(which):
        return remote(
            full_head.at[:, which],
            full_head.at[:, which],
            gather_send.at[0],
            gather_recv.at[positions],
            mate,
        )

    @pl.when(is_last)
    def _():
        for offset in farthest_first:
            gather_copy(offset).start()
        full_head[position, core] = head_ref[...]

    @pl.when(jnp.logical_not(source_is_me))
    def _():
        pl.semaphore_signal(
            ready, inc=1, device_id=(sections - 1, head_source), device_id_type=MESH
        )

    normed_copy = remote(normed.at[3], normed.at[0], pair_send.at[0], pair_recv.at[0], mate)
    normed_copy.start()
    normed_far = remote(normed.at[3], normed.at[1], pair_send.at[1], pair_recv.at[1], opposite)
    normed_relay = remote(normed.at[1], normed.at[2], pair_send.at[2], pair_recv.at[2], mate)
    active_copy = remote(active.at[4], active.at[0], pair_send.at[3], pair_recv.at[3], mate)
    active_far = remote(active.at[3], active.at[1], pair_send.at[4], pair_recv.at[4], opposite)
    active_cross = remote(active.at[4], active.at[2], pair_send.at[5], pair_recv.at[5], diagonal)

    normed_far.start()
    down_load.wait()
    step = min(256, half)
    all_normed = normed[3].reshape(rows_all, width)
    for part in range(2):
        where = 3 + lax.rem(core + part, 2)

        def forward(number, unused, part=part, where=where):
            columns = pl.ds(pl.multiple_of(part * half + number * step, step), step)
            inner = pl.ds(pl.multiple_of(number * step, step), step)
            hidden = matmul(all_normed, down[:, columns])
            bell = 0.5 * (1.0 + lax.erf(hidden * SQRT_HALF))
            active[where, :, :, inner] = (
                (hidden * bell).astype(BF16).reshape(units, unit, step)
            )
            slope = bell + hidden * jnp.exp(-0.5 * hidden * hidden) * INV_SQRT_TAU
            slopes[part, :, :, inner] = slope.reshape(units, unit, step)
            hiddens[part, :, :, inner] = hidden.reshape(units, unit, step)
            return unused

        lax.fori_loop(0, half // step, forward, 0)

    active_copy.start()
    active_far.start()
    active_cross.start()
    up_load.wait()

    @pl.when(is_last)
    def _():
        wide_step = min(256, width)

        def output_columns(number, unused):
            columns = pl.ds(pl.multiple_of(number * wide_step, wide_step), wide_step)
            total = wide[:, :, columns].astype(F32).reshape(rows_all, wide_step)
            for part in range(2):
                where = 3 + lax.rem(core + part, 2)
                total = total + matmul(
                    active[where].reshape(rows_all, half),
                    up[columns, part * half : (part + 1) * half],
                    NT,
                )
            outputs[:, :, columns] = total.astype(BF16).reshape(units, unit, wide_step)
            return unused

        lax.fori_loop(0, width // wide_step, output_columns, 0)

    turn_step = min(256, width)

    def turn_columns(number, unused):
        block = pl.ds(pl.multiple_of(number * turn_step, turn_step), turn_step)
        down_turned[block, :] = down[:, block].T
        return unused

    lax.fori_loop(0, 2 * half // turn_step, turn_columns, 0)

    @pl.when(is_last)
    def _():
        def arrive(offset, unused):
            gather_wait(offset)
            return unused

        lax.fori_loop(1, positions, arrive, 0)
        gather_mate(core).start()
        gather_mate(1 - core).wait_recv()

    def head_slot(slot):
        these = pl.ds(slot * per_slot, per_slot)
        rows = per_slot * unit
        choice = lax.broadcasted_iota(jnp.int32, levels_ref.shape, 0) == index_ref[...]
        threshold = jnp.sum(jnp.where(choice, levels_ref[...], 0.0), axis=0, keepdims=True)
        head = full_head[...].reshape(width, full_head.shape[3])
        values = outputs[these].astype(F32).reshape(rows, width)
        inverse = inverse_rms(values)
        head_in = (values * inverse * head_gain_ref[...]).astype(BF16)
        head_ins[these] = head_in.reshape(per_slot, unit, width)
        predicted = matmul(head_in, head)
        slope = crps_slope(predicted, targets_ref[plan_ref[slot]], threshold).astype(BF16)
        head_slopes[these] = slope.reshape(per_slot, unit, slope.shape[1])
        upstream = matmul(slope, head, NT)
        cotangent = norm_backward(values, inverse, head_gain_ref[...], upstream)
        cots[these] = cotangent.astype(BF16).reshape(per_slot, unit, width)

    def cot_copy(slot, piece):
        columns = slice(piece * column_half, (piece + 1) * column_half)
        return remote(
            grads.at[slot, :, columns],
            cots.at[slot, :, columns],
            cot_send.at[slot, piece],
            cot_recv.at[slot, piece],
            receiver,
        )

    def slot_copies(slot):
        these = pl.ds(slot * per_slot, per_slot)
        return (
            remote(
                sided.at[3, these], sided.at[0, these], slot_send.at[0, slot], slot_recv.at[0, slot], mate
            ),
            remote(
                backs.at[4, these], backs.at[0, these], slot_send.at[1, slot], slot_recv.at[1, slot], mate
            ),
        )

    def far_copies(number):
        theirs = pl.ds(pl.multiple_of((1 - side) * column_half, column_half), column_half)
        return (
            remote(
                backs.at[5, number], backs.at[1, number], far_send.at[0, number], far_recv.at[0, number], opposite
            ),
            remote(
                backs.at[6, number], backs.at[2, number], far_send.at[1, number], far_recv.at[1, number], diagonal
            ),
            remote(
                cots.at[number, :, theirs],
                sided.at[1, number],
                far_send.at[2, number],
                far_recv.at[2, number],
                opposite,
            ),
        )

    def relay_copy(slot):
        these = pl.ds(slot * per_slot, per_slot)
        return remote(sided.at[1, these], sided.at[2, these], relay_send.at[slot], relay_recv.at[slot], mate)

    def send_slot(slot):
        for copy in slot_copies(slot):
            copy.start()

    def send_far(number):
        for copy in far_copies(number):
            copy.start()

    def backward(first, count, arriving, passing, far):
        these = pl.ds(first, count)
        rows = count * unit
        back_active = None
        for piece in range(2):
            if arriving:
                cot_copy(first, piece).wait_recv()
            columns = slice(piece * column_half, (piece + 1) * column_half)
            if not passing and piece == 1:
                for number in range(count):
                    far_copies(first + number)[2].start()
            part = matmul(cots[these, :, columns].reshape(rows, column_half), up[columns, :])
            back_active = part if back_active is None else back_active + part
        dot = jnp.zeros((rows, 1), F32)
        back_parts = []
        for part in range(2):
            columns = slice(part * half, (part + 1) * half)
            back = (back_active[:, columns] * slopes[part, these].reshape(rows, half)).astype(BF16)
            for of_side in range(2):
                role = lax.rem(core + part, 2) + 2 * lax.rem(side + of_side, 2)
                backs[3 + role, these] = back[:, of_side * quarter : (of_side + 1) * quarter].reshape(
                    count, unit, quarter
                )
            dot = dot + jnp.sum(
                back.astype(F32) * hiddens[part, these].reshape(rows, half), axis=-1, keepdims=True
            )
            back_parts.append(back)
        if not passing:
            for number in range(count):
                for copy in far_copies(first + number)[:2]:
                    copy.start()
        inverse = inverses[these].reshape(rows, 1)
        pull = inverse * inverse * dot * (1.0 / width)
        for piece in range(2):
            columns = slice(piece * column_half, (piece + 1) * column_half)
            back_normed = matmul(back_parts[0], down_turned[0:half, columns]) + matmul(
                back_parts[1], down_turned[half : 2 * half, columns]
            )
            grad = (
                cots[these, :, columns].astype(F32).reshape(rows, column_half)
                + inverse * (gain_ref[:, columns] * back_normed)
                - wide[these, :, columns].astype(F32).reshape(rows, column_half) * pull
            )
            grads[these, :, columns] = grad.astype(BF16).reshape(count, unit, column_half)

            if passing:
                for number in range(count):
                    cot_copy(first + number, piece).start()

        ours = pl.ds(pl.multiple_of(side * column_half, column_half), column_half)
        sided[3, these] = cots[these, :, ours]

        if far and passing:

            @pl.when(streams)
            def _():
                for number in range(count):
                    send_far(first + number)

    @pl.when(is_last)
    def _():
        def from_head(slot, unused):
            head_slot(slot)
            backward(slot * per_slot, per_slot, False, True, False)
            send_slot(slot)
            return unused

        lax.fori_loop(0, micro, from_head, 0)

    def receive(passing):
        def from_next(number, unused):
            backward(number, 1, True, passing, True)

            @pl.when(lax.rem(number, per_slot) == per_slot - 1)
            def _():
                send_slot(lax.div(number, per_slot))

            return unused

        lax.fori_loop(0, units, from_next, 0)

    @pl.when(jnp.logical_and(not_first, not_last))
    def _():
        receive(True)

    @pl.when(jnp.logical_not(not_first))
    def _():
        receive(False)

    grads_copy = pltpu.make_async_copy(grads, grads_out, load_sem.at[3])
    grads_copy.start()

    other_copy = remote(
        head_parts.at[:, 1 - core], head_other, other_send, other_recv, mate
    )

    def term_copy(offset):
        peer = lax.rem(position + offset, positions)
        return remote(
            head_added.at[peer],
            head_terms.at[position],
            term_send.at[offset],
            term_recv.at[position],
            (section, peer * 2 + core),
        )

    def term_wait(offset):
        peer = lax.rem(position + offset, positions)
        remote(
            head_added.at[peer],
            head_terms.at[peer],
            term_send.at[offset],
            term_recv.at[peer],
            (section, peer * 2 + core),
        ).wait_recv()

    def share_copy(number):
        block = sections * me + number
        target = (lax.div(block, replicas), lax.rem(block, replicas))
        return block, remote(head_sums.at[number], head_mine, share_send.at[number], share_recv, target)

    @pl.when(is_last)
    def _():
        part = matmul(
            head_ins[...].reshape(rows_all, width),
            head_slopes[...].reshape(rows_all, head_slopes.shape[2]),
            TN,
        )
        head_parts[...] = part.reshape(head_parts.shape)
        other_copy.start()
        other_copy.wait_recv()
        head_added[...] = head_parts[:, core] + head_other[...]

        def send(offset, unused):
            term_copy(offset).start()
            return unused

        lax.fori_loop(1, positions, send, 0)

    @pl.when(jnp.logical_not(streams))
    def _():
        def send_cots(number, unused):
            far_copies(number)[2].start()
            return unused

        def send_backs(number, unused):
            for copy in far_copies(number)[:2]:
                copy.start()
            return unused

        lax.fori_loop(0, units, send_cots, 0)
        lax.fori_loop(0, units, send_backs, 0)

    row_step = min(256, column_half)
    tokens_all = 4 * rows_all

    def multiply(item):
        def block(number, unused):
            first = number * row_step
            rows = pl.ds(pl.multiple_of(first, row_step), row_step)
            if item < 2:
                of_side = 1 - side if item == 0 else side
                columns = pl.ds(pl.multiple_of(of_side * column_half + first, row_step), row_step)
                left, right = normed[:, :, :, columns], backs[0:4]
            else:
                left = sided[:, :, :, rows]
                right = active[0:4, :, :, (item - 2) * quarter : (item - 1) * quarter]
            products[item, rows] = matmul(
                left.reshape(tokens_all, row_step), right.reshape(tokens_all, quarter), TN
            ).astype(BF16)
            return unused

        lax.fori_loop(0, column_half // row_step, block, 0)

    longest = levels // 2

    def hops(item, way):
        return longest if item % 2 == way else longest - 1

    def rows_of(position):
        return pl.ds(pl.multiple_of(position * chunk, chunk), chunk)

    def ring_rows(item, way, hop):
        left = hops(item, way) - hop
        return rows_of(lax.rem(level + levels + (left if way == 0 else -left), levels))

    def ring_copy(item, way, hop):
        return remote(
            products.at[item, ring_rows(item, way, hop)],
            ring.at[item, way, hop],
            ring_send.at[item, way, hop],
            ring_recv.at[item, way, hop],
            ahead if way == 0 else behind,
        )

    def ways_of(item):
        return (0, 1) if item % 2 == 0 else (1, 0)

    def ring_start(item):
        for way in ways_of(item):
            ring_copy(item, way, 0).start()

    def ring_turn(item, hop):
        for way in ways_of(item):
            if hop < hops(item, way):
                ring_copy(item, way, hop - 1).wait_recv()
                rows = ring_rows(item, way, hop)
                total = products[item, rows].astype(F32) + ring[item, way, hop - 1].astype(F32)
                products[item, rows] = total.astype(BF16)
                ring_copy(item, way, hop).start()

    def ring_total(item):
        total = products[item, rows_of(level)].astype(F32)
        for way in reversed(ways_of(item)):
            last = hops(item, way) - 1
            ring_copy(item, way, last).wait_recv()
            total = total + ring[item, way, last].astype(F32)
        return total

    def backs_arrived(slot, unused):
        slot_copies(slot)[1].wait_recv()
        for number in range(per_slot):
            for copy in far_copies(slot * per_slot + number)[:2]:
                copy.wait_recv()
        return unused

    def relay_slot(slot, unused):
        for number in range(per_slot):
            far_copies(slot * per_slot + number)[2].wait_recv()
        relay_copy(slot).start()
        return unused

    def cots_arrived(slot, unused):
        slot_copies(slot)[0].wait_recv()
        relay_copy(slot).wait_recv()
        return unused

    across_copy = remote(
        products.at[0, rows_of(level)], across, across_send.at[0], across_recv.at[0], opposite
    )
    def trade_across():
        products[0, rows_of(level)] = ring_total(0).astype(BF16)
        across_copy.start()

    def down_arrived():
        lax.fori_loop(0, micro, backs_arrived, 0)
        normed_copy.wait_recv()
        normed_relay.wait_recv()

    def up_arrived():
        lax.fori_loop(0, micro, cots_arrived, 0)
        for copy in (active_copy, active_far, active_cross):
            copy.wait_recv()

    def make(item):
        multiply(item)
        ring_start(item)

    normed_far.wait_recv()
    normed_relay.start()

    @pl.when(streams)
    def _():
        down_arrived()
        make(0)
        lax.fori_loop(0, micro, relay_slot, 0)
        make(1)
        up_arrived()
        make(2)
        make(3)
        turns = (
            ((0, 1), (1, 1), (2, 1), (0, 2), (3, 1), (1, 2), (0, 3), (2, 2), (3, 2), (1, 3), (2, 3), (3, 3))
            if longest == 4
            else tuple((item, hop) for hop in range(1, longest) for item in range(4))
        )
        for item, hop in turns[:-1]:
            ring_turn(item, hop)
        trade_across()
        for item, hop in turns[-1:]:
            ring_turn(item, hop)

    @pl.when(jnp.logical_not(streams))
    def _():
        lax.fori_loop(0, micro, relay_slot, 0)
        up_arrived()
        make(2)
        make(3)
        @pl.when(is_last)
        def _():
            def add_term(offset, total):
                term_wait(offset)
                return total + head_terms[lax.rem(position + offset, positions)]

            total = lax.fori_loop(1, positions, add_term, head_added[position]) / LOSS_SCALE
            pl.semaphore_wait(ready, sections - jnp.where(me == replicas - 1, 1, 0))
            for number in range(sections):
                head_sums[number] = total[number * final : (number + 1) * final]
            for number in range(sections):
                block, copy = share_copy(number)
                to_me = block == (sections - 1) * replicas + me

                @pl.when(to_me)
                def _():
                    head_mine[...] = head_sums[number]

                @pl.when(jnp.logical_not(to_me))
                def _():
                    copy.start()

        for hop in range(1, longest - 1):
            ring_turn(2, hop)
            ring_turn(3, hop)
        down_arrived()
        make(0)
        make(1)
        for hop in range(1, longest):
            ring_turn(0, hop)
            ring_turn(1, hop)
            if hop == 1:
                ring_turn(2, longest - 1)
                ring_turn(3, longest - 1)
        trade_across()

    def mate_copy(matrix, piece):
        which = piece if matrix == 1 else lax.rem(side + piece, 2)
        columns = pl.ds(pl.multiple_of(which * quarter, quarter), quarter)
        return remote(
            halves.at[matrix, 1 - core, :, columns],
            mates.at[matrix, :, columns],
            mate_send.at[matrix, piece],
            mate_recv.at[matrix, piece],
            mate,
        )

    mine = pl.ds(pl.multiple_of(core * half, half), half)
    theirs = pl.ds(pl.multiple_of((1 - core) * half, half), half)
    results = (down_out, up_out)

    def own_out(matrix):
        return pltpu.make_async_copy(
            halves.at[matrix, core], results[matrix].at[:, mine], out_sem.at[matrix]
        )

    def mate_out(matrix):
        return pltpu.make_async_copy(
            mates.at[matrix], results[matrix].at[:, theirs], out_sem.at[2 + matrix]
        )

    halves[0, :, :, pl.ds(pl.multiple_of(side * quarter, quarter), quarter)] = (
        ring_total(1) / LOSS_SCALE
    ).reshape(2, share, quarter)
    mate_copy(0, 0).start()
    for item in (2, 3):
        halves[1, :, :, (item - 2) * quarter : (item - 1) * quarter] = (
            ring_total(item) / LOSS_SCALE
        ).reshape(2, share, quarter)
        mate_copy(1, item - 2).start()
    own_out(1).start()
    across_copy.wait_recv()
    halves[0, :, :, pl.ds(pl.multiple_of((1 - side) * quarter, quarter), quarter)] = (
        across[...].astype(F32) / LOSS_SCALE
    ).reshape(2, share, quarter)
    mate_copy(0, 1).start()
    own_out(0).start()

    for matrix in (1, 0):
        for piece in range(2):
            mate_copy(matrix, piece).wait_recv()
        mate_out(matrix).start()

    @pl.when(jnp.logical_not(source_is_me))
    def _():
        share_copy(0)[1].wait_recv()

    head_write = pltpu.make_async_copy(head_mine, head_out, out_sem.at[4])
    head_write.start()

    grads_copy.wait()
    for matrix in range(2):
        own_out(matrix).wait()
        mate_out(matrix).wait()
    head_write.wait()
    for copy in (
        normed_copy,
        normed_far,
        normed_relay,
        active_copy,
        active_far,
        active_cross,
        across_copy,
    ):
        copy.wait_send()

    def slot_left(slot, unused):
        for copy in slot_copies(slot):
            copy.wait_send()
        relay_copy(slot).wait_send()
        for number in range(per_slot):
            for copy in far_copies(slot * per_slot + number):
                copy.wait_send()
        return unused

    lax.fori_loop(0, micro, slot_left, 0)

    @pl.when(not_first)
    def _():
        def cot_left(slot, unused):
            cot_copy(slot, 0).wait_send()
            cot_copy(slot, 1).wait_send()
            return unused

        lax.fori_loop(0, units, cot_left, 0)

    for item in range(4):
        for way in range(2):
            for hop in range(hops(item, way)):
                ring_copy(item, way, hop).wait_send()
    for matrix in range(2):
        for piece in range(2):
            mate_copy(matrix, piece).wait_send()

    @pl.when(is_last)
    def _():
        def head_left(offset, unused):
            term_copy(offset).wait_send()
            gather_copy(offset).wait_send()
            return unused

        lax.fori_loop(1, positions, head_left, 0)
        other_copy.wait_send()
        gather_mate(core).wait_send()
        for number in range(sections):
            block, copy = share_copy(number)

            @pl.when(block != (sections - 1) * replicas + me)
            def _():
                copy.wait_send()


def hand_out(*refs):
    sources, results, held, sem = refs[:4], refs[4:8], refs[8:12], refs[12]
    incoming = [
        pltpu.make_async_copy(source, middle, sem.at[0, number])
        for number, (source, middle) in enumerate(zip(sources, held))
    ]
    outgoing = [
        pltpu.make_async_copy(middle, result, sem.at[1, number])
        for number, (middle, result) in enumerate(zip(held, results))
    ]
    for copy in incoming:
        copy.start()
    for arrival, copy in zip(incoming, outgoing):
        arrival.wait()
        copy.start()
    for copy in outgoing:
        copy.wait()


def local(
    sections,
    replicas,
    saved_inputs,
    norm_gain,
    down_weight,
    up_weight,
    head_weight,
    head_gain,
    targets,
    levels,
    level_index,
    plan,
):
    micro, tokens, width = saved_inputs.shape[1:]
    units = down_weight.shape[2]
    half = units // 2
    cols = head_weight.shape[1]
    rings = replicas // 4
    chunk = width // (2 * rings)
    share = width // replicas
    final = share // sections
    unit = tokens // 2
    units_all = 2 * micro
    quarter = half // 2
    longest = rings // 2
    anywhere = pl.BlockSpec(memory_space=pl.ANY)
    dma = pltpu.SemaphoreType.DMA
    grads, down_grad, up_grad, head_grad = pl.pallas_call(
        functools.partial(body, sections, replicas),
        out_shape=(
            jax.ShapeDtypeStruct((units_all, unit, width), BF16),
            jax.ShapeDtypeStruct((share, units), F32),
            jax.ShapeDtypeStruct((share, units), F32),
            jax.ShapeDtypeStruct((final, cols), F32),
        ),
        in_specs=[anywhere] * 10,
        out_specs=(anywhere,) * 4,
        scratch_shapes=[
            pltpu.SMEM(plan.shape, jnp.int32),
            pltpu.VMEM((1, level_index.shape[0]), jnp.int32),
            pltpu.VMEM(norm_gain.shape, F32),
            pltpu.VMEM(head_weight.shape, BF16),
            pltpu.VMEM((1, width), F32),
            pltpu.VMEM(targets.shape, F32),
            pltpu.VMEM(levels.T.shape, F32),
            pltpu.VMEM((micro, tokens, width), BF16),
            pltpu.VMEM((width, units), BF16),
            pltpu.VMEM((width, units), BF16),
            pltpu.VMEM((units, width), BF16),
            pltpu.VMEM((units_all, unit, width), BF16),
            pltpu.VMEM((units_all, unit, 1), F32),
            pltpu.VMEM((4, units_all, unit, width), BF16),
            pltpu.VMEM((5, units_all, unit, half), BF16),
            pltpu.VMEM((2, units_all, unit, half), F32),
            pltpu.VMEM((2, units_all, unit, half), F32),
            pltpu.VMEM((units_all, unit, width), BF16),
            pltpu.VMEM((4, units_all, unit, width // 2), BF16),
            pltpu.VMEM((7, units_all, unit, quarter), BF16),
            pltpu.VMEM((units_all, unit, width), BF16),
            pltpu.VMEM((4, width // 2, quarter), BF16),
            pltpu.VMEM((4, 2, longest, chunk, quarter), BF16),
            pltpu.VMEM((chunk, quarter), BF16),
            pltpu.VMEM((2, 2, share, half), F32),
            pltpu.VMEM((2, share, half), F32),
            pltpu.VMEM((replicas // 2, 2, share, cols), BF16),
            pltpu.VMEM((units_all, unit, width), BF16),
            pltpu.VMEM((units_all, unit, width), BF16),
            pltpu.VMEM((units_all, unit, cols), BF16),
            pltpu.VMEM((replicas // 2, 2, share, cols), F32),
            pltpu.VMEM((replicas // 2, share, cols), F32),
            pltpu.VMEM((replicas // 2, share, cols), F32),
            pltpu.VMEM((replicas // 2, share, cols), F32),
            pltpu.VMEM((sections, final, cols), F32),
            pltpu.VMEM((final, cols), F32),
            dma((4,)),
            dma((units_all, 2)),
            dma((units_all, 2)),
            dma((6,)),
            dma((6,)),
            dma((2, micro)),
            dma((2, micro)),
            dma((3, units_all)),
            dma((3, units_all)),
            dma((micro,)),
            dma((micro,)),
            dma((4, 2, longest)),
            dma((4, 2, longest)),
            dma((1,)),
            dma((1,)),
            dma((2, 2)),
            dma((2, 2)),
            dma((replicas // 2,)),
            dma((replicas // 2 + 1,)),
            dma((replicas // 2,)),
            dma((replicas // 2,)),
            dma((sections,)),
            dma(()),
            dma(()),
            dma(()),
            pltpu.SemaphoreType.REGULAR,
            dma((7,)),
            dma((5,)),
        ],
        compiler_params=pltpu.CompilerParams(
            collective_id=0, has_side_effects=True, vmem_limit_bytes=56 * 1024 * 1024
        ),
    )(
        plan,
        level_index.reshape(1, -1),
        saved_inputs[0],
        norm_gain,
        down_weight[0],
        up_weight[0],
        head_weight,
        head_gain.reshape(1, -1),
        targets,
        levels.T,
    )
    grads, down_grad, up_grad, head_grad = pl.pallas_call(
        hand_out,
        out_shape=tuple(
            jax.ShapeDtypeStruct(value.shape, value.dtype)
            for value in (grads, down_grad, up_grad, head_grad)
        ),
        in_specs=[anywhere] * 4,
        out_specs=(anywhere,) * 4,
        scratch_shapes=[
            pltpu.VMEM(value.shape, value.dtype)
            for value in (grads, down_grad, up_grad, head_grad)
        ]
        + [dma((2, 4))],
    )(grads, down_grad, up_grad, head_grad)
    return grads.reshape(1, micro, tokens, width), down_grad[None], up_grad[None], head_grad


def solution(mesh):
    return jax.shard_map(
        functools.partial(local, mesh.shape["section"], mesh.shape["dp"]),
        mesh=mesh,
        in_specs=(
            P("section", None, "dp", None),
            P("section", None),
            P("section", None, None),
            P("section", None, None),
            P("dp", None),
            P(),
            P(None, "dp", None),
            P(),
            P(),
            P(),
        ),
        out_specs=(
            P("section", None, "dp", None),
            P("section", "dp", None),
            P("section", "dp", None),
            P(("section", "dp"), None),
        ),
        check_vma=False,
    )
```
